32 devices in a mesh: section: 4 (over y, x), dp: 8 (over z, core).
Axes of the slice: x: 2, y: 2, z: 4, core: 2. Of those that a mesh axis runs over, the one named last changes fastest.
Arguments:
- inputs: bfloat16 [4, 1024, 512], P('section', 'dp'), may hold values from -6 to 6
- cotangent: bfloat16 [4, 1024, 512], P('section', 'dp'), may hold values from -6 to 6
- section_weights: bfloat16 [2048, 4096], P('section')
- norm_gains: float32 [2048], P('section'), may hold values from 0.5 to 1.5
- doc_lengths: int32 [4, 8, 6], P('section', 'dp'), may hold values from 1 to 64, 128 in all within a row
- slot_fill: int32 [4, 8], P('section', 'dp'), may hold values from 96 to 128, as said below
Outputs:
- input_grad: bfloat16 [4, 1024, 512], P('section', 'dp')
- weight_grads: float32 [2048, 4096], P('section')
- gain_grads: float32 [2048], P('section')
- forget_mean: float32 [2], replicated
The draws below stay inside these ranges and needn't reach their ends.
Inputs may be any that keep to these rules, and one draw needn't show every extreme that they name: `slot_fill`: every slot is filled from its start; some slot of every draw is full. `doc_lengths`: the lengths of a slot's documents add up to 128.
All inputs are finite; a program needn't handle non-finite values.
Results may differ from the reference program's by a relative error of at most 0.01.
Values may be sent and summed in bfloat16 or wider, within the bound.
A program may use at most 320 MiB of HBM per device.

```python
import math
import jax
import jax.numpy as jnp
import numpy as np
from jax import lax

D = 512
GATE = 1024
FF = 2048
SLOT = 128
DOCS = 6
MICRO = 4
NTOK = 1024
N_SECTION = 4
N_DP = 8


def draw_section_weights(key, part):
    key = jax.random.fold_in(key, 5)
    values = jax.random.normal(key, (N_SECTION * D, 4 * GATE), jnp.float32)
    rows = jnp.arange(N_SECTION * D, dtype=jnp.int32)[:, None] // D
    columns = jnp.arange(4 * GATE, dtype=jnp.int32)[None, :]
    mixer_scale = jnp.where(columns < 3 * GATE, D ** (-0.5), GATE ** (-0.5))
    dense_scale = jnp.where(columns < FF, D ** (-0.5), FF ** (-0.5))
    scale = jnp.where(rows % 2 == 0, mixer_scale, dense_scale)
    return (values * scale).astype(jnp.bfloat16)


def draw_slot_fill(key, part):
    key = jax.random.fold_in(key, 11)
    first_key, second_key = jax.random.split(key)
    shortfall = jax.random.randint(first_key, (MICRO, N_DP), 0, SLOT // 4 + 1)
    complete = jax.random.randint(second_key, (MICRO, N_DP), 0, 4) == 0
    shortfall = jnp.where(complete, 0, shortfall)
    shortfall = shortfall.at[0, 0].set(0)
    return (SLOT - shortfall).astype(jnp.int32)


def levels(stream_key, shape, cuts, low, top_value):
    def one(dim, parts):
        heights = jax.random.uniform(jax.random.fold_in(jax.random.fold_in(stream_key, 6), dim), (parts,), jnp.float32, low / len(cuts), top_value / len(cuts))
        return jnp.repeat(jnp.exp(heights), shape[dim] // parts).reshape((-1,) + (1,) * (len(shape) - dim - 1))

    level = one(*cuts[0])
    for cut in cuts[1:]:
        level = level * one(*cut)
    return level


def profile(count, total, most, slope):
    loads = [(1 << 20) // math.isqrt(rank ** slope) + 1 for rank in range(2, count + 1)]
    surplus, holding = total - most - (count - 1), [1] * (count - 1)
    while surplus > 0:
        movable = [i for i in range(count - 1) if holding[i] < most]
        whole, remaining = sum([loads[i] for i in movable]), surplus
        for i in movable:
            extra = min(most - holding[i], max(1, remaining * loads[i] // whole), surplus)
            holding[i] = holding[i] + extra
            surplus = surplus - extra
    return np.array([most] + holding)


def ragged(rng, number_of, total, most, slope):
    if number_of == 2:
        one = jax.random.randint(rng, (), max(1, total - most), min(most, total - 1) + 1)
        return jnp.stack([one, total - one])
    sizes = jnp.asarray(profile(number_of, total, most, slope), jnp.int32)
    pairs = (number_of - 1) // 2
    donor, taker = sizes[1:1 + 2 * pairs:2], sizes[2:2 + 2 * pairs:2]
    margin = jnp.minimum(donor - 1, most - taker)
    passed = jax.random.randint(jax.random.fold_in(rng, 1), (pairs,), 0, 1 << 20) % (margin + 1)
    sizes = sizes.at[1:1 + 2 * pairs:2].set(donor - passed).at[2:2 + 2 * pairs:2].set(taker + passed)
    return sizes[jax.random.permutation(jax.random.fold_in(rng, 2), number_of)]


def bell_draw(own_key, extent, scale, most, cuts=(), kind=jnp.bfloat16):
    factor_of = levels(own_key, extent, cuts, -0.22, 0.18) if cuts else 1.0
    values = jax.random.normal(own_key, extent, jnp.float32) * scale * factor_of
    return jnp.minimum(jnp.maximum(values, -most), most).astype(kind)


def setup_inputs(seed: int = 0) -> dict:
    key_list = jax.random.split(jax.random.key(seed), 7)
    return {
        "inputs": bell_draw(key_list[0], (MICRO, NTOK, D), 1.0, 6.0, ((0, 4), (1, 8))),
        "cotangent": bell_draw(key_list[1], (MICRO, NTOK, D), 1.0, 6.0, ((0, 4), (1, 8))),
        "section_weights": draw_section_weights(jax.random.fold_in(key_list[6], 71), 0),
        "norm_gains": jnp.clip(1.0 + 0.1 * jax.random.normal(key_list[3], (N_SECTION * D,), jnp.float32), 0.5, 1.5),
        "doc_lengths": jax.vmap(lambda own: ragged(own, DOCS, SLOT, SLOT // 2, 2))(jax.random.split(key_list[4], MICRO * N_DP)).reshape((MICRO, N_DP, DOCS)).astype(jnp.int32),
        "slot_fill": draw_slot_fill(jax.random.fold_in(key_list[6], 71), 0),
    }


EPS = 1e-06

@jax.custom_vjp
def low(v):
    return lax.optimization_barrier(v.astype(jnp.bfloat16)).astype(jnp.float32)

@jax.custom_vjp
def low_back(v):
    return v

def low_keep(v):
    return (low(v), None)

def low_pass(kept, grad):
    return (grad,)

def back_keep(v):
    return (v, None)

def back_low(kept, grad):
    return (low(grad),)
low.defvjp(low_keep, low_pass)
low_back.defvjp(back_keep, back_low)

def product(left, right):
    return jnp.dot(left, right, precision=lax.Precision.HIGHEST, preferred_element_type=jnp.float32)

def rms_norm(values, norm_gain):
    return values * lax.rsqrt(lax.optimization_barrier(jnp.mean(values * values, axis=-1, keepdims=True)) + EPS) * norm_gain

def mix_gates(projection, keep_mask):
    width = projection.shape[1] // 3
    gate_gap = jax.nn.softplus(-projection[:, :width]) - jax.nn.softplus(-projection[:, width:2 * width])
    forget = jnp.exp(-jax.nn.softplus(gate_gap))
    drive_term = jnp.exp(-jax.nn.softplus(-gate_gap)) * jax.nn.softplus(projection[:, 2 * width:])
    return (forget * keep_mask[:, None], drive_term, forget)

def combine(earlier, later):
    return (earlier[0] * later[0], later[0] * earlier[1] + later[1])

def recurrence(decay_rate, drive_term):
    return lax.associative_scan(combine, (decay_rate, drive_term), axis=0)[1]

def mixer_layer(residual, norm_gain, weight_block, keep_mask, valid_mask):
    width = weight_block.shape[1] // 4
    normed = low(rms_norm(residual, norm_gain))
    projection = low_back(product(normed, weight_block[:, :3 * width]))
    decay_rate, drive_term, forget = mix_gates(projection, keep_mask)
    hidden_state = low(recurrence(decay_rate, drive_term))
    branch_out = low_back(product(hidden_state, weight_block[:, 3 * width:].T))
    return (residual + branch_out, jnp.sum(forget * valid_mask[:, None]))

def feed_forward(residual, norm_gain, weight_block):
    width = weight_block.shape[1] // 2
    normed = low(rms_norm(residual, norm_gain))
    hidden_units = low_back(product(normed, weight_block[:, :width]))
    activated = low(jax.nn.gelu(hidden_units, approximate=False))
    return residual + low_back(product(activated, weight_block[:, width:].T))

def boundary(values):
    return low_back(low(values))

def slot_masks(lengths, used):
    positions = jnp.arange(SLOT, dtype=jnp.int32)
    lengths = lengths.astype(jnp.int32)
    starts = (jnp.cumsum(lengths) - lengths).astype(jnp.int32)
    keep_mask = 1.0 - jnp.any(positions[:, None] == starts[None, :], axis=1).astype(jnp.float32)
    valid_mask = (positions < used).astype(jnp.float32)
    return (keep_mask, valid_mask)

def full_forward(residual, weights, gains, keeps, valids):
    blocks = [weights[layer_index * D:(layer_index + 1) * D] for layer_index in range(4)]
    norms = [gains[layer_index * D:(layer_index + 1) * D] for layer_index in range(4)]

    def one_slot(slot_input, keep_mask, valid_mask):
        first_out, first_sum = mixer_layer(slot_input, norms[0], blocks[0], keep_mask, valid_mask)
        second_out = feed_forward(boundary(first_out), norms[1], blocks[1])
        third_out, third_sum = mixer_layer(boundary(second_out), norms[2], blocks[2], keep_mask, valid_mask)
        final_out = feed_forward(boundary(third_out), norms[3], blocks[3])
        return (final_out, jnp.stack([first_sum, third_sum]))
    checked = jax.checkpoint(one_slot)

    def scan_step(totals, slot_item):
        final_out, sums = checked(*slot_item)
        return (totals + sums, final_out)
    totals, outputs = lax.scan(scan_step, jnp.zeros((2,), jnp.float32), (residual, keeps, valids))
    return (outputs, totals)

def reference(inputs, cotangent, section_weights, norm_gains, doc_lengths, slot_fill):
    lengths = doc_lengths.reshape(MICRO * N_DP, DOCS)
    fills = slot_fill.reshape(MICRO * N_DP)
    keeps, valids = jax.vmap(slot_masks)(lengths, fills)
    residual = inputs.astype(jnp.float32).reshape(MICRO * N_DP, SLOT, D)

    def whole_block(start_values, weights, gains):
        return full_forward(low_back(start_values), weights, gains, keeps, valids)
    outputs, pull, totals = jax.vjp(whole_block, residual, section_weights.astype(jnp.float32), norm_gains, has_aux=True)
    seed_grad = cotangent.astype(jnp.float32).reshape(MICRO * N_DP, SLOT, D) * valids[:, :, None]
    input_grad, weight_grads, gain_grads = pull(seed_grad)
    forget_mean = totals / (jnp.sum(valids) * GATE)
    return (input_grad.reshape(MICRO, N_DP * SLOT, D).astype(jnp.bfloat16), weight_grads, gain_grads, forget_mean)
```

```python
import functools

import jax
import jax.numpy as jnp
from jax import lax
from jax.experimental import pallas as pl
from jax.experimental.pallas import tpu as pltpu
from jax.sharding import PartitionSpec as P

EPS = 1e-06
MESH = pl.DeviceIdType.MESH
F32 = jnp.float32
BF16 = jnp.bfloat16
LANES = 128
MIX_CHUNK = 256
DENSE_CHUNK = 512
SUM_CHUNK = 128


def dot_nn(left, right):
    return jnp.dot(left, right, preferred_element_type=F32)


def dot_nt(left, right):
    return lax.dot_general(left, right, (((1,), (1,)), ((), ())), preferred_element_type=F32)


def scan_down(decay, drive):
    for by in (1, 2, 4):
        drive = drive + decay * pltpu.roll(drive, by, 0)
        decay = decay * pltpu.roll(decay, by, 0)
    blocks = [drive[:8]]
    for at in range(8, drive.shape[0], 8):
        blocks.append(drive[at : at + 8] + decay[at : at + 8] * blocks[-1])
    return jnp.concatenate(blocks, 0)


def scan_up(decay_next, source):
    rows = source.shape[0]
    for by in (1, 2, 4):
        source = source + decay_next * pltpu.roll(source, rows - by, 0)
        decay_next = decay_next * pltpu.roll(decay_next, rows - by, 0)
    blocks = [source[rows - 8 :]]
    for at in range(rows - 16, -1, -8):
        blocks.append(source[at : at + 8] + decay_next[at : at + 8] * blocks[-1])
    return jnp.concatenate(blocks[::-1], 0)


def wide(column, width):
    return jnp.concatenate([column] * (width // LANES), 1)


def unit(x):
    return lax.rsqrt(jnp.mean(x * x, axis=-1, keepdims=True) + EPS)


def norm_back(x, q, gain, d_normed, grad_out):
    x_hat = x * q
    scaled = d_normed * gain
    mean = jnp.mean(scaled * x_hat, axis=-1, keepdims=True)
    d_gain = jnp.sum(d_normed * x_hat, axis=0, keepdims=True)
    return grad_out + q * (scaled - x_hat * mean), d_gain


def gelu_parts(u):
    cdf = 0.5 * lax.erf(u * 0.7071067811865476) + 0.5
    slope = cdf + u * (0.3989422804014327 * jnp.exp(-0.5 * u * u))
    return u * cdf, slope


def kernel(
    count,
    x_ref, cot_ref, w_hbm, gain_ref, len_ref, fill_ref,
    ig_ref, dw_ref, dgain_ref, fmean_ref,
    w, res, grad, out, gout, dy_own, mask, mask_own,
    decay_next, coef, slope, da, rows, left, forget_acc,
    sib_out, sib_in, outer_in, part, tot_in, work,
    small, small_sib, small_outer, small_part, small_tot, small_far,
    w_sem, x_send, dy_send, mask_send, res_send, res_recv, grad_send, grad_recv, mask_recv, ig_recv,
    sib_send, sib_recv, part_send, outer_recv, tot_send, tot_recv, fin_send, fin_recv,
    small_send, small_recv, far_send, far_recv,
):
    s = lax.axis_index("section")
    d = lax.axis_index("dp")
    core = lax.rem(d, 2)
    chip = d // 2
    chips = count // 2
    sections, slot, width = res.shape
    pack = w.shape[1]
    gate = pack // 4
    ff = pack // 2
    half = pack // 2
    pieces = sib_in.shape[0]
    piece = sib_in.shape[2]
    last = sections - 1
    is_first = s == 0
    is_last = s == last
    is_mixer = lax.rem(s, 2) == 0
    on_left = chip < chips // 2
    is_middle = (chip == chips // 2 - 1) | (chip == chips // 2)
    is_end = (chip == 0) | (chip == chips - 1)
    sibling = (s, d + 1 - 2 * core)
    inner = (s, jnp.where(on_left, d + 2, d - 2))
    outer = (s, jnp.where(on_left, d - 2, d + 2))

    w_copy = pltpu.make_async_copy(w_hbm, w, w_sem)
    w_copy.start()

    barrier = pltpu.get_barrier_semaphore()
    for by in range(1, sections):
        pl.semaphore_signal(barrier, inc=1, device_id=(lax.rem(s + by, sections), d), device_id_type=MESH)
    pl.semaphore_signal(barrier, inc=1, device_id=sibling, device_id_type=MESH)

    @pl.when(chip > 0)
    def _():
        pl.semaphore_signal(barrier, inc=1, device_id=(s, d - 2), device_id_type=MESH)

    @pl.when(chip < chips - 1)
    def _():
        pl.semaphore_signal(barrier, inc=1, device_id=(s, d + 2), device_id_type=MESH)

    def remote(src, dst, send, recv, target):
        return pltpu.make_async_remote_copy(
            src_ref=src, dst_ref=dst, send_sem=send, recv_sem=recv, device_id=target, device_id_type=MESH
        )

    lane = lax.broadcasted_iota(jnp.int32, (8, slot), 1)
    row = lax.broadcasted_iota(jnp.int32, (8, slot), 0)
    starts = lane == 0
    position = len_ref[0, 0, 0]
    for k in range(1, len_ref.shape[2]):
        starts = starts | (lane == position)
        position = position + len_ref[0, 0, k]
    keep_rows = jnp.where(starts, 0.0, 1.0)
    valid_rows = jnp.where(lane < fill_ref[0, 0], 1.0, 0.0)
    mask_own[...] = jnp.where(row == 0, keep_rows, valid_rows)
    tokens = lax.broadcasted_iota(jnp.int32, (slot, width), 0)
    dy_own[...] = jnp.where(tokens < fill_ref[0, 0], cot_ref[0].astype(F32), 0.0).astype(BF16)
    forget_acc[...] = jnp.zeros_like(forget_acc)
    small[...] = jnp.zeros_like(small)

    pl.semaphore_wait(
        barrier, sections + jnp.where(chip > 0, 1, 0) + jnp.where(chip < chips - 1, 1, 0)
    )

    x_copy = remote(x_ref.at[0], res.at[s], x_send, res_recv.at[s], (0, d))
    dy_copy = remote(dy_own, grad.at[s], dy_send, grad_recv.at[s], (last, d))
    mask_copies = [
        remote(mask_own, mask.at[s], mask_send.at[k], mask_recv.at[s], (2 * k, d))
        for k in range(sections // 2)
    ]

    @pl.when(is_first)
    def _():
        res[0] = x_ref[0]

    @pl.when(s != 0)
    def _():
        x_copy.start()

    for k in range(sections // 2):

        @pl.when(s == 2 * k)
        def _():
            mask[s] = mask_own[...]

        @pl.when(s != 2 * k)
        def _():
            mask_copies[k].start()

    @pl.when(is_last)
    def _():
        grad[last] = dy_own[...]

    @pl.when(s != last)
    def _():
        dy_copy.start()

    def res_in(m):
        return remote(out.at[m], res.at[m], res_send.at[m], res_recv.at[m], (jnp.minimum(s + 1, last), d))

    def grad_in(m):
        return remote(gout.at[m], grad.at[m], grad_send.at[m], grad_recv.at[m], (jnp.maximum(s - 1, 0), d))

    def wait_res(m):
        @pl.when((s != 0) | (m != 0))
        def _():
            res_in(m).wait_recv()

    def wait_grad(m):
        @pl.when((s != last) | (m != last))
        def _():
            grad_in(m).wait_recv()

    def send_grad(m):
        @pl.when(s != 0)
        def _():
            grad_in(m).start()

        @pl.when((s == 0) & (m == 0))
        def _():
            ig_ref[0] = gout[m]

        @pl.when((s == 0) & (m != 0))
        def _():
            remote(gout.at[m], ig_ref.at[0], grad_send.at[m], ig_recv, (m, d)).start()

    gain = gain_ref[...]
    w_copy.wait()

    @pl.when(is_mixer)
    def _():
        def forward(m, carry):
            wait_res(m)

            @pl.when(m != s)
            def _():
                remote(mask_own, mask.at[m], mask_send.at[0], mask_recv.at[m], (0, d)).wait_recv()

            at = pl.ds(pl.multiple_of(m * slot, slot), slot)
            masks = mask[m]
            keep = wide(jnp.broadcast_to(masks[0:1], (slot, slot)).T, MIX_CHUNK)
            valid = wide(jnp.broadcast_to(masks[1:2], (slot, slot)).T, MIX_CHUNK)
            x = res[m].astype(F32)
            normed = (x * unit(x) * gain).astype(BF16)
            total = x
            for c in range(0, gate, MIX_CHUNK):
                f_in = dot_nn(normed, w[:, c : c + MIX_CHUNK])
                i_in = dot_nn(normed, w[:, gate + c : gate + c + MIX_CHUNK])
                c_in = dot_nn(normed, w[:, 2 * gate + c : 2 * gate + c + MIX_CHUNK])
                top = jnp.maximum(jnp.maximum(-f_in, -i_in), 0.0)
                e_zero = jnp.exp(-top)
                e_f = jnp.exp(-f_in - top)
                e_i = jnp.exp(-i_in - top)
                u_f = e_zero + e_f
                u_i = e_zero + e_i
                inv = 1.0 / (u_f + u_i)
                forget = u_i * inv
                intake = u_f * inv
                e_c = jnp.exp(-jnp.abs(c_in))
                soft = jnp.maximum(c_in, 0.0) + jnp.log1p(e_c)
                decay = forget * keep
                state = scan_down(decay, intake * soft)
                state_low = state.astype(BF16)
                total = total + dot_nt(state_low, w[:, 3 * gate + c : 3 * gate + c + MIX_CHUNK])
                rows[at, 3 * gate + c : 3 * gate + c + MIX_CHUNK] = state_low
                bend = soft - keep * pltpu.roll(state, 1, 0)
                decay_next[m, :, c : c + MIX_CHUNK] = pltpu.roll(decay, slot - 1, 0)
                coef[m, :, c : c + MIX_CHUNK] = -forget * (e_f * inv) * bend
                coef[m, :, gate + c : gate + c + MIX_CHUNK] = intake * (e_i * inv) * bend
                coef[m, :, 2 * gate + c : 2 * gate + c + MIX_CHUNK] = (
                    intake * jnp.where(c_in >= 0.0, 1.0, e_c) / (1.0 + e_c)
                )
                counted = forget * valid
                folded = counted[:8]
                for k in range(8, slot, 8):
                    folded = folded + counted[k : k + 8]
                forget_acc[...] += folded
            out[m] = total.astype(BF16)
            res_in(m).start()
            left[0, :, at] = normed.astype(F32).T.astype(BF16)
            return carry

        lax.fori_loop(0, sections, forward, 0)

        def backward(m, carry):
            wait_grad(m)
            at = pl.ds(pl.multiple_of(m * slot, slot), slot)
            g_low = grad[m]
            x = res[m].astype(F32)
            q = unit(x)
            d_normed = jnp.zeros((slot, width), F32)
            for c in range(0, gate, MIX_CHUNK):
                d_state = dot_nn(g_low, w[:, 3 * gate + c : 3 * gate + c + MIX_CHUNK])
                adjoint = scan_up(decay_next[m, :, c : c + MIX_CHUNK], d_state)
                for k in range(3):
                    part_at = slice(k * gate + c, k * gate + c + MIX_CHUNK)
                    low = (adjoint * coef[m, :, part_at]).astype(BF16)
                    rows[at, part_at] = low
                    d_normed = d_normed + dot_nt(low, w[:, part_at])
            g_high = g_low.astype(F32)
            d_res, d_gain = norm_back(x, q, gain, d_normed, g_high)
            gout[m] = d_res.astype(BF16)
            send_grad(m)
            small[0:1, :] += d_gain
            left[1, :, at] = g_high.T.astype(BF16)
            return carry

        lax.fori_loop(0, sections, backward, 0)

    @pl.when((lax.rem(s, 2) == 1) & (s != last))
    def _():
        def forward(m, carry):
            wait_res(m)
            at = pl.ds(pl.multiple_of(m * slot, slot), slot)
            x = res[m].astype(F32)
            normed = (x * unit(x) * gain).astype(BF16)
            total = x
            for c in range(0, ff, DENSE_CHUNK):
                hidden, bend = gelu_parts(dot_nn(normed, w[:, c : c + DENSE_CHUNK]))
                low = hidden.astype(BF16)
                total = total + dot_nt(low, w[:, ff + c : ff + c + DENSE_CHUNK])
                rows[at, ff + c : ff + c + DENSE_CHUNK] = low
                slope[m, :, c : c + DENSE_CHUNK] = bend
            out[m] = total.astype(BF16)
            res_in(m).start()
            left[0, :, at] = normed.astype(F32).T.astype(BF16)
            return carry

        lax.fori_loop(0, sections, forward, 0)

        def backward(m, carry):
            wait_grad(m)
            at = pl.ds(pl.multiple_of(m * slot, slot), slot)
            g_low = grad[m]
            x = res[m].astype(F32)
            q = unit(x)
            d_normed = jnp.zeros((slot, width), F32)
            for c in range(0, ff, DENSE_CHUNK):
                d_act = dot_nn(g_low, w[:, ff + c : ff + c + DENSE_CHUNK])
                low = (d_act * slope[m, :, c : c + DENSE_CHUNK]).astype(BF16)
                rows[at, c : c + DENSE_CHUNK] = low
                d_normed = d_normed + dot_nt(low, w[:, c : c + DENSE_CHUNK])
            g_high = g_low.astype(F32)
            d_res, d_gain = norm_back(x, q, gain, d_normed, g_high)
            gout[m] = d_res.astype(BF16)
            send_grad(m)
            small[0:1, :] += d_gain
            left[1, :, at] = g_high.T.astype(BF16)
            return carry

        lax.fori_loop(0, sections, backward, 0)

    @pl.when(is_last)
    def _():
        def prepare(m, carry):
            wait_grad(m)
            at = pl.ds(pl.multiple_of(m * slot, slot), slot)
            g_low = grad[m]
            for c in range(0, ff, DENSE_CHUNK):
                da[m, :, c : c + DENSE_CHUNK] = dot_nn(g_low, w[:, ff + c : ff + c + DENSE_CHUNK])
            left[1, :, at] = g_low.astype(F32).T.astype(BF16)
            return carry

        lax.fori_loop(0, sections, prepare, 0)

        def both(m, carry):
            wait_res(m)
            at = pl.ds(pl.multiple_of(m * slot, slot), slot)
            x = res[m].astype(F32)
            q = unit(x)
            normed = (x * q * gain).astype(BF16)
            d_normed = jnp.zeros((slot, width), F32)
            for c in range(0, ff, DENSE_CHUNK):
                hidden, bend = gelu_parts(dot_nn(normed, w[:, c : c + DENSE_CHUNK]))
                rows[at, ff + c : ff + c + DENSE_CHUNK] = hidden.astype(BF16)
                low = (da[m, :, c : c + DENSE_CHUNK] * bend).astype(BF16)
                rows[at, c : c + DENSE_CHUNK] = low
                d_normed = d_normed + dot_nt(low, w[:, c : c + DENSE_CHUNK])
            d_res, d_gain = norm_back(x, q, gain, d_normed, grad[m].astype(F32))
            gout[m] = d_res.astype(BF16)
            send_grad(m)
            small[0:1, :] += d_gain
            left[0, :, at] = normed.astype(F32).T.astype(BF16)
            return carry

        lax.fori_loop(0, sections, both, 0)

    @pl.when(is_mixer)
    def _():
        small[1:2, 0:MIX_CHUNK] = jnp.sum(forget_acc[...], axis=0, keepdims=True)
        used = mask[0, 1:2]
        for m in range(1, sections):
            used = used + mask[m, 1:2]
        small[2:3, 0:slot] = used

    split = jnp.where(is_mixer, 3 * gate, ff)

    def grad_piece(col):
        side = jnp.where(col < split, 0, 1)
        return dot_nn(left[side], rows[:, pl.ds(pl.multiple_of(col, piece), piece)])

    def sib_copy(k):
        return remote(sib_out.at[k], sib_in.at[k], sib_send.at[k], sib_recv.at[k], sibling)

    def inward(k):
        return remote(part.at[k], outer_in.at[k], part_send.at[k], outer_recv.at[k], inner)

    def across(k):
        return remote(part.at[k], tot_in.at[k], part_send.at[k], tot_recv.at[k], inner)

    def outward(k):
        return remote(tot_in.at[k], tot_in.at[k], tot_send.at[k], tot_recv.at[k], outer)

    def own_at(k):
        return pl.ds(pl.multiple_of(core * half + k * piece, piece), piece)

    def final(k):
        return remote(tot_in.at[k], dw_ref.at[:, own_at(k)], fin_send.at[k], fin_recv.at[k], sibling)

    small_swap = remote(small, small_sib, small_send.at[0], small_recv.at[0], sibling)
    small_inward = remote(small_part, small_outer, small_send.at[1], small_recv.at[1], inner)
    small_across = remote(small_part, small_tot, small_send.at[1], small_recv.at[2], inner)
    small_outward = remote(small_tot, small_tot, small_send.at[2], small_recv.at[2], outer)

    small_swap.start()

    def to_sibling(k, carry):
        sib_out[k] = grad_piece((1 - core) * half + k * piece).astype(BF16)
        sib_copy(k).start()
        return carry

    lax.fori_loop(0, pieces, to_sibling, 0)

    def reduce_small():
        small_swap.wait_recv()

        @pl.when(is_end)
        def _():
            small_part[...] = small[...] + small_sib[...]

        @pl.when(jnp.logical_not(is_end))
        def _():
            small_inward.wait_recv()
            small_part[...] = small[...] + small_sib[...] + small_outer[...]

        @pl.when(is_middle)
        def _():
            small_across.start()

        @pl.when(jnp.logical_not(is_middle))
        def _():
            small_inward.start()

    def far_copy(k):
        return remote(
            small_tot, small_far.at[s // 2], far_send.at[k - 1], far_recv.at[s // 2], (lax.rem(s + k, sections), d)
        )

    def total_small():
        small_across.wait_recv()

        @pl.when(is_middle)
        def _():
            small_tot[...] = small_tot[...] + small_part[...]

        @pl.when(jnp.logical_not(is_end))
        def _():
            small_outward.start()

        @pl.when(is_mixer)
        def _():
            small_far[s // 2] = small_tot[...]
            for k in range(1, sections):
                far_copy(k).start()

    def reduce_piece(k):
        work[...] = grad_piece(core * half + k * piece)
        sib_copy(k).wait_recv()

        @pl.when(is_end)
        def _():
            part[k] = (work[...] + sib_in[k].astype(F32)).astype(BF16)

        @pl.when(jnp.logical_not(is_end))
        def _():
            inward(k).wait_recv()
            part[k] = (work[...] + sib_in[k].astype(F32) + outer_in[k].astype(F32)).astype(BF16)

        @pl.when(is_middle)
        def _():
            across(k).start()

        @pl.when(jnp.logical_not(is_middle))
        def _():
            inward(k).start()

    def total_piece(k):
        across(k).wait_recv()

        @pl.when(is_middle)
        def _():
            tot_in[k] = (tot_in[k].astype(F32) + part[k].astype(F32)).astype(BF16)

        @pl.when(jnp.logical_not(is_end))
        def _():
            outward(k).start()

        final(k).start()
        dw_ref[:, own_at(k)] = tot_in[k]

    lag = jnp.where(is_middle, 2, pieces)

    def step(i, carry):
        @pl.when(i == 0)
        def _():
            reduce_small()

        @pl.when(i < pieces)
        def _():
            reduce_piece(i)

        @pl.when(i == lag)
        def _():
            total_small()

        @pl.when(i >= lag)
        def _():
            total_piece(i - lag)

        return carry

    lax.fori_loop(0, pieces + lag, step, 0)

    for k in range(sections // 2):

        @pl.when(s != 2 * k)
        def _():
            remote(small_tot, small_far.at[k], far_send.at[0], far_recv.at[k], sibling).wait_recv()

    dgain_ref[...] = small_tot[0:1, :]
    lanes = lax.broadcasted_iota(jnp.int32, (1, LANES), 1)
    means = jnp.zeros((1, LANES), F32)
    for k in range(sections // 2):
        sums = jnp.sum(small_far[k], axis=1, keepdims=True)
        means = jnp.where(lanes == k, sums[1:2] / (sums[2:3] * gate), means)
    fmean_ref[...] = means

    @pl.when(s != 0)
    def _():
        remote(gout.at[0], ig_ref.at[0], grad_send.at[0], ig_recv, (s, d)).wait_recv()
        x_copy.wait_send()

    @pl.when(s != last)
    def _():
        dy_copy.wait_send()

    for k in range(sections // 2):

        @pl.when(s != 2 * k)
        def _():
            mask_copies[k].wait_send()

    for m in range(sections):

        @pl.when(s != last)
        def _():
            res_in(m).wait_send()

        @pl.when((s != 0) | (m != 0))
        def _():
            grad_in(m).wait_send()

    small_swap.wait_send()
    small_across.wait_send()

    @pl.when(jnp.logical_not(is_end))
    def _():
        small_outward.wait_send()

    @pl.when(is_mixer)
    def _():
        for k in range(1, sections):
            far_copy(k).wait_send()

    def finish(k, carry):
        sib_copy(k).wait_send()
        across(k).wait_send()

        @pl.when(jnp.logical_not(is_end))
        def _():
            outward(k).wait_send()

        final(k).wait()
        return carry

    lax.fori_loop(0, pieces, finish, 0)


def local(count, inputs, cotangent, section_weights, norm_gains, doc_lengths, slot_fill):
    sections = lax.axis_size("section")
    slot, width = inputs.shape[1:]
    pack = section_weights.shape[1]
    gate, ff, half = pack // 4, pack // 2, pack // 2
    tokens = sections * slot
    pieces = half // SUM_CHUNK
    dma = pltpu.SemaphoreType.DMA
    halves = pltpu.VMEM((pieces, width, SUM_CHUNK), BF16)
    small = pltpu.VMEM((8, width), F32)
    stack = pltpu.VMEM((sections, slot, width), BF16)
    vmem = pl.BlockSpec(memory_space=pltpu.VMEM)
    smem = pl.BlockSpec(memory_space=pltpu.SMEM)
    input_grad, weight_grads, gain_grads, means = pl.pallas_call(
        functools.partial(kernel, count),
        out_shape=(
            jax.ShapeDtypeStruct((1, slot, width), BF16),
            jax.ShapeDtypeStruct((width, pack), BF16),
            jax.ShapeDtypeStruct((1, width), F32),
            jax.ShapeDtypeStruct((1, LANES), F32),
        ),
        in_specs=[vmem, vmem, pl.BlockSpec(memory_space=pl.ANY), vmem, smem, smem],
        out_specs=(vmem, vmem, vmem, vmem),
        scratch_shapes=[
            pltpu.VMEM((width, pack), BF16),
            stack, stack, stack, stack,
            pltpu.VMEM((slot, width), BF16),
            pltpu.VMEM((sections, 8, slot), F32),
            pltpu.VMEM((8, slot), F32),
            pltpu.VMEM((sections, slot, gate), F32),
            pltpu.VMEM((sections, slot, 3 * gate), F32),
            pltpu.VMEM((sections, slot, ff), F32),
            pltpu.VMEM((sections, slot, ff), F32),
            pltpu.VMEM((tokens, pack), BF16),
            pltpu.VMEM((2, width, tokens), BF16),
            pltpu.VMEM((8, MIX_CHUNK), F32),
            halves, halves, halves, halves, halves,
            pltpu.VMEM((width, SUM_CHUNK), F32),
            small, small, small, small, small,
            pltpu.VMEM((sections // 2, 8, width), F32),
            dma, dma, dma,
            dma((sections // 2,)),
            dma((sections,)), dma((sections,)), dma((sections,)), dma((sections,)),
            dma((sections,)), dma,
            dma((pieces,)), dma((pieces,)), dma((pieces,)), dma((pieces,)),
            dma((pieces,)), dma((pieces,)), dma((pieces,)), dma((pieces,)),
            dma((3,)), dma((3,)), dma((sections - 1,)), dma((sections // 2,)),
        ],
        compiler_params=pltpu.CompilerParams(
            collective_id=0, has_side_effects=True, vmem_limit_bytes=56 * 1024 * 1024
        ),
    )(inputs, cotangent, section_weights, norm_gains.reshape(1, width), doc_lengths, slot_fill)
    return (
        input_grad,
        weight_grads.astype(F32),
        gain_grads.reshape(width),
        means[0, : sections // 2],
    )


def solution(mesh):
    placed = (
        P("section", "dp", None),
        P("section", "dp", None),
        P("section", None),
        P("section"),
        P("section", "dp", None),
        P("section", "dp"),
    )
    return jax.shard_map(
        functools.partial(local, mesh.shape["dp"]),
        mesh=mesh,
        in_specs=placed,
        out_specs=(P("section", "dp", None), P("section", None), P("section"), P()),
        check_vma=False,
    )
```

```python
import functools

import jax
import jax.numpy as jnp
from jax import lax
from jax.experimental import pallas as pl
from jax.experimental.pallas import tpu as pltpu
from jax.sharding import PartitionSpec as P

EPS = 1e-06
MESH = pl.DeviceIdType.MESH
F32 = jnp.float32
BF16 = jnp.bfloat16
LANES = 128
GATE_CHUNK = 256
BACK_CHUNK = 512
DENSE_CHUNK = 512
LAST_CHUNK = 256
TURN = 256
PIECE = (256, 128)
GUESTS = 5
LAG = 3
SMALL_STEP = 3
FINISH_ROWS = 32


def dot(left, right):
    return jnp.dot(left, right, preferred_element_type=F32)


def time_of_row(slot, shape, axis):
    row = lax.broadcasted_iota(jnp.int32, shape, axis)
    return (row & 7) * (slot // 8) + (row >> 3)


def scan_down(decay, drive):
    blocks = range(8, decay.shape[0], 8)
    factor, value = [decay[:8]], [drive[:8]]
    for at in blocks:
        here = decay[at : at + 8]
        value.append(drive[at : at + 8] + here * value[-1])
        factor.append(here * factor[-1])
    joined, through = value[-1], factor[-1]
    for by in (1, 2, 4):
        joined = joined + through * pltpu.roll(joined, by, 0)
        through = through * pltpu.roll(through, by, 0)
    before = pltpu.roll(joined, 1, 0)
    state = [v + f * before for v, f in zip(value, factor)]
    return jnp.concatenate(state, 0), jnp.concatenate([before] + state[:-1], 0)


def scan_up(decay, source):
    rows = decay.shape[0]
    ahead = [decay[at : at + 8] for at in range(8, rows, 8)] + [pltpu.roll(decay[:8], 7, 0)]
    factor, value = [ahead[-1]], [source[rows - 8 :]]
    for k in range(rows // 8 - 2, -1, -1):
        value.append(source[8 * k : 8 * k + 8] + ahead[k] * value[-1])
        factor.append(ahead[k] * factor[-1])
    joined, through = value[-1], factor[-1]
    for by in (1, 2, 4):
        joined = joined + through * pltpu.roll(joined, 8 - by, 0)
        through = through * pltpu.roll(through, 8 - by, 0)
    after = pltpu.roll(joined, 7, 0)
    return jnp.concatenate([v + f * after for v, f in zip(value[::-1], factor[::-1])], 0)


def ahead_of(starts, compute):
    coming = compute(starts[0])
    for k, start in enumerate(starts):
        now = coming
        if k + 1 < len(starts):
            coming = compute(starts[k + 1])
        yield start, now


def wide(column, width):
    return jnp.concatenate([column] * (width // LANES), 1)


def unit(x):
    return lax.rsqrt(jnp.mean(x * x, axis=-1, keepdims=True) + EPS)


def norm_back(x, q, gain, d_normed, grad_out):
    x_hat = x * q
    scaled = d_normed * gain
    mean = jnp.mean(scaled * x_hat, axis=-1, keepdims=True)
    d_gain = jnp.sum(d_normed * x_hat, axis=0, keepdims=True)
    return grad_out + q * (scaled - x_hat * mean), d_gain


def gelu_parts(u):
    cdf = 0.5 * lax.erf(u * 0.7071067811865476) + 0.5
    slope = cdf + u * (0.3989422804014327 * jnp.exp(-0.5 * u * u))
    return u * cdf, slope


def kernel(
    count,
    x_hbm, cot_hbm, w_hbm, gain_hbm, len_hbm, fill_hbm,
    ig_ref, dw_ref, dgain_ref, fmean_ref,
    w, wt, res, grad, out, gout, normal, x_own, dy_own, mask, mask_own, keep_col, valid_col, x_ref, cot_ref, gain_ref, len_ref, fill_ref,
    stash, rows, left, forget_acc,
    sib_out, sib_in, outer_in, part, tot_in, guest_in, work,
    small, small_sib, small_outer, small_part, small_tot, small_far,
    w_sem, load_sem, x_send, dy_send, mask_send, res_send, res_recv, grad_send, grad_recv, mask_recv, ig_recv,
    sib_send, sib_recv, part_send, outer_recv, tot_send, tot_recv, fin_send, fin_recv, guest_recv, back_send,
    small_send, small_recv, far_send, far_recv,
):
    s = lax.axis_index("section")
    d = lax.axis_index("dp")
    core = lax.rem(d, 2)
    chip = d // 2
    chips = count // 2
    sections, slot = mask.shape[0], mask.shape[2]
    tokens, width = res.shape
    pack = w.shape[1]
    gate = pack // 4
    ff = pack // 2
    half = pack // 2
    pieces = sib_in.shape[0]
    guests = guest_in.shape[0]
    piece_rows, piece = sib_in.shape[1:]
    stacked = width // piece_rows
    last = sections - 1
    giver, host = 0, last
    is_first = s == 0
    is_last = s == last
    is_mixer = lax.rem(s, 2) == 0
    on_left = chip < chips // 2
    is_middle = (chip == chips // 2 - 1) | (chip == chips // 2)
    is_end = (chip == 0) | (chip == chips - 1)
    other = d + 1 - 2 * core
    sibling = (s, other)
    inner = (s, jnp.where(on_left, d + 2, d - 2))
    outer = (s, jnp.where(on_left, d - 2, d + 2))

    loads = [
        pltpu.make_async_copy(src, dst, load_sem.at[k])
        for k, (src, dst) in enumerate(
            ((x_hbm, x_ref), (len_hbm, len_ref), (fill_hbm, fill_ref), (cot_hbm, cot_ref), (gain_hbm, gain_ref))
        )
    ]
    w_copy = pltpu.make_async_copy(w_hbm, w, w_sem)
    for load in loads:
        load.start()
    w_copy.start()

    barrier = pltpu.get_barrier_semaphore()
    for by in range(1, sections):
        for lane_of in (d, other):
            pl.semaphore_signal(
                barrier, inc=1, device_id=(lax.rem(s + by, sections), lane_of), device_id_type=MESH
            )
    pl.semaphore_signal(barrier, inc=1, device_id=sibling, device_id_type=MESH)

    @pl.when(chip > 0)
    def _():
        pl.semaphore_signal(barrier, inc=1, device_id=(s, d - 2), device_id_type=MESH)

    @pl.when(chip < chips - 1)
    def _():
        pl.semaphore_signal(barrier, inc=1, device_id=(s, d + 2), device_id_type=MESH)

    def remote(src, dst, send, recv, target):
        return pltpu.make_async_remote_copy(
            src_ref=src, dst_ref=dst, send_sem=send, recv_sem=recv, device_id=target, device_id_type=MESH
        )

    order = jnp.where(
        lax.broadcasted_iota(jnp.int32, (slot, slot), 1) == time_of_row(slot, (slot, slot), 0), 1.0, 0.0
    )
    order_low = order.astype(BF16)
    for load in loads:
        load.wait()
    x_own[...] = dot(order_low, x_ref[0]).astype(BF16)
    lane = lax.broadcasted_iota(jnp.int32, (8, slot), 1)
    row = lax.broadcasted_iota(jnp.int32, (8, slot), 0)
    starts = lane == 0
    position = len_ref[0, 0, 0]
    for k in range(1, len_ref.shape[2]):
        starts = starts | (lane == position)
        position = position + len_ref[0, 0, k]
    keep_rows = jnp.where(starts, 0.0, 1.0)
    valid_rows = jnp.where(lane < fill_ref[0, 0], 1.0, 0.0)
    mask_own[...] = jnp.where(row == 0, keep_rows, valid_rows)
    used_rows = jnp.where(time_of_row(slot, (slot, LANES), 0) < fill_ref[0, 0], 1.0, 0.0)
    dy_own[...] = (dot(order_low, cot_ref[0]) * wide(used_rows, width)).astype(BF16)
    forget_acc[...] = jnp.zeros_like(forget_acc)
    small[...] = jnp.zeros_like(small)

    def whole(m):
        return pl.ds(pl.multiple_of(m * slot, slot), slot)

    def res_in(m):
        return remote(
            out.at[whole(m)], res.at[whole(m)], res_send.at[m], res_recv.at[m], (jnp.minimum(s + 1, last), other)
        )

    def grad_in(m):
        return remote(
            gout.at[whole(m)], grad.at[whole(m)], grad_send.at[m], grad_recv.at[m], (jnp.maximum(s - 1, 0), other)
        )

    def home(m, to):
        return remote(gout.at[whole(m)], ig_ref.at[0], grad_send.at[m], ig_recv, (to, d))

    def wait_res(m):
        @pl.when((s != 0) | (m != 0))
        def _():
            res_in(m).wait_recv()

    def send_grad(m):
        @pl.when((s != 0) & (m > 0))
        def _():
            grad_in(m - 1).wait_send()

        @pl.when(s != 0)
        def _():
            grad_in(m).start()

        @pl.when((s == 0) & (m == 0))
        def _():
            ig_ref[0] = gout[whole(m)]

        @pl.when((s == 0) & (m != 0))
        def _():
            home(m, m).start()

    def turn(side, source, m):
        at = whole(m)
        left[side, :, at] = source[at].T

    def turn_weights(start, stop):
        def one(k, carry):
            at = pl.ds(pl.multiple_of(k * TURN, TURN), TURN)
            wt[at, :] = w[:, at].T
            return carry

        lax.fori_loop(start, stop, one, 0)

    def norm_in(m):
        x = res[whole(m)].astype(F32)
        q = unit(x)
        return x, q, (x * q * gain).astype(BF16)

    def finish_back(m, x, q, d_normed):
        d_res, d_gain = norm_back(x, q, gain, d_normed, grad[whole(m)].astype(F32))
        gout[whole(m)] = d_res.astype(BF16)
        send_grad(m)
        small[0:1, :] += d_gain

    gain = gain_ref[...]

    def mixer_forward(m):
        at = whole(m)
        masks = mask[m]
        keep_col[...] = jnp.broadcast_to(jnp.sum(order * masks[0:1], axis=1, keepdims=True), (slot, LANES))
        valid_col[...] = jnp.broadcast_to(jnp.sum(order * masks[1:2], axis=1, keepdims=True), (slot, LANES))
        wait_res(m)
        keep = wide(keep_col[...], GATE_CHUNK)
        valid = wide(valid_col[...], GATE_CHUNK)
        x, _, normed = norm_in(m)
        normal[at] = normed
        total = x

        def project(c):
            return [dot(normed, w[:, k * gate + c : k * gate + c + GATE_CHUNK]) for k in range(3)]

        for c, (f_in, i_in, c_in) in ahead_of(range(0, gate, GATE_CHUNK), project):
            top = jnp.maximum(jnp.maximum(-f_in, -i_in), 0.0)
            e_zero = jnp.exp(-top)
            e_f = jnp.exp(-f_in - top)
            e_i = jnp.exp(-i_in - top)
            u_f = e_zero + e_f
            u_i = e_zero + e_i
            inv = 1.0 / (u_f + u_i)
            forget = u_i * inv
            intake = u_f * inv
            e_c = jnp.exp(-jnp.abs(c_in))
            soft = jnp.maximum(c_in, 0.0) + jnp.log1p(e_c)
            decay = forget * keep
            state, previous = scan_down(decay, intake * soft)
            state_low = state.astype(BF16)
            total = total + dot(state_low, wt[3 * gate + c : 3 * gate + c + GATE_CHUNK, :])
            rows[at, 3 * gate + c : 3 * gate + c + GATE_CHUNK] = state_low
            bend = soft - keep * previous
            stash[at, c : c + GATE_CHUNK] = -forget * (e_f * inv) * bend
            stash[at, gate + c : gate + c + GATE_CHUNK] = intake * (e_i * inv) * bend
            stash[at, 2 * gate + c : 2 * gate + c + GATE_CHUNK] = (
                intake * jnp.where(c_in >= 0.0, 1.0, e_c) / (1.0 + e_c)
            )
            stash[at, 3 * gate + c : 3 * gate + c + GATE_CHUNK] = decay
            counted = forget * valid
            folded = counted[:8]
            for k in range(8, slot, 8):
                folded = folded + counted[k : k + 8]
            forget_acc[...] += folded
        out[at] = total.astype(BF16)

    inner_turns = 3 * gate // TURN

    @pl.when(is_first)
    def _():
        res[0:slot] = x_own[...]
        mask[0] = mask_own[...]
        w_copy.wait()
        turn_weights(inner_turns, pack // TURN)
        mixer_forward(0)

    pl.semaphore_wait(
        barrier, 2 * sections - 1 + jnp.where(chip > 0, 1, 0) + jnp.where(chip < chips - 1, 1, 0)
    )

    x_copy = remote(x_own, res.at[whole(s)], x_send, res_recv.at[s], (0, d))
    dy_copy = remote(
        dy_own, grad.at[whole(s)], dy_send, grad_recv.at[s], (last, jnp.where(last % 2 == 1, other, d))
    )
    mask_copies = [
        remote(mask_own, mask.at[s], mask_send.at[k], mask_recv.at[s], (2 * k, d))
        for k in range(sections // 2)
    ]

    for k in range(sections // 2):

        @pl.when((s == 2 * k) & (s != 0))
        def _():
            mask[s] = mask_own[...]

        @pl.when(s != 2 * k)
        def _():
            mask_copies[k].start()

    def start_first():
        @pl.when(is_first)
        def _():
            res_in(0).start()

        @pl.when(s != 0)
        def _():
            x_copy.start()

    @pl.when(s != 0)
    def _():
        w_copy.wait()

    @pl.when(core == 0)
    def _():
        start_first()

    turn_weights(0, inner_turns)

    @pl.when(core == 1)
    def _():
        start_first()

    @pl.when(is_first)
    def _():
        turn(0, normal, 0)
        res_in(0).wait_send()

    @pl.when(s != 0)
    def _():
        turn_weights(inner_turns, pack // TURN)

    dy_copy.start()

    @pl.when(is_mixer)
    def _():
        begin = jnp.where(is_first, 1, 0)

        def forward(m, carry):
            @pl.when(m != s)
            def _():
                remote(mask_own, mask.at[m], mask_send.at[0], mask_recv.at[m], (0, d)).wait_recv()

            mixer_forward(m)

            @pl.when(m > begin)
            def _():
                res_in(m - 1).wait_send()

            res_in(m).start()
            turn(0, normal, m)
            return carry

        lax.fori_loop(begin, sections, forward, 0)

        def backward(m, carry):
            at = whole(m)
            x, q, _ = norm_in(m)
            grad_in(m).wait_recv()
            g_low = grad[at]
            d_normed = jnp.zeros((slot, width), F32)

            def project(c):
                return dot(g_low, w[:, 3 * gate + c : 3 * gate + c + BACK_CHUNK])

            for c, d_state in ahead_of(range(0, gate, BACK_CHUNK), project):
                adjoint = scan_up(stash[at, 3 * gate + c : 3 * gate + c + BACK_CHUNK], d_state)
                for k in range(3):
                    here = slice(k * gate + c, k * gate + c + BACK_CHUNK)
                    low = (adjoint * stash[at, here]).astype(BF16)
                    rows[at, here] = low
                    d_normed = d_normed + dot(low, wt[here, :])
            finish_back(m, x, q, d_normed)
            turn(1, grad, m)
            return carry

        lax.fori_loop(0, sections, backward, 0)

    @pl.when((lax.rem(s, 2) == 1) & (s != last))
    def _():
        def forward(m, carry):
            wait_res(m)
            at = whole(m)
            x, _, normed = norm_in(m)
            normal[at] = normed
            total = x

            def project(c):
                return dot(normed, w[:, c : c + DENSE_CHUNK])

            for c, hidden_in in ahead_of(range(0, ff, DENSE_CHUNK), project):
                hidden, bend = gelu_parts(hidden_in)
                low = hidden.astype(BF16)
                total = total + dot(low, wt[ff + c : ff + c + DENSE_CHUNK, :])
                rows[at, ff + c : ff + c + DENSE_CHUNK] = low
                stash[at, c : c + DENSE_CHUNK] = bend
            out[at] = total.astype(BF16)

            @pl.when(m > 0)
            def _():
                res_in(m - 1).wait_send()

            res_in(m).start()
            turn(0, normal, m)
            return carry

        lax.fori_loop(0, sections, forward, 0)

        def backward(m, carry):
            at = whole(m)
            x, q, _ = norm_in(m)
            grad_in(m).wait_recv()
            g_low = grad[at]
            d_normed = jnp.zeros((slot, width), F32)

            def project(c):
                return dot(g_low, w[:, ff + c : ff + c + DENSE_CHUNK])

            for c, d_act in ahead_of(range(0, ff, DENSE_CHUNK), project):
                low = (d_act * stash[at, c : c + DENSE_CHUNK]).astype(BF16)
                rows[at, c : c + DENSE_CHUNK] = low
                d_normed = d_normed + dot(low, wt[c : c + DENSE_CHUNK, :])
            finish_back(m, x, q, d_normed)
            turn(1, grad, m)
            return carry

        lax.fori_loop(0, sections, backward, 0)

    @pl.when(is_last)
    def _():
        def prepare(k, carry):
            m = last - k
            grad_in(m).wait_recv()
            at = whole(m)
            g_low = grad[at]
            for c in range(0, ff, DENSE_CHUNK):
                stash[at, c : c + DENSE_CHUNK] = dot(g_low, w[:, ff + c : ff + c + DENSE_CHUNK])
            turn(1, grad, m)
            return carry

        lax.fori_loop(0, sections, prepare, 0)

        def both(m, carry):
            wait_res(m)
            at = whole(m)
            x, q, normed = norm_in(m)
            normal[at] = normed
            d_normed = jnp.zeros((slot, width), F32)

            def project(c):
                return dot(normed, w[:, c : c + LAST_CHUNK])

            for c, hidden_in in ahead_of(range(0, ff, LAST_CHUNK), project):
                hidden, bend = gelu_parts(hidden_in)
                rows[at, ff + c : ff + c + LAST_CHUNK] = hidden.astype(BF16)
                low = (stash[at, c : c + LAST_CHUNK] * bend).astype(BF16)
                rows[at, c : c + LAST_CHUNK] = low
                d_normed = d_normed + dot(low, wt[c : c + LAST_CHUNK, :])
            finish_back(m, x, q, d_normed)
            turn(0, normal, m)
            return carry

        lax.fori_loop(0, sections, both, 0)

    @pl.when(is_mixer)
    def _():
        small[1:2, 0:GATE_CHUNK] = jnp.sum(forget_acc[...], axis=0, keepdims=True)
        used = mask[0, 1:2]
        for m in range(1, sections):
            used = used + mask[m, 1:2]
        small[2:3, 0:slot] = used

    split = jnp.where(is_mixer, 3 * gate, ff)

    def rows_at(k):
        return pl.ds(pl.multiple_of(lax.rem(k, stacked) * piece_rows, piece_rows), piece_rows)

    def cols_at(k, part_of):
        return pl.ds(pl.multiple_of(part_of * half + k // stacked * piece, piece), piece)

    def grad_piece(k, part_of):
        side = jnp.where(part_of * half + k // stacked * piece < split, 0, 1)
        return dot(left[side, rows_at(k)], rows[:, cols_at(k, part_of)])

    def sib_copy(k):
        return remote(sib_out.at[k], sib_in.at[k], sib_send, sib_recv.at[k], sibling)

    def inward(k):
        return remote(part.at[k], outer_in.at[k], part_send, outer_recv.at[k], inner)

    def across(k):
        return remote(part.at[k], tot_in.at[k], part_send, tot_recv.at[k], inner)

    def outward(k):
        return remote(tot_in.at[k], tot_in.at[k], tot_send, tot_recv.at[k], outer)

    def lend(k):
        return remote(part.at[2 * k + 1], guest_in.at[k], part_send, guest_recv.at[k], (host, d))

    def give_back(k):
        return remote(tot_in.at[pieces + k], tot_in.at[2 * k + 1], back_send, tot_recv.at[2 * k + 1], (giver, d))

    def final(k):
        return remote(
            tot_in.at[k], dw_ref.at[rows_at(k), cols_at(k, core)], fin_send, fin_recv, sibling
        )

    small_swap = remote(small, small_sib, small_send.at[0], small_recv.at[0], sibling)
    small_inward = remote(small_part, small_outer, small_send.at[1], small_recv.at[1], inner)
    small_across = remote(small_part, small_tot, small_send.at[1], small_recv.at[2], inner)
    small_outward = remote(small_tot, small_tot, small_send.at[2], small_recv.at[2], outer)

    def to_sibling(k):
        sib_out[k] = grad_piece(k, 1 - core).astype(BF16)
        sib_copy(k).start()

    to_sibling(0)
    small_swap.start()

    def reduce_small():
        small_swap.wait_recv()

        @pl.when(is_end)
        def _():
            small_part[...] = small[...] + small_sib[...]

        @pl.when(jnp.logical_not(is_end))
        def _():
            small_inward.wait_recv()
            small_part[...] = small[...] + small_sib[...] + small_outer[...]

        @pl.when(is_middle)
        def _():
            small_across.start()

        @pl.when(jnp.logical_not(is_middle))
        def _():
            small_inward.start()

    def far_copy(k):
        return remote(
            small_tot, small_far.at[s // 2], far_send.at[k - 1], far_recv.at[s // 2], (lax.rem(s + k, sections), other)
        )

    def total_small():
        small_across.wait_recv()

        @pl.when(is_middle)
        def _():
            small_tot[...] = small_tot[...] + small_part[...]

        @pl.when(jnp.logical_not(is_end))
        def _():
            small_outward.start()

        @pl.when(is_mixer)
        def _():
            small_far[s // 2] = small_tot[...]
            for k in range(1, sections):
                far_copy(k).start()

    def is_lent(k):
        return (s == giver) & (k < 2 * guests) & (lax.rem(k, 2) == 1)

    def reduce_piece(k):
        @pl.when(k < pieces)
        def _():
            work[...] = grad_piece(k, core)
            sib_copy(k).wait_recv()
            work[...] += sib_in[k].astype(F32)

        @pl.when(k >= pieces)
        def _():
            lend(k - pieces).wait_recv()
            work[...] = guest_in[k - pieces].astype(F32)

        on_line = jnp.logical_not(is_lent(k))

        @pl.when(is_lent(k) | is_end)
        def _():
            part[k] = work[...].astype(BF16)

        @pl.when(on_line & jnp.logical_not(is_end))
        def _():
            inward(k).wait_recv()
            part[k] = (work[...] + outer_in[k].astype(F32)).astype(BF16)

        @pl.when(is_lent(k))
        def _():
            lend(k // 2).start()

        @pl.when(on_line & is_middle)
        def _():
            across(k).start()

        @pl.when(on_line & jnp.logical_not(is_middle))
        def _():
            inward(k).start()

    def total_piece(k):
        across(k).wait_recv()
        on_line = jnp.logical_not(is_lent(k))

        @pl.when(on_line & is_middle)
        def _():
            tot_in[k] = (tot_in[k].astype(F32) + part[k].astype(F32)).astype(BF16)

        @pl.when(on_line & jnp.logical_not(is_end))
        def _():
            outward(k).start()

        @pl.when(k < pieces)
        def _():
            final(k).start()
            dw_ref[rows_at(k), cols_at(k, core)] = tot_in[k]

        @pl.when(k >= pieces)
        def _():
            give_back(k - pieces).start()

    on_list = pieces + jnp.where(s == host, guests, 0)
    lent = jnp.where(s == giver, guests, 0)
    lag = jnp.where(is_middle, lent + LAG, on_list)

    def in_order(p):
        return jnp.where(
            p < lent, 2 * p, jnp.where(p < on_list - lent, p + lent, 2 * (p - (on_list - lent)) + 1)
        )

    def step(i, carry):
        @pl.when(i + 1 < pieces)
        def _():
            to_sibling(i + 1)

        @pl.when(i < on_list)
        def _():
            reduce_piece(i)

        @pl.when(i == SMALL_STEP)
        def _():
            reduce_small()

        @pl.when(i == lag + SMALL_STEP)
        def _():
            total_small()

        @pl.when(i >= lag)
        def _():
            total_piece(jnp.where(s == giver, in_order(i - lag), i - lag))

        return carry

    lax.fori_loop(0, on_list + lag, step, 0)

    for k in range(sections // 2):

        @pl.when(s != 2 * k)
        def _():
            remote(small_tot, small_far.at[k], far_send.at[0], far_recv.at[k], sibling).wait_recv()

    dgain_ref[...] = small_tot[0:1, :]
    lanes = lax.broadcasted_iota(jnp.int32, (1, LANES), 1)
    means = jnp.zeros((1, LANES), F32)
    for k in range(sections // 2):
        sums = jnp.sum(small_far[k], axis=1, keepdims=True)
        means = jnp.where(lanes == k, sums[1:2] / (sums[2:3] * gate), means)
    fmean_ref[...] = means

    @pl.when(s != 0)
    def _():
        home(0, s).wait_recv()
        x_copy.wait_send()
        grad_in(last).wait_send()

    @pl.when(is_first)
    def _():
        for m in range(1, sections):
            grad_in(m).wait_send()

    dy_copy.wait_send()

    for k in range(sections // 2):

        @pl.when(s != 2 * k)
        def _():
            mask_copies[k].wait_send()

    @pl.when(s != last)
    def _():
        res_in(last).wait_send()

    small_swap.wait_send()
    small_across.wait_send()

    @pl.when(jnp.logical_not(is_end))
    def _():
        small_outward.wait_send()

    @pl.when(is_mixer)
    def _():
        for k in range(1, sections):
            far_copy(k).wait_send()

    remote(sib_out, sib_in, sib_send, sib_recv.at[0], sibling).wait_send()

    def sent(source, sem, n):
        remote(source.at[pl.ds(0, n)], source.at[pl.ds(0, n)], sem, sib_recv.at[0], sibling).wait_send()

    for n, holds in ((pieces - guests, s == giver), (pieces, (s != giver) & (s != host)), (pieces + guests, s == host)):

        @pl.when(holds & jnp.logical_not(is_end))
        def _():
            sent(tot_in, tot_send, n)

    @pl.when(s == host)
    def _():
        sent(part, part_send, pieces + guests)
        sent(guest_in, back_send, guests)

    @pl.when(s != host)
    def _():
        sent(part, part_send, pieces)

    sent(tot_in, fin_send, pieces)
    their_half = dw_ref.at[:, pl.ds(pl.multiple_of((1 - core) * half, half), half)]
    remote(their_half, their_half, fin_send, fin_recv, sibling).wait_recv()


def finish_kernel(dw_ref, ig_ref, dgain_ref, fmean_ref, ig_out, dw_out, dgain_out, fmean_out, wide_dw, sem):
    dgain_out[...] = dgain_ref[0]
    fmean_out[...] = fmean_ref[0, : fmean_out.shape[0]]
    slots, step = wide_dw.shape[:2]
    steps = dw_ref.shape[0] // step

    def copy(k):
        at = pl.ds(pl.multiple_of(k * step, step), step)
        return pltpu.make_async_copy(wide_dw.at[lax.rem(k, slots)], dw_out.at[at], sem.at[lax.rem(k, slots)])

    for k in range(steps):
        if k >= slots:
            copy(k - slots).wait()
        wide_dw[k % slots] = dw_ref[k * step : (k + 1) * step].astype(F32)
        copy(k).start()
    slot = ig_ref.shape[1]
    token_rows = lax.broadcasted_iota(jnp.int32, (slot, slot), 0)
    order = jnp.where(time_of_row(slot, (slot, slot), 1) == token_rows, 1.0, 0.0).astype(BF16)
    ig_out[0] = dot(order, ig_ref[0]).astype(BF16)
    for k in range(steps - slots, steps):
        copy(k).wait()


def finish(input_grad, weight_grads, gain_grads, means, sections):
    width, pack = weight_grads.shape
    vmem = pl.BlockSpec(memory_space=pltpu.VMEM)
    return pl.pallas_call(
        finish_kernel,
        out_shape=(
            jax.ShapeDtypeStruct(input_grad.shape, BF16),
            jax.ShapeDtypeStruct(weight_grads.shape, F32),
            jax.ShapeDtypeStruct((width,), F32),
            jax.ShapeDtypeStruct((sections // 2,), F32),
        ),
        in_specs=[vmem] * 4,
        out_specs=(vmem, pl.BlockSpec(memory_space=pl.ANY), vmem, vmem),
        scratch_shapes=[pltpu.VMEM((4, FINISH_ROWS, pack), F32), pltpu.SemaphoreType.DMA((4,))],
        compiler_params=pltpu.CompilerParams(vmem_limit_bytes=16 * 1024 * 1024),
    )(weight_grads, input_grad, gain_grads, means)


def local(count, inputs, cotangent, section_weights, norm_gains, doc_lengths, slot_fill):
    sections = lax.axis_size("section")
    slot, width = inputs.shape[1:]
    pack = section_weights.shape[1]
    gate, ff, half = pack // 4, pack // 2, pack // 2
    tokens = sections * slot
    pieces = half * width // (PIECE[0] * PIECE[1])
    dma = pltpu.SemaphoreType.DMA
    own = pltpu.VMEM((pieces, *PIECE), BF16)
    hosted = pltpu.VMEM((pieces + GUESTS, *PIECE), BF16)
    small = pltpu.VMEM((8, width), F32)
    stack = pltpu.VMEM((tokens, width), BF16)
    vmem = pl.BlockSpec(memory_space=pltpu.VMEM)
    anywhere = pl.BlockSpec(memory_space=pl.ANY)
    input_grad, weight_grads, gain_grads, means = pl.pallas_call(
        functools.partial(kernel, count),
        out_shape=(
            pltpu.VMEM((1, slot, width), BF16),
            pltpu.VMEM((width, pack), BF16),
            pltpu.VMEM((1, width), F32),
            pltpu.VMEM((1, LANES), F32),
        ),
        in_specs=[anywhere] * 6,
        out_specs=(vmem, vmem, vmem, vmem),
        scratch_shapes=[
            pltpu.VMEM((width, pack), BF16), pltpu.VMEM((pack, width), BF16),
            stack, stack, stack, stack, stack,
            pltpu.VMEM((slot, width), BF16), pltpu.VMEM((slot, width), BF16),
            pltpu.VMEM((sections, 8, slot), F32), pltpu.VMEM((8, slot), F32),
            pltpu.VMEM((slot, LANES), F32), pltpu.VMEM((slot, LANES), F32),
            pltpu.VMEM(inputs.shape, BF16), pltpu.VMEM(inputs.shape, BF16), pltpu.VMEM((1, width), F32),
            pltpu.SMEM(doc_lengths.shape, jnp.int32), pltpu.SMEM(slot_fill.shape, jnp.int32),
            pltpu.VMEM((tokens, pack), F32),
            pltpu.VMEM((tokens, pack), BF16),
            pltpu.VMEM((2, width, tokens), BF16),
            pltpu.VMEM((8, GATE_CHUNK), F32),
            own, own, hosted, hosted, hosted,
            pltpu.VMEM((GUESTS, *PIECE), BF16), pltpu.VMEM(PIECE, F32),
            small, small, small, small, small,
            pltpu.VMEM((sections // 2, 8, width), F32),
            dma, dma((5,)), dma, dma,
            dma((sections // 2,)),
            dma((sections,)), dma((sections,)), dma((sections,)), dma((sections,)),
            dma((sections,)), dma,
            dma, dma((pieces,)), dma, dma((pieces + GUESTS,)),
            dma, dma((pieces + GUESTS,)), dma, dma, dma((GUESTS,)), dma,
            dma((3,)), dma((3,)), dma((sections - 1,)), dma((sections // 2,)),
        ],
        compiler_params=pltpu.CompilerParams(
            collective_id=0, has_side_effects=True, vmem_limit_bytes=56 * 1024 * 1024
        ),
    )(inputs, cotangent, section_weights, norm_gains.reshape(1, width), doc_lengths, slot_fill)
    return finish(input_grad, weight_grads, gain_grads, means, sections)


def solution(mesh):
    placed = (
        P("section", "dp", None),
        P("section", "dp", None),
        P("section", None),
        P("section"),
        P("section", "dp", None),
        P("section", "dp"),
    )
    return jax.shard_map(
        functools.partial(local, mesh.shape["dp"]),
        mesh=mesh,
        in_specs=placed,
        out_specs=(P("section", "dp", None), P("section", None), P("section"), P()),
        check_vma=False,
    )
```

```python
import functools

import jax
import jax.numpy as jnp
from jax import lax
from jax.experimental import pallas as pl
from jax.experimental.pallas import tpu as pltpu
from jax.sharding import PartitionSpec as P

EPS = 1e-06
MESH = pl.DeviceIdType.MESH
F32 = jnp.float32
BF16 = jnp.bfloat16
LANES = 128
GATE_CHUNK = 256
BACK_CHUNK = 512
DENSE_CHUNK = 512
LAST_CHUNK = 256
TURN = 256
PIECE = (256, 128)
LENT = (7, 2)
HOST_AT = 24
SUB = 1
LAG = 2
STRIDE = 3
AHEAD = 2
SECOND_TURNS = 14
FIRST_TURNS = 4
SMALL_STEP = 3
FINISH_ROWS = 32


def dot(left, right):
    return jnp.dot(left, right, preferred_element_type=F32)


def time_of_row(slot, shape, axis):
    row = lax.broadcasted_iota(jnp.int32, shape, axis)
    return (row & 7) * (slot // 8) + (row >> 3)


def scan_down(decay, drive):
    blocks = range(8, decay.shape[0], 8)
    factor, value = [decay[:8]], [drive[:8]]
    for at in blocks:
        here = decay[at : at + 8]
        value.append(drive[at : at + 8] + here * value[-1])
        factor.append(here * factor[-1])
    joined, through = value[-1], factor[-1]
    for by in (1, 2, 4):
        joined = joined + through * pltpu.roll(joined, by, 0)
        through = through * pltpu.roll(through, by, 0)
    before = pltpu.roll(joined, 1, 0)
    state = [v + f * before for v, f in zip(value, factor)]
    return jnp.concatenate(state, 0), jnp.concatenate([before] + state[:-1], 0)


def scan_up(decay, source):
    rows = decay.shape[0]
    ahead = [decay[at : at + 8] for at in range(8, rows, 8)] + [pltpu.roll(decay[:8], 7, 0)]
    factor, value = [ahead[-1]], [source[rows - 8 :]]
    for k in range(rows // 8 - 2, -1, -1):
        value.append(source[8 * k : 8 * k + 8] + ahead[k] * value[-1])
        factor.append(ahead[k] * factor[-1])
    joined, through = value[-1], factor[-1]
    for by in (1, 2, 4):
        joined = joined + through * pltpu.roll(joined, 8 - by, 0)
        through = through * pltpu.roll(through, 8 - by, 0)
    after = pltpu.roll(joined, 7, 0)
    return jnp.concatenate([v + f * after for v, f in zip(value[::-1], factor[::-1])], 0)


def ahead_of(starts, compute):
    coming = compute(starts[0])
    for k, start in enumerate(starts):
        now = coming
        if k + 1 < len(starts):
            coming = compute(starts[k + 1])
        yield start, now


def wide(column, width):
    return jnp.concatenate([column] * (width // LANES), 1)


def unit(x):
    return lax.rsqrt(jnp.mean(x * x, axis=-1, keepdims=True) + EPS)


def norm_back(x, q, gain, d_normed, grad_out):
    x_hat = x * q
    scaled = d_normed * gain
    mean = jnp.mean(scaled * x_hat, axis=-1, keepdims=True)
    d_gain = jnp.sum(d_normed * x_hat, axis=0, keepdims=True)
    return grad_out + q * (scaled - x_hat * mean), d_gain


def gelu_parts(u):
    cdf = 0.5 * lax.erf(u * 0.7071067811865476) + 0.5
    slope = cdf + u * (0.3989422804014327 * jnp.exp(-0.5 * u * u))
    return u * cdf, slope


def kernel(
    count,
    x_hbm, cot_hbm, w_hbm, gain_hbm, len_hbm, fill_hbm,
    ig_ref, dw_ref, dgain_ref, fmean_ref,
    w, wt, res, grad, out, gout, normal, x_own, dy_own, mask, mask_own, keep_col, valid_col, relay, x_ref, cot_ref, gain_ref, len_ref, fill_ref,
    stash, rows, left, forget_acc,
    sib_out, sib_in, outer_in, part, tot_in, guest_in, work,
    small, small_sib, small_outer, small_part, small_tot, small_far,
    w_sem, load_sem, x_send, dy_send, mask_send, res_send, res_recv, grad_send, grad_recv, mask_recv, ig_recv, relay_send, relay_recv, turn_sem,
    sib_send, sib_recv, part_send, outer_recv, tot_send, tot_recv, fin_send, fin_recv, guest_recv, back_send,
    small_send, small_recv, far_send, far_recv,
):
    s = lax.axis_index("section")
    d = lax.axis_index("dp")
    core = lax.rem(d, 2)
    chip = d // 2
    chips = count // 2
    sections, slot = mask.shape[0], mask.shape[2]
    tokens, width = res.shape
    pack = w.shape[1]
    gate = pack // 4
    ff = pack // 2
    half = pack // 2
    pieces = sib_in.shape[0]
    piece_rows, piece = sib_in.shape[1:]
    stacked = width // piece_rows
    last = sections - 1
    partner = last - s
    lent = jnp.where(s == 0, LENT[0], jnp.where(s == 1, LENT[1], 0))
    hosted = jnp.where(partner == 0, LENT[0], jnp.where(partner == 1, LENT[1], 0))
    mine = lax.rem(core + chip, 2)
    is_first = s == 0
    is_last = s == last
    is_mixer = lax.rem(s, 2) == 0
    on_left = chip < chips // 2
    is_middle = (chip == chips // 2 - 1) | (chip == chips // 2)
    is_end = (chip == 0) | (chip == chips - 1)
    other = d + 1 - 2 * core
    sibling = (s, other)
    inner = (s, jnp.where(on_left, other + 2, other - 2))
    outer = (s, jnp.where(on_left, other - 2, other + 2))

    loads = [
        pltpu.make_async_copy(src, dst, load_sem.at[k])
        for k, (src, dst) in enumerate(
            ((x_hbm, x_ref), (len_hbm, len_ref), (fill_hbm, fill_ref), (cot_hbm, cot_ref), (gain_hbm, gain_ref))
        )
    ]
    w_copy = pltpu.make_async_copy(w_hbm, w, w_sem)
    for load in loads:
        load.start()
    w_early = is_first | is_last | (core == 1)

    @pl.when(w_early)
    def _():
        w_copy.start()

    barrier = pltpu.get_barrier_semaphore()
    for by in range(1, sections):
        for lane_of in (d, other):
            pl.semaphore_signal(
                barrier, inc=1, device_id=(lax.rem(s + by, sections), lane_of), device_id_type=MESH
            )
    pl.semaphore_signal(barrier, inc=1, device_id=sibling, device_id_type=MESH)

    @pl.when(chip > 0)
    def _():
        pl.semaphore_signal(barrier, inc=1, device_id=(s, other - 2), device_id_type=MESH)

    @pl.when(chip < chips - 1)
    def _():
        pl.semaphore_signal(barrier, inc=1, device_id=(s, other + 2), device_id_type=MESH)

    def remote(src, dst, send, recv, target):
        return pltpu.make_async_remote_copy(
            src_ref=src, dst_ref=dst, send_sem=send, recv_sem=recv, device_id=target, device_id_type=MESH
        )

    order = jnp.where(
        lax.broadcasted_iota(jnp.int32, (slot, slot), 1) == time_of_row(slot, (slot, slot), 0), 1.0, 0.0
    )
    order_low = order.astype(BF16)
    for load in loads:
        load.wait()
    x_own[...] = dot(order_low, x_ref[0]).astype(BF16)
    lane = lax.broadcasted_iota(jnp.int32, (8, slot), 1)
    row = lax.broadcasted_iota(jnp.int32, (8, slot), 0)
    starts = lane == 0
    position = len_ref[0, 0, 0]
    for k in range(1, len_ref.shape[2]):
        starts = starts | (lane == position)
        position = position + len_ref[0, 0, k]
    keep_rows = jnp.where(starts, 0.0, 1.0)
    valid_rows = jnp.where(lane < fill_ref[0, 0], 1.0, 0.0)
    mask_own[...] = jnp.where(row == 0, keep_rows, valid_rows)
    used_rows = jnp.where(time_of_row(slot, (slot, LANES), 0) < fill_ref[0, 0], 1.0, 0.0)
    dy_own[...] = (dot(order_low, cot_ref[0]) * wide(used_rows, width)).astype(BF16)
    forget_acc[...] = jnp.zeros_like(forget_acc)
    small[...] = jnp.zeros_like(small)

    def whole(m):
        return pl.ds(pl.multiple_of(m * slot, slot), slot)

    def res_in(m):
        return remote(
            out.at[whole(m)], res.at[whole(m)], res_send.at[m], res_recv.at[m], (jnp.minimum(s + 1, last), other)
        )

    def grad_in(m):
        return remote(
            gout.at[whole(m)], grad.at[whole(m)], grad_send.at[m], grad_recv.at[m], (jnp.maximum(s - 1, 0), other)
        )

    def home(m, to):
        return remote(gout.at[whole(m)], ig_ref.at[0], grad_send.at[m], ig_recv, (to, d))

    def wait_res(m):
        @pl.when((s != 0) | (m != 0))
        def _():
            res_in(m).wait_recv()

    def send_grad(m):
        @pl.when(s != 0)
        def _():
            grad_in(m).start()

        @pl.when((s == 0) & (m == 0))
        def _():
            ig_ref[0] = gout[whole(m)]

        @pl.when((s == 0) & (m != 0))
        def _():
            home(m, m).start()

    def turn(side, source, m):
        at = whole(m)
        left[side, :, at] = source[at].T

    def turn_weights(start, stop):
        def one(k, carry):
            at = pl.ds(pl.multiple_of(k * TURN, TURN), TURN)
            wt[at, :] = w[:, at].T
            return carry

        lax.fori_loop(start, stop, one, 0)

    def norm_in(m):
        x = res[whole(m)].astype(F32)
        q = unit(x)
        return x, q, (x * q * gain).astype(BF16)

    def finish_back(m, x, q, d_normed):
        d_res, d_gain = norm_back(x, q, gain, d_normed, grad[whole(m)].astype(F32))
        gout[whole(m)] = d_res.astype(BF16)
        send_grad(m)
        small[0:1, :] += d_gain

    gain = gain_ref[...]

    def mixer_forward(m, halfway=None):
        at = whole(m)
        masks = mask[m]
        keep_col[...] = jnp.broadcast_to(jnp.sum(order * masks[0:1], axis=1, keepdims=True), (slot, LANES))
        valid_col[...] = jnp.broadcast_to(jnp.sum(order * masks[1:2], axis=1, keepdims=True), (slot, LANES))
        wait_res(m)
        keep = wide(keep_col[...], GATE_CHUNK)
        valid = wide(valid_col[...], GATE_CHUNK)
        x, _, normed = norm_in(m)
        normal[at] = normed
        total = x

        def project(c):
            return [dot(normed, w[:, k * gate + c : k * gate + c + GATE_CHUNK]) for k in range(3)]

        for c, (f_in, i_in, c_in) in ahead_of(range(0, gate, GATE_CHUNK), project):
            top = jnp.maximum(jnp.maximum(-f_in, -i_in), 0.0)
            e_zero = jnp.exp(-top)
            e_f = jnp.exp(-f_in - top)
            e_i = jnp.exp(-i_in - top)
            u_f = e_zero + e_f
            u_i = e_zero + e_i
            inv = 1.0 / (u_f + u_i)
            forget = u_i * inv
            intake = u_f * inv
            e_c = jnp.exp(-jnp.abs(c_in))
            soft = jnp.maximum(c_in, 0.0) + jnp.log1p(e_c)
            decay = forget * keep
            state, previous = scan_down(decay, intake * soft)
            state_low = state.astype(BF16)
            total = total + dot(state_low, wt[3 * gate + c : 3 * gate + c + GATE_CHUNK, :])
            rows[at, 3 * gate + c : 3 * gate + c + GATE_CHUNK] = state_low
            bend = soft - keep * previous
            if halfway is not None and c == gate // 4:
                halfway()
            stash[at, c : c + GATE_CHUNK] = -forget * (e_f * inv) * bend
            stash[at, gate + c : gate + c + GATE_CHUNK] = intake * (e_i * inv) * bend
            stash[at, 2 * gate + c : 2 * gate + c + GATE_CHUNK] = (
                intake * jnp.where(c_in >= 0.0, 1.0, e_c) / (1.0 + e_c)
            )
            stash[at, 3 * gate + c : 3 * gate + c + GATE_CHUNK] = decay
            counted = forget * valid
            folded = counted[:8]
            for k in range(8, slot, 8):
                folded = folded + counted[k : k + 8]
            forget_acc[...] += folded
        out[at] = total.astype(BF16)

    inner_turns = 3 * gate // TURN

    @pl.when(is_first)
    def _():
        res[0:slot] = x_own[...]
        mask[0] = mask_own[...]
        w_copy.wait()
        turn_weights(inner_turns, pack // TURN)
        mixer_forward(0)

    pl.semaphore_wait(
        barrier, 2 * sections - 1 + jnp.where(chip > 0, 1, 0) + jnp.where(chip < chips - 1, 1, 0)
    )

    x_copy = remote(x_own, res.at[whole(s)], x_send, res_recv.at[s], (0, d))
    dy_copy = remote(
        dy_own, grad.at[whole(s)], dy_send, grad_recv.at[s], (last, jnp.where(last % 2 == 1, other, d))
    )
    dy_relayed = remote(dy_own, relay, dy_send, relay_recv, (2, d))
    dy_onward = remote(relay, grad.at[whole(0)], relay_send, grad_recv.at[0], (last, other))
    mask_copies = [
        remote(mask_own, mask.at[s], mask_send.at[k], mask_recv.at[s], (2 * k, d))
        for k in range(sections // 2)
    ]

    for k in range(sections // 2):

        @pl.when((s == 2 * k) & (s != 0))
        def _():
            mask[s] = mask_own[...]

        @pl.when(s != 2 * k)
        def _():
            mask_copies[k].start()

    @pl.when(jnp.logical_not(w_early))
    def _():
        x_copy.start()
        x_copy.wait_send()
        w_copy.start()

    @pl.when(s != 0)
    def _():
        w_copy.wait()
        turn_weights(0, SECOND_TURNS)

        @pl.when((s != last) & (core == 1))
        def _():
            x_copy.start()

        turn_weights(SECOND_TURNS, pack // TURN)

        @pl.when(s == last)
        def _():
            x_copy.start()

    @pl.when(is_first)
    def _():
        @pl.when(core == 0)
        def _():
            res_in(0).start()

        dy_relayed.start()
        turn_weights(0, FIRST_TURNS)

        @pl.when(core == 1)
        def _():
            res_in(0).start()

        turn(0, normal, 0)

    def give_turn():
        pl.semaphore_signal(turn_sem, inc=1, device_id=sibling, device_id_type=MESH)

    def take_turn():
        pl.semaphore_wait(turn_sem, 1)

    @pl.when(s != 0)
    def _():
        dy_copy.start()

    @pl.when(is_mixer)
    def _():
        @pl.when(s == 2)
        def _():
            dy_relayed.wait_recv()
            dy_onward.start()

        def forward(m, carry):
            @pl.when(m != s)
            def _():
                remote(mask_own, mask.at[m], mask_send.at[0], mask_recv.at[m], (0, d)).wait_recv()

            mixer_forward(m)

            @pl.when(is_first & (core == 1))
            def _():
                take_turn()

            res_in(m).start()
            turn(0, normal, m)
            return carry

        lax.fori_loop(jnp.where(is_first, 1, 0), jnp.where(is_first, 2, sections), forward, 0)

        @pl.when(is_first)
        def _():
            def by_turns(m, carry):
                remote(mask_own, mask.at[m], mask_send.at[0], mask_recv.at[m], (0, d)).wait_recv()
                mixer_forward(m, give_turn)
                take_turn()
                res_in(m).start()
                turn(0, normal, m)
                return carry

            lax.fori_loop(2, sections, by_turns, 0)
            turn_weights(FIRST_TURNS, inner_turns)

            @pl.when(core == 0)
            def _():
                give_turn()

        def backward(m, carry):
            at = whole(m)
            x, q, _ = norm_in(m)
            grad_in(m).wait_recv()
            g_low = grad[at]
            d_normed = jnp.zeros((slot, width), F32)

            def project(c):
                return dot(g_low, w[:, 3 * gate + c : 3 * gate + c + BACK_CHUNK])

            for c, d_state in ahead_of(range(0, gate, BACK_CHUNK), project):
                adjoint = scan_up(stash[at, 3 * gate + c : 3 * gate + c + BACK_CHUNK], d_state)
                for k in range(3):
                    here = slice(k * gate + c, k * gate + c + BACK_CHUNK)
                    low = (adjoint * stash[at, here]).astype(BF16)
                    rows[at, here] = low
                    d_normed = d_normed + dot(low, wt[here, :])
            finish_back(m, x, q, d_normed)
            turn(1, grad, m)
            return carry

        lax.fori_loop(0, sections, backward, 0)

    @pl.when((lax.rem(s, 2) == 1) & (s != last))
    def _():
        def forward(m, carry):
            wait_res(m)
            at = whole(m)
            x, _, normed = norm_in(m)
            normal[at] = normed
            total = x

            def project(c):
                return dot(normed, w[:, c : c + DENSE_CHUNK])

            for c, hidden_in in ahead_of(range(0, ff, DENSE_CHUNK), project):
                hidden, bend = gelu_parts(hidden_in)
                low = hidden.astype(BF16)
                total = total + dot(low, wt[ff + c : ff + c + DENSE_CHUNK, :])
                rows[at, ff + c : ff + c + DENSE_CHUNK] = low
                stash[at, c : c + DENSE_CHUNK] = bend
            out[at] = total.astype(BF16)

            res_in(m).start()
            turn(0, normal, m)
            return carry

        lax.fori_loop(0, sections, forward, 0)

        def backward(m, carry):
            at = whole(m)
            x, q, _ = norm_in(m)
            grad_in(m).wait_recv()
            g_low = grad[at]
            d_normed = jnp.zeros((slot, width), F32)

            def project(c):
                return dot(g_low, w[:, ff + c : ff + c + DENSE_CHUNK])

            for c, d_act in ahead_of(range(0, ff, DENSE_CHUNK), project):
                low = (d_act * stash[at, c : c + DENSE_CHUNK]).astype(BF16)
                rows[at, c : c + DENSE_CHUNK] = low
                d_normed = d_normed + dot(low, wt[c : c + DENSE_CHUNK, :])
            finish_back(m, x, q, d_normed)
            turn(1, grad, m)
            return carry

        lax.fori_loop(0, sections, backward, 0)

    @pl.when(is_last)
    def _():
        def prepare(k, carry):
            m = last - k
            grad_in(m).wait_recv()
            at = whole(m)
            g_low = grad[at]
            for c in range(0, ff, DENSE_CHUNK):
                stash[at, c : c + DENSE_CHUNK] = dot(g_low, w[:, ff + c : ff + c + DENSE_CHUNK])
            turn(1, grad, m)
            return carry

        lax.fori_loop(0, sections, prepare, 0)

        def both(m, carry):
            wait_res(m)
            at = whole(m)
            x, q, normed = norm_in(m)
            normal[at] = normed
            d_normed = jnp.zeros((slot, width), F32)

            def project(c):
                return dot(normed, w[:, c : c + LAST_CHUNK])

            for c, hidden_in in ahead_of(range(0, ff, LAST_CHUNK), project):
                hidden, bend = gelu_parts(hidden_in)
                rows[at, ff + c : ff + c + LAST_CHUNK] = hidden.astype(BF16)
                low = (stash[at, c : c + LAST_CHUNK] * bend).astype(BF16)
                rows[at, c : c + LAST_CHUNK] = low
                d_normed = d_normed + dot(low, wt[c : c + LAST_CHUNK, :])
            finish_back(m, x, q, d_normed)
            turn(0, normal, m)
            return carry

        lax.fori_loop(0, sections, both, 0)

    @pl.when(is_mixer)
    def _():
        small[1:2, 0:GATE_CHUNK] = jnp.sum(forget_acc[...], axis=0, keepdims=True)
        used = mask[0, 1:2]
        for m in range(1, sections):
            used = used + mask[m, 1:2]
        small[2:3, 0:slot] = used

    split = jnp.where(is_mixer, 3 * gate, ff)

    def rows_at(k):
        return pl.ds(pl.multiple_of(lax.rem(k, stacked) * piece_rows, piece_rows), piece_rows)

    def cols_at(k, part_of):
        return pl.ds(pl.multiple_of(part_of * half + k // stacked * piece, piece), piece)

    def grad_piece(k, part_of):
        side = jnp.where(part_of * half + k // stacked * piece < split, 0, 1)
        return dot(left[side, rows_at(k)], rows[:, cols_at(k, part_of)])

    def sib_copy(k):
        return remote(sib_out.at[k], sib_in.at[k], sib_send, sib_recv.at[k], sibling)

    sub_rows = piece_rows // SUB

    def sub(buffer, k, q):
        return buffer.at[k, q * sub_rows : (q + 1) * sub_rows]

    def sub_at(k, q):
        first = lax.rem(k, stacked) * piece_rows + q * sub_rows
        return pl.ds(pl.multiple_of(first, sub_rows), sub_rows)

    def inward(k, q):
        return remote(sub(part, k, q), sub(outer_in, k, q), part_send, outer_recv.at[k * SUB + q], inner)

    def across(k, q):
        return remote(sub(part, k, q), sub(tot_in, k, q), part_send, tot_recv.at[k * SUB + q], inner)

    def outward(k, q):
        return remote(sub(tot_in, k, q), sub(tot_in, k, q), tot_send, tot_recv.at[k * SUB + q], outer)

    def lent_piece(j):
        return STRIDE * j + STRIDE - 1

    def lend(k):
        return remote(part.at[lent_piece(k)], guest_in.at[k], part_send, guest_recv.at[k], (partner, d))

    def give_back(k, q):
        to = lent_piece(k - pieces)
        return remote(sub(tot_in, k, q), sub(tot_in, to, q), back_send, tot_recv.at[to * SUB + q], (partner, d))

    def final(k, q):
        return remote(sub(tot_in, k, q), dw_ref.at[sub_at(k, q), cols_at(k, mine)], fin_send, fin_recv, sibling)

    small_swap = remote(small, small_sib, small_send.at[0], small_recv.at[0], sibling)
    small_inward = remote(small_part, small_outer, small_send.at[1], small_recv.at[1], inner)
    small_across = remote(small_part, small_tot, small_send.at[1], small_recv.at[2], inner)
    small_outward = remote(small_tot, small_tot, small_send.at[2], small_recv.at[2], outer)

    def to_sibling(k):
        sib_out[k] = grad_piece(k, 1 - mine).astype(BF16)
        sib_copy(k).start()

    for k in range(AHEAD):
        to_sibling(k)
    small_swap.start()

    def reduce_small():
        small_swap.wait_recv()

        @pl.when(is_end)
        def _():
            small_part[...] = small[...] + small_sib[...]

        @pl.when(jnp.logical_not(is_end))
        def _():
            small_inward.wait_recv()
            small_part[...] = small[...] + small_sib[...] + small_outer[...]

        @pl.when(is_middle)
        def _():
            small_across.start()

        @pl.when(jnp.logical_not(is_middle))
        def _():
            small_inward.start()

    def far_copy(k):
        return remote(
            small_tot, small_far.at[s // 2], far_send.at[k - 1], far_recv.at[s // 2], (lax.rem(s + k, sections), other)
        )

    def total_small():
        small_across.wait_recv()

        @pl.when(is_middle)
        def _():
            small_tot[...] = small_tot[...] + small_part[...]

        @pl.when(jnp.logical_not(is_end))
        def _():
            small_outward.start()

        @pl.when(is_mixer)
        def _():
            small_far[s // 2] = small_tot[...]
            for k in range(1, sections):
                far_copy(k).start()

    def is_lent(k):
        return (k < STRIDE * lent) & (lax.rem(k, STRIDE) == STRIDE - 1)

    def reduce_piece(k):
        @pl.when(k < pieces)
        def _():
            work[...] = grad_piece(k, mine)
            sib_copy(k).wait_recv()
            work[...] += sib_in[k].astype(F32)

        @pl.when(k >= pieces)
        def _():
            lend(k - pieces).wait_recv()
            work[...] = guest_in[k - pieces].astype(F32)

        on_line = jnp.logical_not(is_lent(k))

        def pass_on(has_outer, send):
            if not has_outer:
                part[k] = work[...].astype(BF16)
            for q in range(SUB):
                if has_outer:
                    inward(k, q).wait_recv()
                    here = slice(q * sub_rows, (q + 1) * sub_rows)
                    part[k, here] = (work[here] + outer_in[k, here].astype(F32)).astype(BF16)
                send(k, q).start()

        @pl.when(is_lent(k))
        def _():
            part[k] = work[...].astype(BF16)
            lend(k // STRIDE).start()

        @pl.when(on_line & is_middle)
        def _():
            pass_on(chips > 2, across)

        if chips > 2:

            @pl.when(on_line & is_end)
            def _():
                pass_on(False, inward)

        if chips > 4:

            @pl.when(on_line & jnp.logical_not(is_end | is_middle))
            def _():
                pass_on(True, inward)

    def total_piece(k):
        on_line = jnp.logical_not(is_lent(k))
        for q in range(SUB):
            here = slice(q * sub_rows, (q + 1) * sub_rows)
            across(k, q).wait_recv()

            @pl.when(on_line & is_middle)
            def _():
                tot_in[k, here] = (tot_in[k, here].astype(F32) + part[k, here].astype(F32)).astype(BF16)

            @pl.when(on_line & jnp.logical_not(is_end))
            def _():
                outward(k, q).start()

            @pl.when(k < pieces)
            def _():
                final(k, q).start()

            @pl.when(k >= pieces)
            def _():
                give_back(k, q).start()

        @pl.when(k < pieces)
        def _():
            dw_ref[rows_at(k), cols_at(k, mine)] = tot_in[k]

    on_list = pieces + hosted
    on_line = on_list - lent
    late = on_line - LAG

    def listed(i):
        return jnp.where(
            i < HOST_AT, i, jnp.where(i < HOST_AT + hosted, i - HOST_AT + pieces, i - hosted)
        )

    def line_place(i):
        return jnp.where(i < STRIDE * lent, i // STRIDE * (STRIDE - 1) + lax.rem(i, STRIDE), i - lent)

    def of_line(r):
        few = STRIDE - 1
        return listed(jnp.where(r < few * lent, r // few * STRIDE + lax.rem(r, few), r + lent))

    def in_order(p):
        return jnp.where(
            p < late, of_line(p), jnp.where(p < late + lent, lent_piece(p - late), of_line(p - lent))
        )

    def step(i, carry):
        own = jnp.where(i < HOST_AT, i, i - hosted)
        working = i < on_list

        @pl.when((own + AHEAD < pieces) & ((i < HOST_AT) | (i >= HOST_AT + hosted)))
        def _():
            to_sibling(own + AHEAD)

        @pl.when(working)
        def _():
            reduce_piece(listed(i))

        @pl.when(i == SMALL_STEP)
        def _():
            reduce_small()

        @pl.when(i == jnp.where(is_middle, 3 * SMALL_STEP, on_list + SMALL_STEP))
        def _():
            total_small()

        place = line_place(i)
        taken = is_middle & working & jnp.logical_not(is_lent(i)) & (place >= LAG)
        at = jnp.where(working, place - LAG, jnp.where(is_middle, late, 0) + i - on_list)

        @pl.when(taken | jnp.logical_not(working))
        def _():
            total_piece(in_order(at))

        return carry

    lax.fori_loop(0, on_list + jnp.where(is_middle, LAG + lent, on_list), step, 0)

    for k in range(sections // 2):

        @pl.when(s != 2 * k)
        def _():
            remote(small_tot, small_far.at[k], far_send.at[0], far_recv.at[k], sibling).wait_recv()

    dgain_ref[...] = small_tot[0:1, :]
    lanes = lax.broadcasted_iota(jnp.int32, (1, LANES), 1)
    means = jnp.zeros((1, LANES), F32)
    for k in range(sections // 2):
        sums = jnp.sum(small_far[k], axis=1, keepdims=True)
        means = jnp.where(lanes == k, sums[1:2] / (sums[2:3] * gate), means)
    fmean_ref[...] = means

    @pl.when(s != 0)
    def _():
        home(0, s).wait_recv()
        grad_in(0).wait_send()

    for m in range(1, sections):
        grad_in(m).wait_send()

    @pl.when(s == 2)
    def _():
        dy_onward.wait_send()

    dy_copy.wait_send()

    @pl.when(w_early & (s != 0))
    def _():
        x_copy.wait_send()

    for k in range(sections // 2):

        @pl.when(s != 2 * k)
        def _():
            mask_copies[k].wait_send()

    for m in range(sections):

        @pl.when(s != last)
        def _():
            res_in(m).wait_send()

    small_swap.wait_send()
    small_across.wait_send()

    @pl.when(jnp.logical_not(is_end))
    def _():
        small_outward.wait_send()

    @pl.when(is_mixer)
    def _():
        for k in range(1, sections):
            far_copy(k).wait_send()

    remote(sib_out, sib_in, sib_send, sib_recv.at[0], sibling).wait_send()

    def sent(source, sem, n):
        remote(source.at[pl.ds(0, n)], source.at[pl.ds(0, n)], sem, sib_recv.at[0], sibling).wait_send()

    for q in range(sections):
        given = LENT[q] if q < len(LENT) else 0
        taken = LENT[last - q] if last - q < len(LENT) else 0

        @pl.when((s == q) & jnp.logical_not(is_end))
        def _():
            sent(tot_in, tot_send, pieces - given + taken)

        @pl.when(s == q)
        def _():
            sent(part, part_send, pieces + taken)
            if taken:
                sent(guest_in, back_send, taken)

    sent(tot_in, fin_send, pieces)
    their_half = dw_ref.at[:, pl.ds(pl.multiple_of((1 - mine) * half, half), half)]
    remote(their_half, their_half, fin_send, fin_recv, sibling).wait_recv()


def finish_kernel(
    dw_ref, ig_ref, dgain_ref, fmean_ref, ig_out, dw_out, dgain_out, fmean_out, wide_dw, ig, dgain, fmean, sem, small_sem
):
    slots, step = wide_dw.shape[:2]
    steps = dw_ref.shape[0] // step

    def copy(k):
        return pltpu.make_async_copy(
            wide_dw.at[k % slots], dw_out.at[pl.ds(k * step, step)], sem.at[k % slots]
        )

    def convert(k):
        wide_dw[k % slots] = dw_ref[k * step : (k + 1) * step].astype(F32)
        copy(k).start()

    for k in range(slots):
        convert(k)
    slot = ig_ref.shape[1]
    token_rows = lax.broadcasted_iota(jnp.int32, (slot, slot), 0)
    order = jnp.where(time_of_row(slot, (slot, slot), 1) == token_rows, 1.0, 0.0).astype(BF16)
    ig[0] = dot(order, ig_ref[0]).astype(BF16)
    dgain[...] = dgain_ref[0]
    fmean[...] = fmean_ref[0, : fmean.shape[0]]
    small = [
        pltpu.make_async_copy(src, dst, small_sem.at[k])
        for k, (src, dst) in enumerate(((ig, ig_out), (dgain, dgain_out), (fmean, fmean_out)))
    ]
    for one in small:
        one.start()
    for k in range(slots, steps):
        copy(k - slots).wait()
        convert(k)
    for one in small:
        one.wait()
    for k in range(steps - slots, steps):
        copy(k).wait()


def finish(input_grad, weight_grads, gain_grads, means, sections):
    width, pack = weight_grads.shape
    vmem = pl.BlockSpec(memory_space=pltpu.VMEM)
    anywhere = pl.BlockSpec(memory_space=pl.ANY)
    slots = 8
    return pl.pallas_call(
        finish_kernel,
        out_shape=(
            jax.ShapeDtypeStruct(input_grad.shape, BF16),
            jax.ShapeDtypeStruct(weight_grads.shape, F32),
            jax.ShapeDtypeStruct((width,), F32),
            jax.ShapeDtypeStruct((sections // 2,), F32),
        ),
        in_specs=[vmem] * 4,
        out_specs=(anywhere,) * 4,
        scratch_shapes=[
            pltpu.VMEM((slots, FINISH_ROWS, pack), F32),
            pltpu.VMEM(input_grad.shape, BF16),
            pltpu.VMEM((width,), F32),
            pltpu.VMEM((sections // 2,), F32),
            pltpu.SemaphoreType.DMA((slots,)),
            pltpu.SemaphoreType.DMA((3,)),
        ],
        compiler_params=pltpu.CompilerParams(vmem_limit_bytes=16 * 1024 * 1024),
    )(weight_grads, input_grad, gain_grads, means)


def local(count, inputs, cotangent, section_weights, norm_gains, doc_lengths, slot_fill):
    sections = lax.axis_size("section")
    slot, width = inputs.shape[1:]
    pack = section_weights.shape[1]
    gate, ff, half = pack // 4, pack // 2, pack // 2
    tokens = sections * slot
    pieces = half * width // (PIECE[0] * PIECE[1])
    dma = pltpu.SemaphoreType.DMA
    own = pltpu.VMEM((pieces, *PIECE), BF16)
    hosted = pltpu.VMEM((pieces + max(LENT), *PIECE), BF16)
    small = pltpu.VMEM((8, width), F32)
    stack = pltpu.VMEM((tokens, width), BF16)
    vmem = pl.BlockSpec(memory_space=pltpu.VMEM)
    anywhere = pl.BlockSpec(memory_space=pl.ANY)
    input_grad, weight_grads, gain_grads, means = pl.pallas_call(
        functools.partial(kernel, count),
        out_shape=(
            pltpu.VMEM((1, slot, width), BF16),
            pltpu.VMEM((width, pack), BF16),
            pltpu.VMEM((1, width), F32),
            pltpu.VMEM((1, LANES), F32),
        ),
        in_specs=[anywhere] * 6,
        out_specs=(vmem, vmem, vmem, vmem),
        scratch_shapes=[
            pltpu.VMEM((width, pack), BF16), pltpu.VMEM((pack, width), BF16),
            stack, stack, stack, stack, stack,
            pltpu.VMEM((slot, width), BF16), pltpu.VMEM((slot, width), BF16),
            pltpu.VMEM((sections, 8, slot), F32), pltpu.VMEM((8, slot), F32),
            pltpu.VMEM((slot, LANES), F32), pltpu.VMEM((slot, LANES), F32),
            pltpu.VMEM((slot, width), BF16),
            pltpu.VMEM(inputs.shape, BF16), pltpu.VMEM(inputs.shape, BF16), pltpu.VMEM((1, width), F32),
            pltpu.SMEM(doc_lengths.shape, jnp.int32), pltpu.SMEM(slot_fill.shape, jnp.int32),
            pltpu.VMEM((tokens, pack), F32),
            pltpu.VMEM((tokens, pack), BF16),
            pltpu.VMEM((2, width, tokens), BF16),
            pltpu.VMEM((8, GATE_CHUNK), F32),
            own, own, hosted, hosted, hosted,
            pltpu.VMEM((max(LENT), *PIECE), BF16), pltpu.VMEM(PIECE, F32),
            small, small, small, small, small,
            pltpu.VMEM((sections // 2, 8, width), F32),
            dma, dma((5,)), dma, dma,
            dma((sections // 2,)),
            dma((sections,)), dma((sections,)), dma((sections,)), dma((sections,)),
            dma((sections,)), dma, dma, dma, pltpu.SemaphoreType.REGULAR,
            dma, dma((pieces,)), dma, dma(((pieces + max(LENT)) * SUB,)),
            dma, dma(((pieces + max(LENT)) * SUB,)), dma, dma, dma((max(LENT),)), dma,
            dma((3,)), dma((3,)), dma((sections - 1,)), dma((sections // 2,)),
        ],
        compiler_params=pltpu.CompilerParams(
            collective_id=0, has_side_effects=True, vmem_limit_bytes=56 * 1024 * 1024
        ),
    )(inputs, cotangent, section_weights, norm_gains.reshape(1, width), doc_lengths, slot_fill)
    return finish(input_grad, weight_grads, gain_grads, means, sections)


def solution(mesh):
    placed = (
        P("section", "dp", None),
        P("section", "dp", None),
        P("section", None),
        P("section"),
        P("section", "dp", None),
        P("section", "dp"),
    )
    return jax.shard_map(
        functools.partial(local, mesh.shape["dp"]),
        mesh=mesh,
        in_specs=placed,
        out_specs=(P("section", "dp", None), P("section", None), P("section"), P()),
        check_vma=False,
    )
```

```python
import functools

import jax
import jax.numpy as jnp
from jax import lax
from jax.experimental import pallas as pl
from jax.experimental.pallas import tpu as pltpu
from jax.sharding import PartitionSpec as P

EPS = 1e-06
MESH = pl.DeviceIdType.MESH
F32 = jnp.float32
BF16 = jnp.bfloat16
LANES = 128
GATE_CHUNK = 256
BACK_CHUNK = 512
DENSE_CHUNK = 512
LAST_CHUNK = 256
TURN = 256
PIECE = (256, 128)
LENT = (7, 2)
HOST_AT = 26
SUB = 2
RING_PER_CHIP = 3
SIB_RING = 6
LAG = 2
STRIDE = 3
SECOND_TURNS = 10
FIRST_TURNS = 4
SMALL_STEP = 3
FINISH_ROWS = 32


def dot(left, right):
    return jnp.dot(left, right, preferred_element_type=F32)


def time_of_row(slot, shape, axis):
    row = lax.broadcasted_iota(jnp.int32, shape, axis)
    return (row & 7) * (slot // 8) + (row >> 3)


def scan_down(decay, drive):
    blocks = range(8, decay.shape[0], 8)
    factor, value = [decay[:8]], [drive[:8]]
    for at in blocks:
        here = decay[at : at + 8]
        value.append(drive[at : at + 8] + here * value[-1])
        factor.append(here * factor[-1])
    joined, through = value[-1], factor[-1]
    for by in (1, 2, 4):
        joined = joined + through * pltpu.roll(joined, by, 0)
        through = through * pltpu.roll(through, by, 0)
    before = pltpu.roll(joined, 1, 0)
    state = [v + f * before for v, f in zip(value, factor)]
    return jnp.concatenate(state, 0), jnp.concatenate([before] + state[:-1], 0)


def scan_up(decay, source):
    rows = decay.shape[0]
    ahead = [decay[at : at + 8] for at in range(8, rows, 8)] + [pltpu.roll(decay[:8], 7, 0)]
    factor, value = [ahead[-1]], [source[rows - 8 :]]
    for k in range(rows // 8 - 2, -1, -1):
        value.append(source[8 * k : 8 * k + 8] + ahead[k] * value[-1])
        factor.append(ahead[k] * factor[-1])
    joined, through = value[-1], factor[-1]
    for by in (1, 2, 4):
        joined = joined + through * pltpu.roll(joined, 8 - by, 0)
        through = through * pltpu.roll(through, 8 - by, 0)
    after = pltpu.roll(joined, 7, 0)
    return jnp.concatenate([v + f * after for v, f in zip(value[::-1], factor[::-1])], 0)


def ahead_of(starts, compute):
    coming = compute(starts[0])
    for k, start in enumerate(starts):
        now = coming
        if k + 1 < len(starts):
            coming = compute(starts[k + 1])
        yield start, now


def wide(column, width):
    return jnp.concatenate([column] * (width // LANES), 1)


def unit(x):
    return lax.rsqrt(jnp.mean(x * x, axis=-1, keepdims=True) + EPS)


def norm_back(x, q, gain, d_normed, grad_out):
    x_hat = x * q
    scaled = d_normed * gain
    mean = jnp.mean(scaled * x_hat, axis=-1, keepdims=True)
    d_gain = jnp.sum(d_normed * x_hat, axis=0, keepdims=True)
    return grad_out + q * (scaled - x_hat * mean), d_gain


def gelu_parts(u):
    cdf = 0.5 * lax.erf(u * 0.7071067811865476) + 0.5
    slope = cdf + u * (0.3989422804014327 * jnp.exp(-0.5 * u * u))
    return u * cdf, slope


def kernel(
    count,
    x_hbm, cot_hbm, w_hbm, gain_hbm, len_hbm, fill_hbm,
    ig_ref, dw_ref, dgain_ref, fmean_ref,
    w, wt, res, grad, out, gout, normal, x_own, dy_own, mask, mask_own, keep_col, valid_col, relay, x_ref, cot_ref, gain_ref, len_ref, fill_ref,
    stash, rows, left, forget_acc,
    sib_out, sib_in, outer_in, part, tot_in, guest_in, work,
    small, small_sib, small_outer, small_part, small_tot, small_far,
    w_sem, load_sem, x_send, dy_send, mask_send, res_send, res_recv, grad_send, grad_recv, mask_recv, ig_recv, relay_send, relay_recv, turn_sem,
    sib_send, sib_recv, part_send, outer_recv, tot_send, tot_recv, fin_send, fin_recv, guest_recv, back_send, back_recv,
    small_send, small_recv, far_send, far_recv,
):
    s = lax.axis_index("section")
    d = lax.axis_index("dp")
    core = lax.rem(d, 2)
    chip = d // 2
    chips = count // 2
    sections, slot = mask.shape[0], mask.shape[2]
    tokens, width = res.shape
    pack = w.shape[1]
    gate = pack // 4
    ff = pack // 2
    half = pack // 2
    pieces = sib_in.shape[0]
    piece_rows, piece = sib_in.shape[1:]
    ring = outer_recv.shape[0] // SUB
    stacked = width // piece_rows
    last = sections - 1
    partner = last - s
    lent = jnp.where(s == 0, LENT[0], jnp.where(s == 1, LENT[1], 0))
    hosted = jnp.where(partner == 0, LENT[0], jnp.where(partner == 1, LENT[1], 0))
    mine = lax.rem(core + chip, 2)
    is_first = s == 0
    is_last = s == last
    is_mixer = lax.rem(s, 2) == 0
    on_left = chip < chips // 2
    is_middle = (chip == chips // 2 - 1) | (chip == chips // 2)
    is_end = (chip == 0) | (chip == chips - 1)
    other = d + 1 - 2 * core
    sibling = (s, other)
    inner = (s, jnp.where(on_left, other + 2, other - 2))
    outer = (s, jnp.where(on_left, other - 2, other + 2))

    loads = [
        pltpu.make_async_copy(src, dst, load_sem.at[k])
        for k, (src, dst) in enumerate(
            ((x_hbm, x_ref), (len_hbm, len_ref), (fill_hbm, fill_ref), (cot_hbm, cot_ref), (gain_hbm, gain_ref))
        )
    ]
    w_copy = pltpu.make_async_copy(w_hbm, w, w_sem)
    for load in loads:
        load.start()
    w_early = is_first | is_last | (core == 1)

    @pl.when(w_early)
    def _():
        w_copy.start()

    barrier = pltpu.get_barrier_semaphore()
    for by in range(1, sections):
        for lane_of in (d, other):
            pl.semaphore_signal(
                barrier, inc=1, device_id=(lax.rem(s + by, sections), lane_of), device_id_type=MESH
            )
    pl.semaphore_signal(barrier, inc=1, device_id=sibling, device_id_type=MESH)

    @pl.when(chip > 0)
    def _():
        pl.semaphore_signal(barrier, inc=1, device_id=(s, other - 2), device_id_type=MESH)

    @pl.when(chip < chips - 1)
    def _():
        pl.semaphore_signal(barrier, inc=1, device_id=(s, other + 2), device_id_type=MESH)

    def remote(src, dst, send, recv, target):
        return pltpu.make_async_remote_copy(
            src_ref=src, dst_ref=dst, send_sem=send, recv_sem=recv, device_id=target, device_id_type=MESH
        )

    order = jnp.where(
        lax.broadcasted_iota(jnp.int32, (slot, slot), 1) == time_of_row(slot, (slot, slot), 0), 1.0, 0.0
    )
    order_low = order.astype(BF16)
    for load in loads:
        load.wait()
    x_own[...] = dot(order_low, x_ref[0]).astype(BF16)
    lane = lax.broadcasted_iota(jnp.int32, (8, slot), 1)
    row = lax.broadcasted_iota(jnp.int32, (8, slot), 0)
    starts = lane == 0
    position = len_ref[0, 0, 0]
    for k in range(1, len_ref.shape[2]):
        starts = starts | (lane == position)
        position = position + len_ref[0, 0, k]
    keep_rows = jnp.where(starts, 0.0, 1.0)
    valid_rows = jnp.where(lane < fill_ref[0, 0], 1.0, 0.0)
    mask_own[...] = jnp.where(row == 0, keep_rows, valid_rows)
    used_rows = jnp.where(time_of_row(slot, (slot, LANES), 0) < fill_ref[0, 0], 1.0, 0.0)
    dy_own[...] = (dot(order_low, cot_ref[0]) * wide(used_rows, width)).astype(BF16)
    forget_acc[...] = jnp.zeros_like(forget_acc)
    small[...] = jnp.zeros_like(small)

    def whole(m):
        return pl.ds(pl.multiple_of(m * slot, slot), slot)

    def res_in(m):
        return remote(
            out.at[whole(m)], res.at[whole(m)], res_send.at[m], res_recv.at[m], (jnp.minimum(s + 1, last), other)
        )

    def grad_in(m):
        return remote(
            gout.at[whole(m)], grad.at[whole(m)], grad_send.at[m], grad_recv.at[m], (jnp.maximum(s - 1, 0), other)
        )

    def home(m, to):
        return remote(gout.at[whole(m)], ig_ref.at[0], grad_send.at[m], ig_recv, (to, d))

    def wait_res(m):
        @pl.when((s != 0) | (m != 0))
        def _():
            res_in(m).wait_recv()

    def send_grad(m):
        @pl.when(s != 0)
        def _():
            grad_in(m).start()

        @pl.when((s == 0) & (m == 0))
        def _():
            ig_ref[0] = gout[whole(m)]

        @pl.when((s == 0) & (m != 0))
        def _():
            home(m, m).start()

    def turn(side, source, m):
        at = whole(m)
        left[side, :, at] = source[at].T

    def turn_weights(start, stop):
        def one(k, carry):
            at = pl.ds(pl.multiple_of(k * TURN, TURN), TURN)
            wt[at, :] = w[:, at].T
            return carry

        lax.fori_loop(start, stop, one, 0)

    def norm_in(m):
        x = res[whole(m)].astype(F32)
        q = unit(x)
        return x, q, (x * q * gain).astype(BF16)

    def finish_back(m, x, q, d_normed):
        d_res, d_gain = norm_back(x, q, gain, d_normed, grad[whole(m)].astype(F32))
        gout[whole(m)] = d_res.astype(BF16)
        send_grad(m)
        small[0:1, :] += d_gain

    gain = gain_ref[...]

    def mixer_forward(m, halfway=None):
        at = whole(m)
        masks = mask[m]
        keep_col[...] = jnp.broadcast_to(jnp.sum(order * masks[0:1], axis=1, keepdims=True), (slot, LANES))
        valid_col[...] = jnp.broadcast_to(jnp.sum(order * masks[1:2], axis=1, keepdims=True), (slot, LANES))
        wait_res(m)
        keep = wide(keep_col[...], GATE_CHUNK)
        valid = wide(valid_col[...], GATE_CHUNK)
        x, _, normed = norm_in(m)
        normal[at] = normed
        total = x

        def project(c):
            return [dot(normed, w[:, k * gate + c : k * gate + c + GATE_CHUNK]) for k in range(3)]

        for c, (f_in, i_in, c_in) in ahead_of(range(0, gate, GATE_CHUNK), project):
            top = jnp.maximum(jnp.maximum(-f_in, -i_in), 0.0)
            e_zero = jnp.exp(-top)
            e_f = jnp.exp(-f_in - top)
            e_i = jnp.exp(-i_in - top)
            u_f = e_zero + e_f
            u_i = e_zero + e_i
            inv = 1.0 / (u_f + u_i)
            forget = u_i * inv
            intake = u_f * inv
            e_c = jnp.exp(-jnp.abs(c_in))
            soft = jnp.maximum(c_in, 0.0) + jnp.log1p(e_c)
            decay = forget * keep
            state, previous = scan_down(decay, intake * soft)
            state_low = state.astype(BF16)
            total = total + dot(state_low, wt[3 * gate + c : 3 * gate + c + GATE_CHUNK, :])
            rows[at, 3 * gate + c : 3 * gate + c + GATE_CHUNK] = state_low
            bend = soft - keep * previous
            if halfway is not None and c == gate // 4:
                halfway()
            stash[at, c : c + GATE_CHUNK] = -forget * (e_f * inv) * bend
            stash[at, gate + c : gate + c + GATE_CHUNK] = intake * (e_i * inv) * bend
            stash[at, 2 * gate + c : 2 * gate + c + GATE_CHUNK] = (
                intake * jnp.where(c_in >= 0.0, 1.0, e_c) / (1.0 + e_c)
            )
            stash[at, 3 * gate + c : 3 * gate + c + GATE_CHUNK] = decay
            counted = forget * valid
            folded = counted[:8]
            for k in range(8, slot, 8):
                folded = folded + counted[k : k + 8]
            forget_acc[...] += folded
        out[at] = total.astype(BF16)

    inner_turns = 3 * gate // TURN

    @pl.when(is_first)
    def _():
        res[0:slot] = x_own[...]
        mask[0] = mask_own[...]
        w_copy.wait()
        turn_weights(inner_turns, pack // TURN)
        mixer_forward(0)

    pl.semaphore_wait(
        barrier, 2 * sections - 1 + jnp.where(chip > 0, 1, 0) + jnp.where(chip < chips - 1, 1, 0)
    )

    x_copy = remote(x_own, res.at[whole(s)], x_send, res_recv.at[s], (0, d))
    dy_copy = remote(
        dy_own, grad.at[whole(s)], dy_send, grad_recv.at[s], (last, jnp.where(last % 2 == 1, other, d))
    )
    dy_relayed = remote(dy_own, relay, dy_send, relay_recv, (2, d))
    dy_onward = remote(relay, grad.at[whole(0)], relay_send, grad_recv.at[0], (last, other))
    mask_copies = [
        remote(mask_own, mask.at[s], mask_send.at[k], mask_recv.at[s], (2 * k, d))
        for k in range(sections // 2)
    ]

    for k in range(sections // 2):

        @pl.when((s == 2 * k) & (s != 0))
        def _():
            mask[s] = mask_own[...]

        @pl.when(s != 2 * k)
        def _():
            mask_copies[k].start()

    @pl.when(jnp.logical_not(w_early))
    def _():
        x_copy.start()
        x_copy.wait_send()
        w_copy.start()

    @pl.when(s != 0)
    def _():
        w_copy.wait()
        turn_weights(0, SECOND_TURNS)

        @pl.when((s != last) & (core == 1))
        def _():
            x_copy.start()

        turn_weights(SECOND_TURNS, pack // TURN)

        @pl.when(is_last & (core == 0))
        def _():
            x_copy.start()

    @pl.when(is_first)
    def _():
        @pl.when(core == 0)
        def _():
            res_in(0).start()

        dy_relayed.start()
        turn_weights(0, FIRST_TURNS)

        @pl.when(core == 1)
        def _():
            res_in(0).start()

        turn(0, normal, 0)

    def give_turn():
        pl.semaphore_signal(turn_sem, inc=1, device_id=sibling, device_id_type=MESH)

    def take_turn():
        pl.semaphore_wait(turn_sem, 1)

    @pl.when(s != 0)
    def _():
        dy_copy.start()

    @pl.when(is_mixer)
    def _():
        @pl.when(s == 2)
        def _():
            dy_relayed.wait_recv()
            dy_onward.start()

        def forward(m, carry):
            @pl.when(m != s)
            def _():
                remote(mask_own, mask.at[m], mask_send.at[0], mask_recv.at[m], (0, d)).wait_recv()

            mixer_forward(m)

            @pl.when(is_first & (core == 1))
            def _():
                take_turn()

            res_in(m).start()
            turn(0, normal, m)
            return carry

        lax.fori_loop(jnp.where(is_first, 1, 0), jnp.where(is_first, 2, sections), forward, 0)

        @pl.when(is_first)
        def _():
            def by_turns(m, carry):
                remote(mask_own, mask.at[m], mask_send.at[0], mask_recv.at[m], (0, d)).wait_recv()
                mixer_forward(m, give_turn)
                take_turn()
                res_in(m).start()
                turn(0, normal, m)
                return carry

            lax.fori_loop(2, sections, by_turns, 0)
            turn_weights(FIRST_TURNS, inner_turns)

            @pl.when(core == 0)
            def _():
                give_turn()

        def backward(m, carry):
            at = whole(m)
            x, q, _ = norm_in(m)
            grad_in(m).wait_recv()
            g_low = grad[at]
            d_normed = jnp.zeros((slot, width), F32)

            def project(c):
                return dot(g_low, w[:, 3 * gate + c : 3 * gate + c + BACK_CHUNK])

            for c, d_state in ahead_of(range(0, gate, BACK_CHUNK), project):
                adjoint = scan_up(stash[at, 3 * gate + c : 3 * gate + c + BACK_CHUNK], d_state)
                for k in range(3):
                    here = slice(k * gate + c, k * gate + c + BACK_CHUNK)
                    low = (adjoint * stash[at, here]).astype(BF16)
                    rows[at, here] = low
                    d_normed = d_normed + dot(low, wt[here, :])
            finish_back(m, x, q, d_normed)
            turn(1, grad, m)
            return carry

        lax.fori_loop(0, sections, backward, 0)

    @pl.when((lax.rem(s, 2) == 1) & (s != last))
    def _():
        def forward(m, carry):
            wait_res(m)
            at = whole(m)
            x, _, normed = norm_in(m)
            normal[at] = normed
            total = x

            def project(c):
                return dot(normed, w[:, c : c + DENSE_CHUNK])

            for c, hidden_in in ahead_of(range(0, ff, DENSE_CHUNK), project):
                hidden, bend = gelu_parts(hidden_in)
                low = hidden.astype(BF16)
                total = total + dot(low, wt[ff + c : ff + c + DENSE_CHUNK, :])
                rows[at, ff + c : ff + c + DENSE_CHUNK] = low
                stash[at, c : c + DENSE_CHUNK] = bend
            out[at] = total.astype(BF16)

            res_in(m).start()
            turn(0, normal, m)
            return carry

        lax.fori_loop(0, sections, forward, 0)

        def backward(m, carry):
            at = whole(m)
            x, q, _ = norm_in(m)
            grad_in(m).wait_recv()
            g_low = grad[at]
            d_normed = jnp.zeros((slot, width), F32)

            def project(c):
                return dot(g_low, w[:, ff + c : ff + c + DENSE_CHUNK])

            for c, d_act in ahead_of(range(0, ff, DENSE_CHUNK), project):
                low = (d_act * stash[at, c : c + DENSE_CHUNK]).astype(BF16)
                rows[at, c : c + DENSE_CHUNK] = low
                d_normed = d_normed + dot(low, wt[c : c + DENSE_CHUNK, :])
            finish_back(m, x, q, d_normed)
            turn(1, grad, m)
            return carry

        lax.fori_loop(0, sections, backward, 0)

    @pl.when(is_last)
    def _():
        def prepare(k, carry):
            m = last - k
            grad_in(m).wait_recv()
            at = whole(m)
            g_low = grad[at]
            for c in range(0, ff, DENSE_CHUNK):
                stash[at, c : c + DENSE_CHUNK] = dot(g_low, w[:, ff + c : ff + c + DENSE_CHUNK])
            turn(1, grad, m)

            @pl.when((k == 0) & (core == 1))
            def _():
                x_copy.start()

            return carry

        lax.fori_loop(0, sections, prepare, 0)

        def both(m, carry):
            wait_res(m)
            at = whole(m)
            x, q, normed = norm_in(m)
            normal[at] = normed
            d_normed = jnp.zeros((slot, width), F32)

            def project(c):
                return dot(normed, w[:, c : c + LAST_CHUNK])

            for c, hidden_in in ahead_of(range(0, ff, LAST_CHUNK), project):
                hidden, bend = gelu_parts(hidden_in)
                rows[at, ff + c : ff + c + LAST_CHUNK] = hidden.astype(BF16)
                low = (stash[at, c : c + LAST_CHUNK] * bend).astype(BF16)
                rows[at, c : c + LAST_CHUNK] = low
                d_normed = d_normed + dot(low, wt[c : c + LAST_CHUNK, :])
            finish_back(m, x, q, d_normed)
            turn(0, normal, m)
            return carry

        lax.fori_loop(0, sections, both, 0)

    @pl.when(is_mixer)
    def _():
        small[1:2, 0:GATE_CHUNK] = jnp.sum(forget_acc[...], axis=0, keepdims=True)
        used = mask[0, 1:2]
        for m in range(1, sections):
            used = used + mask[m, 1:2]
        small[2:3, 0:slot] = used

    split = jnp.where(is_mixer, 3 * gate, ff)

    def rows_at(k):
        return pl.ds(pl.multiple_of(lax.rem(k, stacked) * piece_rows, piece_rows), piece_rows)

    def cols_at(k, part_of):
        return pl.ds(pl.multiple_of(part_of * half + k // stacked * piece, piece), piece)

    def grad_piece(k, part_of):
        side = jnp.where(part_of * half + k // stacked * piece < split, 0, 1)
        return dot(left[side, rows_at(k)], rows[:, cols_at(k, part_of)])

    def sib_copy(k):
        return remote(sib_out.at[k], sib_in.at[k], sib_send, sib_recv.at[lax.rem(k, sib_recv.shape[0])], sibling)

    sub_rows = piece_rows // SUB

    def sub(buffer, k, q):
        return buffer.at[k, q * sub_rows : (q + 1) * sub_rows]

    def sub_at(k, q):
        first = lax.rem(k, stacked) * piece_rows + q * sub_rows
        return pl.ds(pl.multiple_of(first, sub_rows), sub_rows)

    def sem_at(r, q):
        return lax.rem(r, ring) * SUB + q

    def inward(k, r, q):
        return remote(sub(part, k, q), sub(outer_in, k, q), part_send, outer_recv.at[sem_at(r, q)], inner)

    def across(k, r, q):
        return remote(sub(part, k, q), sub(tot_in, k, q), part_send, tot_recv.at[sem_at(r, q)], inner)

    def outward(k, r, q):
        return remote(sub(tot_in, k, q), sub(tot_in, k, q), tot_send, tot_recv.at[sem_at(r, q)], outer)

    def lent_piece(j):
        return STRIDE * j + STRIDE - 1

    def lend(k):
        return remote(part.at[lent_piece(k)], guest_in.at[k], part_send, guest_recv.at[k], (partner, d))

    def give_back(j):
        return remote(tot_in.at[pieces + j], tot_in.at[lent_piece(j)], back_send, back_recv.at[j], (partner, d))

    def final(k, q):
        return remote(sub(tot_in, k, q), dw_ref.at[sub_at(k, q), cols_at(k, mine)], fin_send, fin_recv, sibling)

    small_swap = remote(small, small_sib, small_send.at[0], small_recv.at[0], sibling)
    small_inward = remote(small_part, small_outer, small_send.at[1], small_recv.at[1], inner)
    small_across = remote(small_part, small_tot, small_send.at[1], small_recv.at[2], inner)
    small_outward = remote(small_tot, small_tot, small_send.at[2], small_recv.at[2], outer)

    def to_sibling(k):
        sib_out[k] = grad_piece(k, 1 - mine).astype(BF16)
        sib_copy(k).start()

    to_sibling(0)
    small_swap.start()

    def reduce_small():
        small_swap.wait_recv()

        @pl.when(is_end)
        def _():
            small_part[...] = small[...] + small_sib[...]

        @pl.when(jnp.logical_not(is_end))
        def _():
            small_inward.wait_recv()
            small_part[...] = small[...] + small_sib[...] + small_outer[...]

        @pl.when(is_middle)
        def _():
            small_across.start()

        @pl.when(jnp.logical_not(is_middle))
        def _():
            small_inward.start()

    def far_copy(k):
        return remote(
            small_tot, small_far.at[s // 2], far_send.at[k - 1], far_recv.at[s // 2], (lax.rem(s + k, sections), other)
        )

    def total_small():
        small_across.wait_recv()

        @pl.when(is_middle)
        def _():
            small_tot[...] = small_tot[...] + small_part[...]

        @pl.when(jnp.logical_not(is_end))
        def _():
            small_outward.start()

        @pl.when(is_mixer)
        def _():
            small_far[s // 2] = small_tot[...]
            for k in range(1, sections):
                far_copy(k).start()

    def is_lent(k):
        return (k < STRIDE * lent) & (lax.rem(k, STRIDE) == STRIDE - 1)

    def reduce_piece(k, r):
        @pl.when(k < pieces)
        def _():
            work[...] = grad_piece(k, mine)
            sib_copy(k).wait_recv()
            work[...] += sib_in[k].astype(F32)

        @pl.when(k >= pieces)
        def _():
            lend(k - pieces).wait_recv()
            work[...] = guest_in[k - pieces].astype(F32)

        on_line = jnp.logical_not(is_lent(k))

        def pass_on(has_outer, send):
            if not has_outer:
                part[k] = work[...].astype(BF16)
            for q in range(SUB):
                if has_outer:
                    inward(k, r, q).wait_recv()
                    here = slice(q * sub_rows, (q + 1) * sub_rows)
                    part[k, here] = (work[here] + outer_in[k, here].astype(F32)).astype(BF16)
                send(k, r, q).start()

        @pl.when(is_lent(k))
        def _():
            part[k] = work[...].astype(BF16)
            lend(k // STRIDE).start()

        @pl.when(on_line & is_middle)
        def _():
            pass_on(chips > 2, across)

        if chips > 2:

            @pl.when(on_line & is_end)
            def _():
                pass_on(False, inward)

        if chips > 4:

            @pl.when(on_line & jnp.logical_not(is_end | is_middle))
            def _():
                pass_on(True, inward)

    def total_piece(k, r):
        @pl.when(is_lent(k))
        def _():
            give_back(k // STRIDE).wait_recv()
            for q in range(SUB):
                final(k, q).start()

        @pl.when(jnp.logical_not(is_lent(k)))
        def _():
            for q in range(SUB):
                here = slice(q * sub_rows, (q + 1) * sub_rows)
                across(k, r, q).wait_recv()

                @pl.when(is_middle)
                def _():
                    tot_in[k, here] = (tot_in[k, here].astype(F32) + part[k, here].astype(F32)).astype(BF16)

                @pl.when(jnp.logical_not(is_end))
                def _():
                    outward(k, r, q).start()

                @pl.when(k < pieces)
                def _():
                    final(k, q).start()

        @pl.when(k < pieces)
        def _():
            dw_ref[rows_at(k), cols_at(k, mine)] = tot_in[k]

        @pl.when(k >= pieces)
        def _():
            give_back(k - pieces).start()

    on_list = pieces + hosted
    on_line = on_list - lent
    late = on_line - LAG

    def listed(i):
        return jnp.where(
            i < HOST_AT, i, jnp.where(i < HOST_AT + hosted, i - HOST_AT + pieces, i - hosted)
        )

    def line_place(i):
        return jnp.where(i < STRIDE * lent, i // STRIDE * (STRIDE - 1) + lax.rem(i, STRIDE), i - lent)

    def of_line(r):
        few = STRIDE - 1
        return listed(jnp.where(r < few * lent, r // few * STRIDE + lax.rem(r, few), r + lent))

    def in_order(p):
        r = jnp.where(p < late, p, p - lent)
        return jnp.where((p >= late) & (p < late + lent), lent_piece(p - late), of_line(r)), r

    lag = jnp.where(is_middle, LAG, jnp.minimum(ring - 2, on_line))

    def step(i, carry):
        own = jnp.where(i < HOST_AT, i, i - hosted)
        working = i < on_list
        place = line_place(i)

        @pl.when((own + 1 < pieces) & ((i < HOST_AT) | (i >= HOST_AT + hosted)))
        def _():
            to_sibling(own + 1)

        @pl.when(working)
        def _():
            reduce_piece(listed(i), place)

        @pl.when(i == SMALL_STEP)
        def _():
            reduce_small()

        @pl.when(i == jnp.where(is_middle, 3 * SMALL_STEP, on_list + SMALL_STEP))
        def _():
            total_small()

        taken = working & jnp.logical_not(is_lent(i)) & (place >= lag)
        at = jnp.where(working, place - lag, on_line - lag + i - on_list)

        @pl.when(taken | jnp.logical_not(working))
        def _():
            total_piece(*in_order(at))

        return carry

    lax.fori_loop(0, on_list + lag + lent, step, 0)

    for k in range(sections // 2):

        @pl.when(s != 2 * k)
        def _():
            remote(small_tot, small_far.at[k], far_send.at[0], far_recv.at[k], sibling).wait_recv()

    dgain_ref[...] = small_tot[0:1, :]
    lanes = lax.broadcasted_iota(jnp.int32, (1, LANES), 1)
    means = jnp.zeros((1, LANES), F32)
    for k in range(sections // 2):
        sums = jnp.sum(small_far[k], axis=1, keepdims=True)
        means = jnp.where(lanes == k, sums[1:2] / (sums[2:3] * gate), means)
    fmean_ref[...] = means

    @pl.when(s != 0)
    def _():
        home(0, s).wait_recv()
        grad_in(0).wait_send()

    for m in range(1, sections):
        grad_in(m).wait_send()

    @pl.when(s == 2)
    def _():
        dy_onward.wait_send()

    dy_copy.wait_send()

    @pl.when(w_early & (s != 0))
    def _():
        x_copy.wait_send()

    for k in range(sections // 2):

        @pl.when(s != 2 * k)
        def _():
            mask_copies[k].wait_send()

    for m in range(sections):

        @pl.when(s != last)
        def _():
            res_in(m).wait_send()

    small_swap.wait_send()
    small_across.wait_send()

    @pl.when(jnp.logical_not(is_end))
    def _():
        small_outward.wait_send()

    @pl.when(is_mixer)
    def _():
        for k in range(1, sections):
            far_copy(k).wait_send()

    remote(sib_out, sib_in, sib_send, sib_recv.at[0], sibling).wait_send()

    def sent(source, sem, n):
        remote(source.at[pl.ds(0, n)], source.at[pl.ds(0, n)], sem, sib_recv.at[0], sibling).wait_send()

    for q in range(sections):
        given = LENT[q] if q < len(LENT) else 0
        taken = LENT[last - q] if last - q < len(LENT) else 0

        @pl.when((s == q) & jnp.logical_not(is_end))
        def _():
            sent(tot_in, tot_send, pieces - given + taken)

        @pl.when(s == q)
        def _():
            sent(part, part_send, pieces + taken)
            if taken:
                sent(guest_in, back_send, taken)

    sent(tot_in, fin_send, pieces)
    their_half = dw_ref.at[:, pl.ds(pl.multiple_of((1 - mine) * half, half), half)]
    remote(their_half, their_half, fin_send, fin_recv, sibling).wait_recv()


def finish_kernel(
    dw_ref, ig_ref, dgain_ref, fmean_ref, ig_out, dw_out, dgain_out, fmean_out, wide_dw, ig, dgain, fmean, sem, small_sem
):
    slots, step = wide_dw.shape[:2]
    steps = dw_ref.shape[0] // step

    def copy(k):
        return pltpu.make_async_copy(
            wide_dw.at[k % slots], dw_out.at[pl.ds(k * step, step)], sem.at[k % slots]
        )

    def convert(k):
        wide_dw[k % slots] = dw_ref[k * step : (k + 1) * step].astype(F32)
        copy(k).start()

    for k in range(slots):
        convert(k)
    slot = ig_ref.shape[1]
    token_rows = lax.broadcasted_iota(jnp.int32, (slot, slot), 0)
    order = jnp.where(time_of_row(slot, (slot, slot), 1) == token_rows, 1.0, 0.0).astype(BF16)
    ig[0] = dot(order, ig_ref[0]).astype(BF16)
    dgain[...] = dgain_ref[0]
    fmean[...] = fmean_ref[0, : fmean.shape[0]]
    small = [
        pltpu.make_async_copy(src, dst, small_sem.at[k])
        for k, (src, dst) in enumerate(((ig, ig_out), (dgain, dgain_out), (fmean, fmean_out)))
    ]
    for one in small:
        one.start()
    for k in range(slots, steps):
        copy(k - slots).wait()
        convert(k)
    for one in small:
        one.wait()
    for k in range(steps - slots, steps):
        copy(k).wait()


def finish(input_grad, weight_grads, gain_grads, means, sections):
    width, pack = weight_grads.shape
    vmem = pl.BlockSpec(memory_space=pltpu.VMEM)
    anywhere = pl.BlockSpec(memory_space=pl.ANY)
    slots = 8
    return pl.pallas_call(
        finish_kernel,
        out_shape=(
            jax.ShapeDtypeStruct(input_grad.shape, BF16),
            jax.ShapeDtypeStruct(weight_grads.shape, F32),
            jax.ShapeDtypeStruct((width,), F32),
            jax.ShapeDtypeStruct((sections // 2,), F32),
        ),
        in_specs=[vmem] * 4,
        out_specs=(anywhere,) * 4,
        scratch_shapes=[
            pltpu.VMEM((slots, FINISH_ROWS, pack), F32),
            pltpu.VMEM(input_grad.shape, BF16),
            pltpu.VMEM((width,), F32),
            pltpu.VMEM((sections // 2,), F32),
            pltpu.SemaphoreType.DMA((slots,)),
            pltpu.SemaphoreType.DMA((3,)),
        ],
        compiler_params=pltpu.CompilerParams(vmem_limit_bytes=16 * 1024 * 1024),
    )(weight_grads, input_grad, gain_grads, means)


def local(count, inputs, cotangent, section_weights, norm_gains, doc_lengths, slot_fill):
    sections = lax.axis_size("section")
    slot, width = inputs.shape[1:]
    pack = section_weights.shape[1]
    gate, ff, half = pack // 4, pack // 2, pack // 2
    tokens = sections * slot
    pieces = half * width // (PIECE[0] * PIECE[1])
    dma = pltpu.SemaphoreType.DMA
    ring = min(pieces + max(LENT), RING_PER_CHIP * (count // 2))
    own = pltpu.VMEM((pieces, *PIECE), BF16)
    hosted = pltpu.VMEM((pieces + max(LENT), *PIECE), BF16)
    small = pltpu.VMEM((8, width), F32)
    stack = pltpu.VMEM((tokens, width), BF16)
    vmem = pl.BlockSpec(memory_space=pltpu.VMEM)
    anywhere = pl.BlockSpec(memory_space=pl.ANY)
    input_grad, weight_grads, gain_grads, means = pl.pallas_call(
        functools.partial(kernel, count),
        out_shape=(
            pltpu.VMEM((1, slot, width), BF16),
            pltpu.VMEM((width, pack), BF16),
            pltpu.VMEM((1, width), F32),
            pltpu.VMEM((1, LANES), F32),
        ),
        in_specs=[anywhere] * 6,
        out_specs=(vmem, vmem, vmem, vmem),
        scratch_shapes=[
            pltpu.VMEM((width, pack), BF16), pltpu.VMEM((pack, width), BF16),
            stack, stack, stack, stack, stack,
            pltpu.VMEM((slot, width), BF16), pltpu.VMEM((slot, width), BF16),
            pltpu.VMEM((sections, 8, slot), F32), pltpu.VMEM((8, slot), F32),
            pltpu.VMEM((slot, LANES), F32), pltpu.VMEM((slot, LANES), F32),
            pltpu.VMEM((slot, width), BF16),
            pltpu.VMEM(inputs.shape, BF16), pltpu.VMEM(inputs.shape, BF16), pltpu.VMEM((1, width), F32),
            pltpu.SMEM(doc_lengths.shape, jnp.int32), pltpu.SMEM(slot_fill.shape, jnp.int32),
            pltpu.VMEM((tokens, pack), F32),
            pltpu.VMEM((tokens, pack), BF16),
            pltpu.VMEM((2, width, tokens), BF16),
            pltpu.VMEM((8, GATE_CHUNK), F32),
            own, own, hosted, hosted, hosted,
            pltpu.VMEM((max(LENT), *PIECE), BF16), pltpu.VMEM(PIECE, F32),
            small, small, small, small, small,
            pltpu.VMEM((sections // 2, 8, width), F32),
            dma, dma((5,)), dma, dma,
            dma((sections // 2,)),
            dma((sections,)), dma((sections,)), dma((sections,)), dma((sections,)),
            dma((sections,)), dma, dma, dma, pltpu.SemaphoreType.REGULAR,
            dma, dma((SIB_RING,)), dma, dma((ring * SUB,)), dma, dma((ring * SUB,)),
            dma, dma, dma((max(LENT),)), dma, dma((max(LENT),)),
            dma((3,)), dma((3,)), dma((sections - 1,)), dma((sections // 2,)),
        ],
        compiler_params=pltpu.CompilerParams(
            collective_id=0, has_side_effects=True, vmem_limit_bytes=56 * 1024 * 1024
        ),
    )(inputs, cotangent, section_weights, norm_gains.reshape(1, width), doc_lengths, slot_fill)
    return finish(input_grad, weight_grads, gain_grads, means, sections)


def solution(mesh):
    placed = (
        P("section", "dp", None),
        P("section", "dp", None),
        P("section", None),
        P("section"),
        P("section", "dp", None),
        P("section", "dp"),
    )
    return jax.shard_map(
        functools.partial(local, mesh.shape["dp"]),
        mesh=mesh,
        in_specs=placed,
        out_specs=(P("section", "dp", None), P("section", None), P("section"), P()),
        check_vma=False,
    )
```

```python
import functools

import jax
import jax.numpy as jnp
from jax import lax
from jax.experimental import pallas as pl
from jax.experimental.pallas import tpu as pltpu
from jax.sharding import PartitionSpec as P

EPS = 1e-06
MESH = pl.DeviceIdType.MESH
F32 = jnp.float32
BF16 = jnp.bfloat16
LANES = 128
GATE_CHUNK = 256
BACK_CHUNK = 512
DENSE_CHUNK = 512
LAST_CHUNK = 256
TURN = 256
PIECE = (256, 128)
LENT = (7, 2)
HOST_AT = 26
SUB = 2
RING_PER_CHIP = 3
SIB_RING = 6
LAG = 2
STRIDE = 3
SECOND_TURNS = 5
FIRST_TURNS = 1
SMALL_STEP = 3
FINISH_ROWS = 32


def dot(left, right):
    return jnp.dot(left, right, preferred_element_type=F32)


def time_of_row(slot, shape, axis):
    row = lax.broadcasted_iota(jnp.int32, shape, axis)
    return (row & 7) * (slot // 8) + (row >> 3)


def scan_down(decay, drive):
    blocks = range(8, decay.shape[0], 8)
    factor, value = [decay[:8]], [drive[:8]]
    for at in blocks:
        here = decay[at : at + 8]
        value.append(drive[at : at + 8] + here * value[-1])
        factor.append(here * factor[-1])
    joined, through = value[-1], factor[-1]
    for by in (1, 2, 4):
        joined = joined + through * pltpu.roll(joined, by, 0)
        through = through * pltpu.roll(through, by, 0)
    before = pltpu.roll(joined, 1, 0)
    state = [v + f * before for v, f in zip(value, factor)]
    return jnp.concatenate(state, 0), jnp.concatenate([before] + state[:-1], 0)


def scan_up(decay, source):
    rows = decay.shape[0]
    ahead = [decay[at : at + 8] for at in range(8, rows, 8)] + [pltpu.roll(decay[:8], 7, 0)]
    factor, value = [ahead[-1]], [source[rows - 8 :]]
    for k in range(rows // 8 - 2, -1, -1):
        value.append(source[8 * k : 8 * k + 8] + ahead[k] * value[-1])
        factor.append(ahead[k] * factor[-1])
    joined, through = value[-1], factor[-1]
    for by in (1, 2, 4):
        joined = joined + through * pltpu.roll(joined, 8 - by, 0)
        through = through * pltpu.roll(through, 8 - by, 0)
    after = pltpu.roll(joined, 7, 0)
    return jnp.concatenate([v + f * after for v, f in zip(value[::-1], factor[::-1])], 0)


def ahead_of(starts, compute):
    coming = compute(starts[0])
    for k, start in enumerate(starts):
        now = coming
        if k + 1 < len(starts):
            coming = compute(starts[k + 1])
        yield start, now


def wide(column, width):
    return jnp.concatenate([column] * (width // LANES), 1)


def unit(x):
    return lax.rsqrt(jnp.mean(x * x, axis=-1, keepdims=True) + EPS)


def norm_back(x, q, gain, d_normed, grad_out):
    x_hat = x * q
    scaled = d_normed * gain
    mean = jnp.mean(scaled * x_hat, axis=-1, keepdims=True)
    d_gain = jnp.sum(d_normed * x_hat, axis=0, keepdims=True)
    return grad_out + q * (scaled - x_hat * mean), d_gain


def gelu_parts(u):
    cdf = 0.5 * lax.erf(u * 0.7071067811865476) + 0.5
    slope = cdf + u * (0.3989422804014327 * jnp.exp(-0.5 * u * u))
    return u * cdf, slope


def kernel(
    count,
    x_hbm, cot_hbm, w_hbm, gain_hbm, len_hbm, fill_hbm,
    ig_ref, dw_ref, dgain_ref, fmean_ref,
    w, wt, res, grad, out, gout, normal, x_own, dy_own, mask, mask_own, keep_col, valid_col, relay, x_ref, cot_ref, gain_ref, len_ref, fill_ref,
    stash, rows, left, forget_acc,
    sib_out, sib_in, outer_in, part, tot_in, guest_in, work,
    small, small_sib, small_outer, small_part, small_tot, small_far,
    w_sem, load_sem, x_send, dy_send, mask_send, res_send, res_recv, grad_send, grad_recv, mask_recv, ig_recv, relay_send, relay_recv, turn_sem,
    sib_send, sib_recv, part_send, outer_recv, tot_send, tot_recv, fin_send, fin_recv, guest_recv, back_send, back_recv,
    small_send, small_recv, far_send, far_recv,
):
    s = lax.axis_index("section")
    d = lax.axis_index("dp")
    core = lax.rem(d, 2)
    chip = d // 2
    chips = count // 2
    sections, slot = mask.shape[0], mask.shape[2]
    tokens, width = res.shape
    pack = w.shape[1]
    gate = pack // 4
    ff = pack // 2
    half = pack // 2
    pieces = sib_in.shape[0]
    piece_rows, piece = sib_in.shape[1:]
    ring = outer_recv.shape[0] // SUB
    stacked = width // piece_rows
    last = sections - 1
    partner = last - s
    lent = jnp.where(s == 0, LENT[0], jnp.where(s == 1, LENT[1], 0))
    hosted = jnp.where(partner == 0, LENT[0], jnp.where(partner == 1, LENT[1], 0))
    mine = lax.rem(core + chip, 2)
    is_first = s == 0
    is_last = s == last
    is_mixer = lax.rem(s, 2) == 0
    on_left = chip < chips // 2
    is_middle = (chip == chips // 2 - 1) | (chip == chips // 2)
    is_end = (chip == 0) | (chip == chips - 1)
    other = d + 1 - 2 * core
    sibling = (s, other)
    inner = (s, jnp.where(on_left, other + 2, other - 2))
    outer = (s, jnp.where(on_left, other - 2, other + 2))

    loads = [
        pltpu.make_async_copy(src, dst, load_sem.at[k])
        for k, (src, dst) in enumerate(
            ((x_hbm, x_ref), (len_hbm, len_ref), (fill_hbm, fill_ref), (cot_hbm, cot_ref), (gain_hbm, gain_ref))
        )
    ]
    w_copy = pltpu.make_async_copy(w_hbm, w, w_sem)
    for load in loads:
        load.start()
    w_early = is_first | is_last | (core == 0)

    @pl.when(w_early)
    def _():
        w_copy.start()

    barrier = pltpu.get_barrier_semaphore()
    for by in range(1, sections):
        for lane_of in (d, other):
            pl.semaphore_signal(
                barrier, inc=1, device_id=(lax.rem(s + by, sections), lane_of), device_id_type=MESH
            )
    pl.semaphore_signal(barrier, inc=1, device_id=sibling, device_id_type=MESH)

    @pl.when(chip > 0)
    def _():
        pl.semaphore_signal(barrier, inc=1, device_id=(s, other - 2), device_id_type=MESH)

    @pl.when(chip < chips - 1)
    def _():
        pl.semaphore_signal(barrier, inc=1, device_id=(s, other + 2), device_id_type=MESH)

    def remote(src, dst, send, recv, target):
        return pltpu.make_async_remote_copy(
            src_ref=src, dst_ref=dst, send_sem=send, recv_sem=recv, device_id=target, device_id_type=MESH
        )

    order = jnp.where(
        lax.broadcasted_iota(jnp.int32, (slot, slot), 1) == time_of_row(slot, (slot, slot), 0), 1.0, 0.0
    )
    order_low = order.astype(BF16)
    for load in loads:
        load.wait()
    x_own[...] = dot(order_low, x_ref[0]).astype(BF16)
    lane = lax.broadcasted_iota(jnp.int32, (8, slot), 1)
    row = lax.broadcasted_iota(jnp.int32, (8, slot), 0)
    starts = lane == 0
    position = len_ref[0, 0, 0]
    for k in range(1, len_ref.shape[2]):
        starts = starts | (lane == position)
        position = position + len_ref[0, 0, k]
    keep_rows = jnp.where(starts, 0.0, 1.0)
    valid_rows = jnp.where(lane < fill_ref[0, 0], 1.0, 0.0)
    mask_own[...] = jnp.where(row == 0, keep_rows, valid_rows)
    used_rows = jnp.where(time_of_row(slot, (slot, LANES), 0) < fill_ref[0, 0], 1.0, 0.0)
    dy_own[...] = (dot(order_low, cot_ref[0]) * wide(used_rows, width)).astype(BF16)
    forget_acc[...] = jnp.zeros_like(forget_acc)
    small[...] = jnp.zeros_like(small)

    def whole(m):
        return pl.ds(pl.multiple_of(m * slot, slot), slot)

    def res_in(m):
        return remote(
            out.at[whole(m)], res.at[whole(m)], res_send.at[m], res_recv.at[m], (jnp.minimum(s + 1, last), other)
        )

    def grad_in(m):
        return remote(
            gout.at[whole(m)], grad.at[whole(m)], grad_send.at[m], grad_recv.at[m], (jnp.maximum(s - 1, 0), other)
        )

    def home(m, to):
        return remote(gout.at[whole(m)], ig_ref.at[0], grad_send.at[m], ig_recv, (to, other))

    def wait_res(m):
        @pl.when((s != 0) | (m != 0))
        def _():
            res_in(m).wait_recv()

    def send_grad(m):
        @pl.when(s != 0)
        def _():
            grad_in(m).start()

        @pl.when((s == 0) & (m == 0))
        def _():
            ig_ref[0] = gout[whole(m)]

        @pl.when((s == 0) & (m != 0))
        def _():
            home(m, m).start()

    def turn(side, source, m):
        at = whole(m)
        left[side, :, at] = source[at].T

    def turn_weights(start, stop):
        def one(k, carry):
            at = pl.ds(pl.multiple_of(k * TURN, TURN), TURN)
            wt[at, :] = w[:, at].T
            return carry

        lax.fori_loop(start, stop, one, 0)

    def norm_in(m):
        x = res[whole(m)].astype(F32)
        q = unit(x)
        return x, q, (x * q * gain).astype(BF16)

    def finish_back(m, x, q, d_normed):
        d_res, d_gain = norm_back(x, q, gain, d_normed, grad[whole(m)].astype(F32))
        gout[whole(m)] = d_res.astype(BF16)
        send_grad(m)
        small[0:1, :] += d_gain

    gain = gain_ref[...]

    def mixer_forward(m, halfway=None):
        at = whole(m)
        masks = mask[m]
        keep_col[...] = jnp.broadcast_to(jnp.sum(order * masks[0:1], axis=1, keepdims=True), (slot, LANES))
        valid_col[...] = jnp.broadcast_to(jnp.sum(order * masks[1:2], axis=1, keepdims=True), (slot, LANES))
        wait_res(m)
        keep = wide(keep_col[...], GATE_CHUNK)
        valid = wide(valid_col[...], GATE_CHUNK)
        x, _, normed = norm_in(m)
        normal[at] = normed
        total = x

        def project(c):
            return [dot(normed, w[:, k * gate + c : k * gate + c + GATE_CHUNK]) for k in range(3)]

        for c, (f_in, i_in, c_in) in ahead_of(range(0, gate, GATE_CHUNK), project):
            least = jnp.minimum(jnp.minimum(f_in, i_in), 0.0)
            e_zero = jnp.exp(least)
            e_f = jnp.exp(least - f_in)
            e_i = jnp.exp(least - i_in)
            u_f = e_zero + e_f
            u_i = e_zero + e_i
            inv = 1.0 / (u_f + u_i)
            forget = u_i * inv
            intake = u_f * inv
            soft = jnp.maximum(c_in, 0.0) + jnp.log1p(jnp.exp(-jnp.abs(c_in)))
            decay = forget * keep
            state, previous = scan_down(decay, intake * soft)
            state_low = state.astype(BF16)
            total = total + dot(state_low, wt[3 * gate + c : 3 * gate + c + GATE_CHUNK, :])
            rows[at, 3 * gate + c : 3 * gate + c + GATE_CHUNK] = state_low
            bend = soft - keep * previous
            if halfway is not None and c == gate // 4:
                halfway()
            stash[at, c : c + GATE_CHUNK] = -forget * (e_f * inv) * bend
            stash[at, gate + c : gate + c + GATE_CHUNK] = intake * (e_i * inv) * bend
            stash[at, 2 * gate + c : 2 * gate + c + GATE_CHUNK] = intake * jnp.exp(c_in - soft)
            stash[at, 3 * gate + c : 3 * gate + c + GATE_CHUNK] = decay
            counted = forget * valid
            folded = counted[:8]
            for k in range(8, slot, 8):
                folded = folded + counted[k : k + 8]
            forget_acc[...] += folded
        out[at] = total.astype(BF16)

    inner_turns = 3 * gate // TURN

    @pl.when(is_first)
    def _():
        res[0:slot] = x_own[...]
        mask[0] = mask_own[...]
        w_copy.wait()
        turn_weights(inner_turns, pack // TURN)
        mixer_forward(0)

    pl.semaphore_wait(
        barrier, 2 * sections - 1 + jnp.where(chip > 0, 1, 0) + jnp.where(chip < chips - 1, 1, 0)
    )

    x_copy = remote(x_own, res.at[whole(s)], x_send, res_recv.at[s], (0, other))
    dy_copy = remote(
        dy_own, grad.at[whole(s)], dy_send, grad_recv.at[s], (last, d)
    )
    dy_relayed = remote(dy_own, relay, dy_send, relay_recv, (2, d))
    dy_onward = remote(relay, grad.at[whole(0)], relay_send, grad_recv.at[0], (last, other))
    mask_copies = [
        remote(mask_own, mask.at[s], mask_send.at[k], mask_recv.at[s], (2 * k, jnp.where(is_first, d, other)))
        for k in range(sections // 2)
    ]

    for k in range(sections // 2):

        @pl.when((s != 0) | (k != 0))
        def _():
            mask_copies[k].start()

    @pl.when(is_last)
    def _():
        grad[whole(last)] = dy_own[...]

    @pl.when(jnp.logical_not(w_early))
    def _():
        x_copy.start()
        x_copy.wait_send()
        w_copy.start()

    @pl.when(s != 0)
    def _():
        w_copy.wait()
        turn_weights(0, SECOND_TURNS)

        @pl.when((s != last) & (core == 0))
        def _():
            x_copy.start()

        turn_weights(SECOND_TURNS, pack // TURN)

        @pl.when(is_last & (core == 1))
        def _():
            x_copy.start()

    @pl.when(is_first)
    def _():
        @pl.when(core == 0)
        def _():
            res_in(0).start()

        dy_relayed.start()
        turn_weights(0, FIRST_TURNS)

        @pl.when(core == 1)
        def _():
            res_in(0).start()

        turn(0, normal, 0)

    def give_turn():
        pl.semaphore_signal(turn_sem, inc=1, device_id=sibling, device_id_type=MESH)

    def take_turn():
        pl.semaphore_wait(turn_sem, 1)

    @pl.when((s != 0) & (s != last))
    def _():
        dy_copy.start()

    @pl.when(is_mixer)
    def _():
        @pl.when(s == 2)
        def _():
            dy_relayed.wait_recv()
            dy_onward.start()

        def forward(m, carry):
            @pl.when((s != 0) | (m != 0))
            def _():
                remote(mask_own, mask.at[m], mask_send.at[0], mask_recv.at[m], (0, d)).wait_recv()

            mixer_forward(m)

            @pl.when(is_first & (core == 1))
            def _():
                take_turn()

            res_in(m).start()
            turn(0, normal, m)
            return carry

        lax.fori_loop(jnp.where(is_first, 1, 0), jnp.where(is_first, 2, sections), forward, 0)

        @pl.when(is_first)
        def _():
            def by_turns(m, carry):
                remote(mask_own, mask.at[m], mask_send.at[0], mask_recv.at[m], (0, d)).wait_recv()
                mixer_forward(m, give_turn)
                take_turn()
                res_in(m).start()
                turn(0, normal, m)
                return carry

            lax.fori_loop(2, sections, by_turns, 0)
            turn_weights(FIRST_TURNS, inner_turns)

            @pl.when(core == 0)
            def _():
                give_turn()

        def backward(m, carry):
            at = whole(m)
            x, q, _ = norm_in(m)
            grad_in(m).wait_recv()
            g_low = grad[at]
            d_normed = jnp.zeros((slot, width), F32)

            def project(c):
                return dot(g_low, w[:, 3 * gate + c : 3 * gate + c + BACK_CHUNK])

            for c, d_state in ahead_of(range(0, gate, BACK_CHUNK), project):
                adjoint = scan_up(stash[at, 3 * gate + c : 3 * gate + c + BACK_CHUNK], d_state)
                for k in range(3):
                    here = slice(k * gate + c, k * gate + c + BACK_CHUNK)
                    low = (adjoint * stash[at, here]).astype(BF16)
                    rows[at, here] = low
                    d_normed = d_normed + dot(low, wt[here, :])
            finish_back(m, x, q, d_normed)
            turn(1, grad, m)
            return carry

        lax.fori_loop(0, sections, backward, 0)

    @pl.when((lax.rem(s, 2) == 1) & (s != last))
    def _():
        def forward(m, carry):
            wait_res(m)
            at = whole(m)
            x, _, normed = norm_in(m)
            normal[at] = normed
            total = x

            def project(c):
                return dot(normed, w[:, c : c + DENSE_CHUNK])

            for c, hidden_in in ahead_of(range(0, ff, DENSE_CHUNK), project):
                hidden, bend = gelu_parts(hidden_in)
                low = hidden.astype(BF16)
                total = total + dot(low, wt[ff + c : ff + c + DENSE_CHUNK, :])
                rows[at, ff + c : ff + c + DENSE_CHUNK] = low
                stash[at, c : c + DENSE_CHUNK] = bend
            out[at] = total.astype(BF16)

            res_in(m).start()
            turn(0, normal, m)
            return carry

        lax.fori_loop(0, sections, forward, 0)

        def backward(m, carry):
            at = whole(m)
            x, q, _ = norm_in(m)
            grad_in(m).wait_recv()
            g_low = grad[at]
            d_normed = jnp.zeros((slot, width), F32)

            def project(c):
                return dot(g_low, w[:, ff + c : ff + c + DENSE_CHUNK])

            for c, d_act in ahead_of(range(0, ff, DENSE_CHUNK), project):
                low = (d_act * stash[at, c : c + DENSE_CHUNK]).astype(BF16)
                rows[at, c : c + DENSE_CHUNK] = low
                d_normed = d_normed + dot(low, wt[c : c + DENSE_CHUNK, :])
            finish_back(m, x, q, d_normed)
            turn(1, grad, m)
            return carry

        lax.fori_loop(0, sections, backward, 0)

    @pl.when(is_last)
    def _():
        def prepare(k, carry):
            m = last - k

            @pl.when(m != last)
            def _():
                grad_in(m).wait_recv()

            at = whole(m)
            g_low = grad[at]
            for c in range(0, ff, DENSE_CHUNK):
                stash[at, c : c + DENSE_CHUNK] = dot(g_low, w[:, ff + c : ff + c + DENSE_CHUNK])
            turn(1, grad, m)

            @pl.when((k == 0) & (core == 0))
            def _():
                x_copy.start()

            return carry

        lax.fori_loop(0, sections, prepare, 0)

        def both(m, carry):
            wait_res(m)
            at = whole(m)
            x, q, normed = norm_in(m)
            normal[at] = normed
            d_normed = jnp.zeros((slot, width), F32)

            def project(c):
                return dot(normed, w[:, c : c + LAST_CHUNK])

            for c, hidden_in in ahead_of(range(0, ff, LAST_CHUNK), project):
                hidden, bend = gelu_parts(hidden_in)
                rows[at, ff + c : ff + c + LAST_CHUNK] = hidden.astype(BF16)
                low = (stash[at, c : c + LAST_CHUNK] * bend).astype(BF16)
                rows[at, c : c + LAST_CHUNK] = low
                d_normed = d_normed + dot(low, wt[c : c + LAST_CHUNK, :])
            finish_back(m, x, q, d_normed)
            turn(0, normal, m)
            return carry

        lax.fori_loop(0, sections, both, 0)

    @pl.when(is_mixer)
    def _():
        small[1:2, 0:GATE_CHUNK] = jnp.sum(forget_acc[...], axis=0, keepdims=True)
        used = mask[0, 1:2]
        for m in range(1, sections):
            used = used + mask[m, 1:2]
        small[2:3, 0:slot] = used

    split = jnp.where(is_mixer, 3 * gate, ff)

    def rows_at(k):
        return pl.ds(pl.multiple_of(lax.rem(k, stacked) * piece_rows, piece_rows), piece_rows)

    def cols_at(k, part_of):
        return pl.ds(pl.multiple_of(part_of * half + k // stacked * piece, piece), piece)

    def grad_piece(k, part_of):
        side = jnp.where(part_of * half + k // stacked * piece < split, 0, 1)
        return dot(left[side, rows_at(k)], rows[:, cols_at(k, part_of)])

    def sib_copy(k):
        return remote(sib_out.at[k], sib_in.at[k], sib_send, sib_recv.at[lax.rem(k, sib_recv.shape[0])], sibling)

    sub_rows = piece_rows // SUB

    def sub(buffer, k, q):
        return buffer.at[k, q * sub_rows : (q + 1) * sub_rows]

    def sub_at(k, q):
        first = lax.rem(k, stacked) * piece_rows + q * sub_rows
        return pl.ds(pl.multiple_of(first, sub_rows), sub_rows)

    def sem_at(r, q):
        return lax.rem(r, ring) * SUB + q

    def inward(k, r, q):
        return remote(sub(part, k, q), sub(outer_in, k, q), part_send, outer_recv.at[sem_at(r, q)], inner)

    def across(k, r, q):
        return remote(sub(part, k, q), sub(tot_in, k, q), part_send, tot_recv.at[sem_at(r, q)], inner)

    def outward(k, r, q):
        return remote(sub(tot_in, k, q), sub(tot_in, k, q), tot_send, tot_recv.at[sem_at(r, q)], outer)

    def lent_piece(j):
        return STRIDE * j + STRIDE - 1

    def lend(k):
        return remote(part.at[lent_piece(k)], guest_in.at[k], part_send, guest_recv.at[k], (partner, d))

    def give_back(j):
        return remote(tot_in.at[pieces + j], tot_in.at[lent_piece(j)], back_send, back_recv.at[j], (partner, d))

    def final(k, q):
        return remote(sub(tot_in, k, q), dw_ref.at[sub_at(k, q), cols_at(k, mine)], fin_send, fin_recv, sibling)

    small_swap = remote(small, small_sib, small_send.at[0], small_recv.at[0], sibling)
    small_inward = remote(small_part, small_outer, small_send.at[1], small_recv.at[1], inner)
    small_across = remote(small_part, small_tot, small_send.at[1], small_recv.at[2], inner)
    small_outward = remote(small_tot, small_tot, small_send.at[2], small_recv.at[2], outer)

    def to_sibling(k):
        sib_out[k] = grad_piece(k, 1 - mine).astype(BF16)
        sib_copy(k).start()

    to_sibling(0)
    small_swap.start()

    def reduce_small():
        small_swap.wait_recv()

        @pl.when(is_end)
        def _():
            small_part[...] = small[...] + small_sib[...]

        @pl.when(jnp.logical_not(is_end))
        def _():
            small_inward.wait_recv()
            small_part[...] = small[...] + small_sib[...] + small_outer[...]

        @pl.when(is_middle)
        def _():
            small_across.start()

        @pl.when(jnp.logical_not(is_middle))
        def _():
            small_inward.start()

    def far_copy(k):
        return remote(
            small_tot, small_far.at[s // 2], far_send.at[k - 1], far_recv.at[s // 2], (lax.rem(s + k, sections), other)
        )

    def total_small():
        small_across.wait_recv()

        @pl.when(is_middle)
        def _():
            small_tot[...] = small_tot[...] + small_part[...]

        @pl.when(jnp.logical_not(is_end))
        def _():
            small_outward.start()

        @pl.when(is_mixer)
        def _():
            small_far[s // 2] = small_tot[...]
            for k in range(1, sections):
                far_copy(k).start()

    def is_lent(k):
        return (k < STRIDE * lent) & (lax.rem(k, STRIDE) == STRIDE - 1)

    def reduce_piece(k, r):
        @pl.when(k < pieces)
        def _():
            work[...] = grad_piece(k, mine)
            sib_copy(k).wait_recv()
            work[...] += sib_in[k].astype(F32)

        @pl.when(k >= pieces)
        def _():
            lend(k - pieces).wait_recv()
            work[...] = guest_in[k - pieces].astype(F32)

        on_line = jnp.logical_not(is_lent(k))

        def pass_on(has_outer, send):
            if not has_outer:
                part[k] = work[...].astype(BF16)
            for q in range(SUB):
                if has_outer:
                    inward(k, r, q).wait_recv()
                    here = slice(q * sub_rows, (q + 1) * sub_rows)
                    part[k, here] = (work[here] + outer_in[k, here].astype(F32)).astype(BF16)
                send(k, r, q).start()

        @pl.when(is_lent(k))
        def _():
            part[k] = work[...].astype(BF16)
            lend(k // STRIDE).start()

        @pl.when(on_line & is_middle)
        def _():
            pass_on(chips > 2, across)

        if chips > 2:

            @pl.when(on_line & is_end)
            def _():
                pass_on(False, inward)

        if chips > 4:

            @pl.when(on_line & jnp.logical_not(is_end | is_middle))
            def _():
                pass_on(True, inward)

    def total_piece(k, r):
        @pl.when(is_lent(k))
        def _():
            give_back(k // STRIDE).wait_recv()
            for q in range(SUB):
                final(k, q).start()

        @pl.when(jnp.logical_not(is_lent(k)))
        def _():
            for q in range(SUB):
                here = slice(q * sub_rows, (q + 1) * sub_rows)
                across(k, r, q).wait_recv()

                @pl.when(is_middle)
                def _():
                    tot_in[k, here] = (tot_in[k, here].astype(F32) + part[k, here].astype(F32)).astype(BF16)

                @pl.when(jnp.logical_not(is_end))
                def _():
                    outward(k, r, q).start()

                @pl.when(k < pieces)
                def _():
                    final(k, q).start()

        @pl.when(k < pieces)
        def _():
            dw_ref[rows_at(k), cols_at(k, mine)] = tot_in[k]

        @pl.when(k >= pieces)
        def _():
            give_back(k - pieces).start()

    on_list = pieces + hosted
    on_line = on_list - lent
    late = on_line - LAG

    def listed(i):
        return jnp.where(
            i < HOST_AT, i, jnp.where(i < HOST_AT + hosted, i - HOST_AT + pieces, i - hosted)
        )

    def line_place(i):
        return jnp.where(i < STRIDE * lent, i // STRIDE * (STRIDE - 1) + lax.rem(i, STRIDE), i - lent)

    def of_line(r):
        few = STRIDE - 1
        return listed(jnp.where(r < few * lent, r // few * STRIDE + lax.rem(r, few), r + lent))

    def in_order(p):
        r = jnp.where(p < late, p, p - lent)
        return jnp.where((p >= late) & (p < late + lent), lent_piece(p - late), of_line(r)), r

    lag = jnp.where(is_middle, LAG, jnp.minimum(ring - 2, on_line))

    def step(i, carry):
        own = jnp.where(i < HOST_AT, i, i - hosted)
        working = i < on_list
        place = line_place(i)

        @pl.when((own + 1 < pieces) & ((i < HOST_AT) | (i >= HOST_AT + hosted)))
        def _():
            to_sibling(own + 1)

        @pl.when(working)
        def _():
            reduce_piece(listed(i), place)

        @pl.when(i == SMALL_STEP)
        def _():
            reduce_small()

        @pl.when(i == jnp.where(is_middle, 3 * SMALL_STEP, on_list + SMALL_STEP))
        def _():
            total_small()

        taken = working & jnp.logical_not(is_lent(i)) & (place >= lag)
        at = jnp.where(working, place - lag, on_line - lag + i - on_list)

        @pl.when(taken | jnp.logical_not(working))
        def _():
            total_piece(*in_order(at))

        return carry

    lax.fori_loop(0, on_list + lag + lent, step, 0)

    for k in range(sections // 2):

        @pl.when(s != 2 * k)
        def _():
            remote(small_tot, small_far.at[k], far_send.at[0], far_recv.at[k], sibling).wait_recv()

    dgain_ref[...] = small_tot[0:1, :]
    lanes = lax.broadcasted_iota(jnp.int32, (1, LANES), 1)
    means = jnp.zeros((1, LANES), F32)
    for k in range(sections // 2):
        sums = jnp.sum(small_far[k], axis=1, keepdims=True)
        means = jnp.where(lanes == k, sums[1:2] / (sums[2:3] * gate), means)
    fmean_ref[...] = means

    @pl.when(s != 0)
    def _():
        home(0, s).wait_recv()
        grad_in(0).wait_send()

    for m in range(1, sections):
        grad_in(m).wait_send()

    @pl.when(s == 2)
    def _():
        dy_onward.wait_send()

    @pl.when(s != last)
    def _():
        dy_copy.wait_send()

    @pl.when(w_early & (s != 0))
    def _():
        x_copy.wait_send()

    for k in range(sections // 2):

        @pl.when((s != 0) | (k != 0))
        def _():
            mask_copies[k].wait_send()

    for m in range(sections):

        @pl.when(s != last)
        def _():
            res_in(m).wait_send()

    small_swap.wait_send()
    small_across.wait_send()

    @pl.when(jnp.logical_not(is_end))
    def _():
        small_outward.wait_send()

    @pl.when(is_mixer)
    def _():
        for k in range(1, sections):
            far_copy(k).wait_send()

    remote(sib_out, sib_in, sib_send, sib_recv.at[0], sibling).wait_send()

    def sent(source, sem, n):
        remote(source.at[pl.ds(0, n)], source.at[pl.ds(0, n)], sem, sib_recv.at[0], sibling).wait_send()

    for q in range(sections):
        given = LENT[q] if q < len(LENT) else 0
        taken = LENT[last - q] if last - q < len(LENT) else 0

        @pl.when((s == q) & jnp.logical_not(is_end))
        def _():
            sent(tot_in, tot_send, pieces - given + taken)

        @pl.when(s == q)
        def _():
            sent(part, part_send, pieces + taken)
            if taken:
                sent(guest_in, back_send, taken)

    sent(tot_in, fin_send, pieces)
    their_half = dw_ref.at[:, pl.ds(pl.multiple_of((1 - mine) * half, half), half)]
    remote(their_half, their_half, fin_send, fin_recv, sibling).wait_recv()


def finish_kernel(
    dw_ref, ig_ref, dgain_ref, fmean_ref, ig_out, dw_out, dgain_out, fmean_out, wide_dw, ig, dgain, fmean, sem, small_sem
):
    slots, step = wide_dw.shape[:2]
    steps = dw_ref.shape[0] // step

    def copy(k):
        return pltpu.make_async_copy(
            wide_dw.at[k % slots], dw_out.at[pl.ds(k * step, step)], sem.at[k % slots]
        )

    def convert(k):
        wide_dw[k % slots] = dw_ref[k * step : (k + 1) * step].astype(F32)
        copy(k).start()

    for k in range(slots):
        convert(k)
    slot = ig_ref.shape[1]
    token_rows = lax.broadcasted_iota(jnp.int32, (slot, slot), 0)
    order = jnp.where(time_of_row(slot, (slot, slot), 1) == token_rows, 1.0, 0.0).astype(BF16)
    ig[0] = dot(order, ig_ref[0]).astype(BF16)
    dgain[...] = dgain_ref[0]
    fmean[...] = fmean_ref[0, : fmean.shape[0]]
    small = [
        pltpu.make_async_copy(src, dst, small_sem.at[k])
        for k, (src, dst) in enumerate(((ig, ig_out), (dgain, dgain_out), (fmean, fmean_out)))
    ]
    for one in small:
        one.start()
    for k in range(slots, steps):
        copy(k - slots).wait()
        convert(k)
    for one in small:
        one.wait()
    for k in range(steps - slots, steps):
        copy(k).wait()


def finish(input_grad, weight_grads, gain_grads, means, sections):
    width, pack = weight_grads.shape
    vmem = pl.BlockSpec(memory_space=pltpu.VMEM)
    anywhere = pl.BlockSpec(memory_space=pl.ANY)
    slots = 8
    return pl.pallas_call(
        finish_kernel,
        out_shape=(
            jax.ShapeDtypeStruct(input_grad.shape, BF16),
            jax.ShapeDtypeStruct(weight_grads.shape, F32),
            jax.ShapeDtypeStruct((width,), F32),
            jax.ShapeDtypeStruct((sections // 2,), F32),
        ),
        in_specs=[vmem] * 4,
        out_specs=(anywhere,) * 4,
        scratch_shapes=[
            pltpu.VMEM((slots, FINISH_ROWS, pack), F32),
            pltpu.VMEM(input_grad.shape, BF16),
            pltpu.VMEM((width,), F32),
            pltpu.VMEM((sections // 2,), F32),
            pltpu.SemaphoreType.DMA((slots,)),
            pltpu.SemaphoreType.DMA((3,)),
        ],
        compiler_params=pltpu.CompilerParams(vmem_limit_bytes=16 * 1024 * 1024),
    )(weight_grads, input_grad, gain_grads, means)


def local(count, inputs, cotangent, section_weights, norm_gains, doc_lengths, slot_fill):
    sections = lax.axis_size("section")
    slot, width = inputs.shape[1:]
    pack = section_weights.shape[1]
    gate, ff, half = pack // 4, pack // 2, pack // 2
    tokens = sections * slot
    pieces = half * width // (PIECE[0] * PIECE[1])
    dma = pltpu.SemaphoreType.DMA
    ring = min(pieces + max(LENT), RING_PER_CHIP * (count // 2))
    own = pltpu.VMEM((pieces, *PIECE), BF16)
    hosted = pltpu.VMEM((pieces + max(LENT), *PIECE), BF16)
    small = pltpu.VMEM((8, width), F32)
    stack = pltpu.VMEM((tokens, width), BF16)
    vmem = pl.BlockSpec(memory_space=pltpu.VMEM)
    anywhere = pl.BlockSpec(memory_space=pl.ANY)
    input_grad, weight_grads, gain_grads, means = pl.pallas_call(
        functools.partial(kernel, count),
        out_shape=(
            pltpu.VMEM((1, slot, width), BF16),
            pltpu.VMEM((width, pack), BF16),
            pltpu.VMEM((1, width), F32),
            pltpu.VMEM((1, LANES), F32),
        ),
        in_specs=[anywhere] * 6,
        out_specs=(vmem, vmem, vmem, vmem),
        scratch_shapes=[
            pltpu.VMEM((width, pack), BF16), pltpu.VMEM((pack, width), BF16),
            stack, stack, stack, stack, stack,
            pltpu.VMEM((slot, width), BF16), pltpu.VMEM((slot, width), BF16),
            pltpu.VMEM((sections, 8, slot), F32), pltpu.VMEM((8, slot), F32),
            pltpu.VMEM((slot, LANES), F32), pltpu.VMEM((slot, LANES), F32),
            pltpu.VMEM((slot, width), BF16),
            pltpu.VMEM(inputs.shape, BF16), pltpu.VMEM(inputs.shape, BF16), pltpu.VMEM((1, width), F32),
            pltpu.SMEM(doc_lengths.shape, jnp.int32), pltpu.SMEM(slot_fill.shape, jnp.int32),
            pltpu.VMEM((tokens, pack), F32),
            pltpu.VMEM((tokens, pack), BF16),
            pltpu.VMEM((2, width, tokens), BF16),
            pltpu.VMEM((8, GATE_CHUNK), F32),
            own, own, hosted, hosted, hosted,
            pltpu.VMEM((max(LENT), *PIECE), BF16), pltpu.VMEM(PIECE, F32),
            small, small, small, small, small,
            pltpu.VMEM((sections // 2, 8, width), F32),
            dma, dma((5,)), dma, dma,
            dma((sections // 2,)),
            dma((sections,)), dma((sections,)), dma((sections,)), dma((sections,)),
            dma((sections,)), dma, dma, dma, pltpu.SemaphoreType.REGULAR,
            dma, dma((SIB_RING,)), dma, dma((ring * SUB,)), dma, dma((ring * SUB,)),
            dma, dma, dma((max(LENT),)), dma, dma((max(LENT),)),
            dma((3,)), dma((3,)), dma((sections - 1,)), dma((sections // 2,)),
        ],
        compiler_params=pltpu.CompilerParams(
            collective_id=0, has_side_effects=True, vmem_limit_bytes=56 * 1024 * 1024
        ),
    )(inputs, cotangent, section_weights, norm_gains.reshape(1, width), doc_lengths, slot_fill)
    return finish(input_grad, weight_grads, gain_grads, means, sections)


def solution(mesh):
    placed = (
        P("section", "dp", None),
        P("section", "dp", None),
        P("section", None),
        P("section"),
        P("section", "dp", None),
        P("section", "dp"),
    )
    return jax.shard_map(
        functools.partial(local, mesh.shape["dp"]),
        mesh=mesh,
        in_specs=placed,
        out_specs=(P("section", "dp", None), P("section", None), P("section"), P()),
        check_vma=False,
    )
```

```python
import functools

import jax
import jax.numpy as jnp
from jax import lax
from jax.experimental import pallas as pl
from jax.experimental.pallas import tpu as pltpu
from jax.sharding import PartitionSpec as P

EPS = 1e-06
MESH = pl.DeviceIdType.MESH
F32 = jnp.float32
BF16 = jnp.bfloat16
LANES = 128
GATE_CHUNK = 256
BACK_CHUNK = 512
DENSE_CHUNK = 512
LAST_CHUNK = 256
TURN = 256
PIECE = (256, 128)
LENT = (7, 2)
HOST_AT = 23
SUB = 2
RING_PER_CHIP = 3
SIB_RING = 6
LAG = 2
STRIDE = 2
SECOND_TURNS = 5
FIRST_TURNS = 1
SMALL_STEP = 3
FINISH_ROWS = 32


def dot(left, right):
    return jnp.dot(left, right, preferred_element_type=F32)


def time_of_row(slot, shape, axis):
    row = lax.broadcasted_iota(jnp.int32, shape, axis)
    return (row & 7) * (slot // 8) + (row >> 3)


def scan_down(decay, drive):
    blocks = range(8, decay.shape[0], 8)
    factor, value = [decay[:8]], [drive[:8]]
    for at in blocks:
        here = decay[at : at + 8]
        value.append(drive[at : at + 8] + here * value[-1])
        factor.append(here * factor[-1])
    joined, through = value[-1], factor[-1]
    for by in (1, 2, 4):
        joined = joined + through * pltpu.roll(joined, by, 0)
        through = through * pltpu.roll(through, by, 0)
    before = pltpu.roll(joined, 1, 0)
    state = [v + f * before for v, f in zip(value, factor)]
    return jnp.concatenate(state, 0), jnp.concatenate([before] + state[:-1], 0)


def scan_up(decay, source):
    rows = decay.shape[0]
    ahead = [decay[at : at + 8] for at in range(8, rows, 8)] + [pltpu.roll(decay[:8], 7, 0)]
    factor, value = [ahead[-1]], [source[rows - 8 :]]
    for k in range(rows // 8 - 2, -1, -1):
        value.append(source[8 * k : 8 * k + 8] + ahead[k] * value[-1])
        factor.append(ahead[k] * factor[-1])
    joined, through = value[-1], factor[-1]
    for by in (1, 2, 4):
        joined = joined + through * pltpu.roll(joined, 8 - by, 0)
        through = through * pltpu.roll(through, 8 - by, 0)
    after = pltpu.roll(joined, 7, 0)
    return jnp.concatenate([v + f * after for v, f in zip(value[::-1], factor[::-1])], 0)


def ahead_of(starts, compute):
    coming = compute(starts[0])
    for k, start in enumerate(starts):
        now = coming
        if k + 1 < len(starts):
            coming = compute(starts[k + 1])
        yield start, now


def wide(column, width):
    return jnp.concatenate([column] * (width // LANES), 1)


def unit(x):
    return lax.rsqrt(jnp.mean(x * x, axis=-1, keepdims=True) + EPS)


def norm_back(x, q, gain, d_normed, grad_out):
    x_hat = x * q
    scaled = d_normed * gain
    mean = jnp.mean(scaled * x_hat, axis=-1, keepdims=True)
    d_gain = jnp.sum(d_normed * x_hat, axis=0, keepdims=True)
    return grad_out + q * (scaled - x_hat * mean), d_gain


def gelu_parts(u):
    cdf = 0.5 * lax.erf(u * 0.7071067811865476) + 0.5
    slope = cdf + u * (0.3989422804014327 * jnp.exp(-0.5 * u * u))
    return u * cdf, slope


def kernel(
    count,
    x_hbm, cot_hbm, w_hbm, gain_hbm, len_hbm, fill_hbm,
    ig_ref, dw_ref, dgain_ref, fmean_ref,
    w, wt, res, grad, out, gout, normal, x_own, dy_own, mask, mask_own, keep_col, valid_col, relay, x_ref, cot_ref, gain_ref, len_ref, fill_ref,
    stash, rows, left, forget_acc,
    sib_out, sib_in, outer_in, part, tot_in, guest_in, work,
    small, small_sib, small_outer, small_part, small_tot, small_far,
    w_sem, load_sem, x_send, dy_send, mask_send, res_send, res_recv, grad_send, grad_recv, mask_recv, ig_recv, relay_send, relay_recv, turn_sem,
    sib_send, sib_recv, part_send, outer_recv, tot_send, tot_recv, fin_send, fin_recv, guest_recv, back_send, back_recv,
    small_send, small_recv, far_send, far_recv,
):
    s = lax.axis_index("section")
    d = lax.axis_index("dp")
    core = lax.rem(d, 2)
    chip = d // 2
    chips = count // 2
    sections, slot = mask.shape[0], mask.shape[2]
    tokens, width = res.shape
    pack = w.shape[1]
    gate = pack // 4
    ff = pack // 2
    half = pack // 2
    pieces = sib_in.shape[0]
    piece_rows, piece = sib_in.shape[1:]
    ring = outer_recv.shape[0] // SUB
    stacked = width // piece_rows
    last = sections - 1
    partner = last - s
    lent = jnp.where(s == 0, LENT[0], jnp.where(s == 1, LENT[1], 0))
    hosted = jnp.where(partner == 0, LENT[0], jnp.where(partner == 1, LENT[1], 0))
    mine = lax.rem(core + chip, 2)
    is_first = s == 0
    is_last = s == last
    is_mixer = lax.rem(s, 2) == 0
    on_left = chip < chips // 2
    is_middle = (chip == chips // 2 - 1) | (chip == chips // 2)
    is_end = (chip == 0) | (chip == chips - 1)
    other = d + 1 - 2 * core
    sibling = (s, other)
    inner = (s, jnp.where(on_left, other + 2, other - 2))
    outer = (s, jnp.where(on_left, other - 2, other + 2))

    loads = [
        pltpu.make_async_copy(src, dst, load_sem.at[k])
        for k, (src, dst) in enumerate(
            ((x_hbm, x_ref), (len_hbm, len_ref), (fill_hbm, fill_ref), (cot_hbm, cot_ref), (gain_hbm, gain_ref))
        )
    ]
    w_copy = pltpu.make_async_copy(w_hbm, w, w_sem)
    for load in loads:
        load.start()
    w_early = is_first | is_last | (core == 0)

    @pl.when(w_early)
    def _():
        w_copy.start()

    barrier = pltpu.get_barrier_semaphore()
    for by in range(1, sections):
        for lane_of in (d, other):
            pl.semaphore_signal(
                barrier, inc=1, device_id=(lax.rem(s + by, sections), lane_of), device_id_type=MESH
            )
    pl.semaphore_signal(barrier, inc=1, device_id=sibling, device_id_type=MESH)

    @pl.when(chip > 0)
    def _():
        pl.semaphore_signal(barrier, inc=1, device_id=(s, other - 2), device_id_type=MESH)

    @pl.when(chip < chips - 1)
    def _():
        pl.semaphore_signal(barrier, inc=1, device_id=(s, other + 2), device_id_type=MESH)

    def remote(src, dst, send, recv, target):
        return pltpu.make_async_remote_copy(
            src_ref=src, dst_ref=dst, send_sem=send, recv_sem=recv, device_id=target, device_id_type=MESH
        )

    order = jnp.where(
        lax.broadcasted_iota(jnp.int32, (slot, slot), 1) == time_of_row(slot, (slot, slot), 0), 1.0, 0.0
    )
    order_low = order.astype(BF16)
    for load in loads:
        load.wait()
    x_own[...] = dot(order_low, x_ref[0]).astype(BF16)
    lane = lax.broadcasted_iota(jnp.int32, (8, slot), 1)
    row = lax.broadcasted_iota(jnp.int32, (8, slot), 0)
    starts = lane == 0
    position = len_ref[0, 0, 0]
    for k in range(1, len_ref.shape[2]):
        starts = starts | (lane == position)
        position = position + len_ref[0, 0, k]
    keep_rows = jnp.where(starts, 0.0, 1.0)
    valid_rows = jnp.where(lane < fill_ref[0, 0], 1.0, 0.0)
    mask_own[...] = jnp.where(row == 0, keep_rows, valid_rows)
    used_rows = jnp.where(time_of_row(slot, (slot, LANES), 0) < fill_ref[0, 0], 1.0, 0.0)
    dy_own[...] = (dot(order_low, cot_ref[0]) * wide(used_rows, width)).astype(BF16)
    forget_acc[...] = jnp.zeros_like(forget_acc)
    small[...] = jnp.zeros_like(small)

    def whole(m):
        return pl.ds(pl.multiple_of(m * slot, slot), slot)

    def res_in(m):
        return remote(
            out.at[whole(m)], res.at[whole(m)], res_send.at[m], res_recv.at[m], (jnp.minimum(s + 1, last), other)
        )

    def grad_in(m):
        return remote(
            gout.at[whole(m)], grad.at[whole(m)], grad_send.at[m], grad_recv.at[m], (jnp.maximum(s - 1, 0), other)
        )

    def home(m, to):
        return remote(gout.at[whole(m)], ig_ref.at[0], grad_send.at[m], ig_recv, (to, other))

    def wait_res(m):
        @pl.when((s != 0) | (m != 0))
        def _():
            res_in(m).wait_recv()

    def send_grad(m):
        @pl.when(s != 0)
        def _():
            grad_in(m).start()

        @pl.when((s == 0) & (m == 0))
        def _():
            ig_ref[0] = gout[whole(m)]

        @pl.when((s == 0) & (m != 0))
        def _():
            home(m, m).start()

    def turn(side, source, m):
        at = whole(m)
        left[side, :, at] = source[at].T

    def turn_weights(start, stop):
        def one(k, carry):
            at = pl.ds(pl.multiple_of(k * TURN, TURN), TURN)
            wt[at, :] = w[:, at].T
            return carry

        lax.fori_loop(start, stop, one, 0)

    def norm_in(m):
        x = res[whole(m)].astype(F32)
        q = unit(x)
        return x, q, (x * q * gain).astype(BF16)

    def finish_back(m, x, q, d_normed):
        d_res, d_gain = norm_back(x, q, gain, d_normed, grad[whole(m)].astype(F32))
        gout[whole(m)] = d_res.astype(BF16)
        send_grad(m)
        small[0:1, :] += d_gain

    gain = gain_ref[...]

    def mixer_forward(m, halfway=None):
        at = whole(m)
        masks = mask[m]
        keep_col[...] = jnp.broadcast_to(jnp.sum(order * masks[0:1], axis=1, keepdims=True), (slot, LANES))
        valid_col[...] = jnp.broadcast_to(jnp.sum(order * masks[1:2], axis=1, keepdims=True), (slot, LANES))
        wait_res(m)
        keep = wide(keep_col[...], GATE_CHUNK)
        valid = wide(valid_col[...], GATE_CHUNK)
        x, _, normed = norm_in(m)
        normal[at] = normed
        total = x

        def project(c):
            return [dot(normed, w[:, k * gate + c : k * gate + c + GATE_CHUNK]) for k in range(3)]

        for c, (f_in, i_in, c_in) in ahead_of(range(0, gate, GATE_CHUNK), project):
            least = jnp.minimum(jnp.minimum(f_in, i_in), 0.0)
            e_zero = jnp.exp(least)
            e_f = jnp.exp(least - f_in)
            e_i = jnp.exp(least - i_in)
            u_f = e_zero + e_f
            u_i = e_zero + e_i
            inv = 1.0 / (u_f + u_i)
            forget = u_i * inv
            intake = u_f * inv
            soft = jnp.maximum(c_in, 0.0) + jnp.log1p(jnp.exp(-jnp.abs(c_in)))
            decay = forget * keep
            state, previous = scan_down(decay, intake * soft)
            state_low = state.astype(BF16)
            total = total + dot(state_low, wt[3 * gate + c : 3 * gate + c + GATE_CHUNK, :])
            rows[at, 3 * gate + c : 3 * gate + c + GATE_CHUNK] = state_low
            bend = soft - keep * previous
            if halfway is not None and c == gate // 4:
                halfway()
            stash[at, c : c + GATE_CHUNK] = -forget * (e_f * inv) * bend
            stash[at, gate + c : gate + c + GATE_CHUNK] = intake * (e_i * inv) * bend
            stash[at, 2 * gate + c : 2 * gate + c + GATE_CHUNK] = intake * jnp.exp(c_in - soft)
            stash[at, 3 * gate + c : 3 * gate + c + GATE_CHUNK] = decay
            counted = forget * valid
            folded = counted[:8]
            for k in range(8, slot, 8):
                folded = folded + counted[k : k + 8]
            forget_acc[...] += folded
        out[at] = total.astype(BF16)

    inner_turns = 3 * gate // TURN

    @pl.when(is_first)
    def _():
        res[0:slot] = x_own[...]
        mask[0] = mask_own[...]
        w_copy.wait()
        turn_weights(inner_turns, pack // TURN)
        mixer_forward(0)

    pl.semaphore_wait(
        barrier, 2 * sections - 1 + jnp.where(chip > 0, 1, 0) + jnp.where(chip < chips - 1, 1, 0)
    )

    x_copy = remote(x_own, res.at[whole(s)], x_send, res_recv.at[s], (0, other))
    dy_copy = remote(
        dy_own, grad.at[whole(s)], dy_send, grad_recv.at[s], (last, d)
    )
    dy_relayed = remote(dy_own, relay, dy_send, relay_recv, (2, d))
    dy_onward = remote(relay, grad.at[whole(0)], relay_send, grad_recv.at[0], (last, other))
    mask_copies = [
        remote(mask_own, mask.at[s], mask_send.at[k], mask_recv.at[s], (2 * k, jnp.where(is_first, d, other)))
        for k in range(sections // 2)
    ]

    for k in range(sections // 2):

        @pl.when((s != 0) | (k != 0))
        def _():
            mask_copies[k].start()

    @pl.when(is_last)
    def _():
        grad[whole(last)] = dy_own[...]

    @pl.when(jnp.logical_not(w_early))
    def _():
        x_copy.start()
        x_copy.wait_send()
        w_copy.start()

    @pl.when(s != 0)
    def _():
        w_copy.wait()
        turn_weights(0, SECOND_TURNS)

        @pl.when((s != last) & (core == 0))
        def _():
            x_copy.start()

        turn_weights(SECOND_TURNS, pack // TURN)

        @pl.when(is_last & (core == 1))
        def _():
            x_copy.start()

    @pl.when(is_first)
    def _():
        @pl.when(core == 0)
        def _():
            res_in(0).start()

        dy_relayed.start()
        turn_weights(0, FIRST_TURNS)

        @pl.when(core == 1)
        def _():
            res_in(0).start()

        turn(0, normal, 0)

    def give_turn():
        pl.semaphore_signal(turn_sem, inc=1, device_id=sibling, device_id_type=MESH)

    def take_turn():
        pl.semaphore_wait(turn_sem, 1)

    @pl.when((s != 0) & (s != last))
    def _():
        dy_copy.start()

    @pl.when(is_mixer)
    def _():
        @pl.when(s == 2)
        def _():
            dy_relayed.wait_recv()
            dy_onward.start()

        def forward(m, carry):
            @pl.when((s != 0) | (m != 0))
            def _():
                remote(mask_own, mask.at[m], mask_send.at[0], mask_recv.at[m], (0, d)).wait_recv()

            mixer_forward(m)

            @pl.when(is_first & (core == 1))
            def _():
                take_turn()

            res_in(m).start()
            turn(0, normal, m)
            return carry

        lax.fori_loop(jnp.where(is_first, 1, 0), jnp.where(is_first, 2, sections), forward, 0)

        @pl.when(is_first)
        def _():
            def by_turns(m, carry):
                remote(mask_own, mask.at[m], mask_send.at[0], mask_recv.at[m], (0, d)).wait_recv()
                mixer_forward(m, give_turn)
                take_turn()
                res_in(m).start()
                turn(0, normal, m)
                return carry

            lax.fori_loop(2, sections, by_turns, 0)
            turn_weights(FIRST_TURNS, inner_turns)

            @pl.when(core == 0)
            def _():
                give_turn()

        def backward(m, carry):
            at = whole(m)
            x, q, _ = norm_in(m)
            grad_in(m).wait_recv()
            g_low = grad[at]
            d_normed = jnp.zeros((slot, width), F32)

            def project(c):
                return dot(g_low, w[:, 3 * gate + c : 3 * gate + c + BACK_CHUNK])

            for c, d_state in ahead_of(range(0, gate, BACK_CHUNK), project):
                adjoint = scan_up(stash[at, 3 * gate + c : 3 * gate + c + BACK_CHUNK], d_state)
                for k in range(3):
                    here = slice(k * gate + c, k * gate + c + BACK_CHUNK)
                    low = (adjoint * stash[at, here]).astype(BF16)
                    rows[at, here] = low
                    d_normed = d_normed + dot(low, wt[here, :])
            finish_back(m, x, q, d_normed)
            turn(1, grad, m)
            return carry

        lax.fori_loop(0, sections, backward, 0)

    @pl.when((lax.rem(s, 2) == 1) & (s != last))
    def _():
        def forward(m, carry):
            wait_res(m)
            at = whole(m)
            x, _, normed = norm_in(m)
            normal[at] = normed
            total = x

            def project(c):
                return dot(normed, w[:, c : c + DENSE_CHUNK])

            for c, hidden_in in ahead_of(range(0, ff, DENSE_CHUNK), project):
                hidden, bend = gelu_parts(hidden_in)
                low = hidden.astype(BF16)
                total = total + dot(low, wt[ff + c : ff + c + DENSE_CHUNK, :])
                rows[at, ff + c : ff + c + DENSE_CHUNK] = low
                stash[at, c : c + DENSE_CHUNK] = bend
            out[at] = total.astype(BF16)

            res_in(m).start()
            turn(0, normal, m)
            return carry

        lax.fori_loop(0, sections, forward, 0)

        def backward(m, carry):
            at = whole(m)
            x, q, _ = norm_in(m)
            grad_in(m).wait_recv()
            g_low = grad[at]
            d_normed = jnp.zeros((slot, width), F32)

            def project(c):
                return dot(g_low, w[:, ff + c : ff + c + DENSE_CHUNK])

            for c, d_act in ahead_of(range(0, ff, DENSE_CHUNK), project):
                low = (d_act * stash[at, c : c + DENSE_CHUNK]).astype(BF16)
                rows[at, c : c + DENSE_CHUNK] = low
                d_normed = d_normed + dot(low, wt[c : c + DENSE_CHUNK, :])
            finish_back(m, x, q, d_normed)
            turn(1, grad, m)
            return carry

        lax.fori_loop(0, sections, backward, 0)

    @pl.when(is_last)
    def _():
        def prepare(k, carry):
            m = last - k

            @pl.when(m != last)
            def _():
                grad_in(m).wait_recv()

            at = whole(m)
            g_low = grad[at]
            for c in range(0, ff, DENSE_CHUNK):
                stash[at, c : c + DENSE_CHUNK] = dot(g_low, w[:, ff + c : ff + c + DENSE_CHUNK])
            turn(1, grad, m)

            @pl.when((k == 0) & (core == 0))
            def _():
                x_copy.start()

            return carry

        lax.fori_loop(0, sections, prepare, 0)

        def both(m, carry):
            wait_res(m)
            at = whole(m)
            x, q, normed = norm_in(m)
            normal[at] = normed
            d_normed = jnp.zeros((slot, width), F32)

            def project(c):
                return dot(normed, w[:, c : c + LAST_CHUNK])

            for c, hidden_in in ahead_of(range(0, ff, LAST_CHUNK), project):
                hidden, bend = gelu_parts(hidden_in)
                rows[at, ff + c : ff + c + LAST_CHUNK] = hidden.astype(BF16)
                low = (stash[at, c : c + LAST_CHUNK] * bend).astype(BF16)
                rows[at, c : c + LAST_CHUNK] = low
                d_normed = d_normed + dot(low, wt[c : c + LAST_CHUNK, :])
            finish_back(m, x, q, d_normed)
            turn(0, normal, m)
            return carry

        lax.fori_loop(0, sections, both, 0)

    @pl.when(is_mixer)
    def _():
        small[1:2, 0:GATE_CHUNK] = jnp.sum(forget_acc[...], axis=0, keepdims=True)
        used = mask[0, 1:2]
        for m in range(1, sections):
            used = used + mask[m, 1:2]
        small[2:3, 0:slot] = used

    split = jnp.where(is_mixer, 3 * gate, ff)

    def rows_at(k):
        return pl.ds(pl.multiple_of(lax.rem(k, stacked) * piece_rows, piece_rows), piece_rows)

    def cols_at(k, part_of):
        return pl.ds(pl.multiple_of(part_of * half + k // stacked * piece, piece), piece)

    def grad_piece(k, part_of):
        side = jnp.where(part_of * half + k // stacked * piece < split, 0, 1)
        return dot(left[side, rows_at(k)], rows[:, cols_at(k, part_of)])

    def sib_copy(k):
        return remote(sib_out.at[k], sib_in.at[k], sib_send, sib_recv.at[lax.rem(k, sib_recv.shape[0])], sibling)

    sub_rows = piece_rows // SUB

    def sub(buffer, k, q):
        return buffer.at[k, q * sub_rows : (q + 1) * sub_rows]

    def sub_at(k, q):
        first = lax.rem(k, stacked) * piece_rows + q * sub_rows
        return pl.ds(pl.multiple_of(first, sub_rows), sub_rows)

    def sem_at(r, q):
        return lax.rem(r, ring) * SUB + q

    def inward(k, r, q):
        return remote(sub(part, k, q), sub(outer_in, k, q), part_send, outer_recv.at[sem_at(r, q)], inner)

    def across(k, r, q):
        return remote(sub(part, k, q), sub(tot_in, k, q), part_send, tot_recv.at[sem_at(r, q)], inner)

    def outward(k, r, q):
        return remote(sub(tot_in, k, q), sub(tot_in, k, q), tot_send, tot_recv.at[sem_at(r, q)], outer)

    def lent_piece(j):
        return STRIDE * j + STRIDE - 1

    def lend(k):
        return remote(part.at[lent_piece(k)], guest_in.at[k], part_send, guest_recv.at[k], (partner, d))

    def give_back(j):
        return remote(tot_in.at[pieces + j], tot_in.at[lent_piece(j)], back_send, back_recv.at[j], (partner, d))

    def final(k, q):
        return remote(sub(tot_in, k, q), dw_ref.at[sub_at(k, q), cols_at(k, mine)], fin_send, fin_recv, sibling)

    small_swap = remote(small, small_sib, small_send.at[0], small_recv.at[0], sibling)
    small_inward = remote(small_part, small_outer, small_send.at[1], small_recv.at[1], inner)
    small_across = remote(small_part, small_tot, small_send.at[1], small_recv.at[2], inner)
    small_outward = remote(small_tot, small_tot, small_send.at[2], small_recv.at[2], outer)

    def to_sibling(k):
        sib_out[k] = grad_piece(k, 1 - mine).astype(BF16)
        sib_copy(k).start()

    to_sibling(0)
    small_swap.start()

    def reduce_small():
        small_swap.wait_recv()

        @pl.when(is_end)
        def _():
            small_part[...] = small[...] + small_sib[...]

        @pl.when(jnp.logical_not(is_end))
        def _():
            small_inward.wait_recv()
            small_part[...] = small[...] + small_sib[...] + small_outer[...]

        @pl.when(is_middle)
        def _():
            small_across.start()

        @pl.when(jnp.logical_not(is_middle))
        def _():
            small_inward.start()

    def far_copy(k):
        return remote(
            small_tot, small_far.at[s // 2], far_send.at[k - 1], far_recv.at[s // 2], (lax.rem(s + k, sections), other)
        )

    def total_small():
        small_across.wait_recv()

        @pl.when(is_middle)
        def _():
            small_tot[...] = small_tot[...] + small_part[...]

        @pl.when(jnp.logical_not(is_end))
        def _():
            small_outward.start()

        @pl.when(is_mixer)
        def _():
            small_far[s // 2] = small_tot[...]
            for k in range(1, sections):
                far_copy(k).start()

    def is_lent(k):
        return (k < STRIDE * lent) & (lax.rem(k, STRIDE) == STRIDE - 1)

    def reduce_piece(k, r):
        @pl.when(k < pieces)
        def _():
            work[...] = grad_piece(k, mine)
            sib_copy(k).wait_recv()
            work[...] += sib_in[k].astype(F32)

        @pl.when(k >= pieces)
        def _():
            lend(k - pieces).wait_recv()
            work[...] = guest_in[k - pieces].astype(F32)

        on_line = jnp.logical_not(is_lent(k))

        def pass_on(has_outer, send):
            if not has_outer:
                part[k] = work[...].astype(BF16)
            for q in range(SUB):
                if has_outer:
                    inward(k, r, q).wait_recv()
                    here = slice(q * sub_rows, (q + 1) * sub_rows)
                    part[k, here] = (work[here] + outer_in[k, here].astype(F32)).astype(BF16)
                send(k, r, q).start()

        @pl.when(is_lent(k))
        def _():
            part[k] = work[...].astype(BF16)
            lend(k // STRIDE).start()

        @pl.when(on_line & is_middle)
        def _():
            pass_on(chips > 2, across)

        if chips > 2:

            @pl.when(on_line & is_end)
            def _():
                pass_on(False, inward)

        if chips > 4:

            @pl.when(on_line & jnp.logical_not(is_end | is_middle))
            def _():
                pass_on(True, inward)

    def total_piece(k, r):
        @pl.when(is_lent(k))
        def _():
            give_back(k // STRIDE).wait_recv()
            for q in range(SUB):
                final(k, q).start()

        @pl.when(jnp.logical_not(is_lent(k)))
        def _():
            for q in range(SUB):
                here = slice(q * sub_rows, (q + 1) * sub_rows)
                across(k, r, q).wait_recv()

                @pl.when(is_middle)
                def _():
                    tot_in[k, here] = (tot_in[k, here].astype(F32) + part[k, here].astype(F32)).astype(BF16)

                @pl.when(jnp.logical_not(is_end))
                def _():
                    outward(k, r, q).start()

                @pl.when(k < pieces)
                def _():
                    final(k, q).start()

        @pl.when(k < pieces)
        def _():
            dw_ref[rows_at(k), cols_at(k, mine)] = tot_in[k]

        @pl.when(k >= pieces)
        def _():
            give_back(k - pieces).start()

    on_list = pieces + hosted
    on_line = on_list - lent
    late = on_line - LAG

    def listed(i):
        return jnp.where(
            i < HOST_AT, i, jnp.where(i < HOST_AT + hosted, i - HOST_AT + pieces, i - hosted)
        )

    def line_place(i):
        return jnp.where(i < STRIDE * lent, i // STRIDE * (STRIDE - 1) + lax.rem(i, STRIDE), i - lent)

    def of_line(r):
        few = STRIDE - 1
        return listed(jnp.where(r < few * lent, r // few * STRIDE + lax.rem(r, few), r + lent))

    def in_order(p):
        r = jnp.where(p < late, p, p - lent)
        return jnp.where((p >= late) & (p < late + lent), lent_piece(p - late), of_line(r)), r

    lag = jnp.where(is_middle, LAG, jnp.minimum(ring - 2, on_line))

    def step(i, carry):
        own = jnp.where(i < HOST_AT, i, i - hosted)
        working = i < on_list
        place = line_place(i)

        @pl.when((own + 1 < pieces) & ((i < HOST_AT) | (i >= HOST_AT + hosted)))
        def _():
            to_sibling(own + 1)

        @pl.when(working)
        def _():
            reduce_piece(listed(i), place)

        @pl.when(i == SMALL_STEP)
        def _():
            reduce_small()

        @pl.when(i == jnp.where(is_middle, 3 * SMALL_STEP, on_list + SMALL_STEP))
        def _():
            total_small()

        taken = working & jnp.logical_not(is_lent(i)) & (place >= lag)
        at = jnp.where(working, place - lag, on_line - lag + i - on_list)

        @pl.when(taken | jnp.logical_not(working))
        def _():
            total_piece(*in_order(at))

        return carry

    lax.fori_loop(0, on_list + lag + lent, step, 0)

    for k in range(sections // 2):

        @pl.when(s != 2 * k)
        def _():
            remote(small_tot, small_far.at[k], far_send.at[0], far_recv.at[k], sibling).wait_recv()

    dgain_ref[...] = small_tot[0:1, :]
    lanes = lax.broadcasted_iota(jnp.int32, (1, LANES), 1)
    means = jnp.zeros((1, LANES), F32)
    for k in range(sections // 2):
        sums = jnp.sum(small_far[k], axis=1, keepdims=True)
        means = jnp.where(lanes == k, sums[1:2] / (sums[2:3] * gate), means)
    fmean_ref[...] = means

    @pl.when(s != 0)
    def _():
        home(0, s).wait_recv()
        grad_in(0).wait_send()

    for m in range(1, sections):
        grad_in(m).wait_send()

    @pl.when(s == 2)
    def _():
        dy_onward.wait_send()

    @pl.when(s != last)
    def _():
        dy_copy.wait_send()

    @pl.when(w_early & (s != 0))
    def _():
        x_copy.wait_send()

    for k in range(sections // 2):

        @pl.when((s != 0) | (k != 0))
        def _():
            mask_copies[k].wait_send()

    for m in range(sections):

        @pl.when(s != last)
        def _():
            res_in(m).wait_send()

    small_swap.wait_send()
    small_across.wait_send()

    @pl.when(jnp.logical_not(is_end))
    def _():
        small_outward.wait_send()

    @pl.when(is_mixer)
    def _():
        for k in range(1, sections):
            far_copy(k).wait_send()

    remote(sib_out, sib_in, sib_send, sib_recv.at[0], sibling).wait_send()

    def sent(source, sem, n):
        remote(source.at[pl.ds(0, n)], source.at[pl.ds(0, n)], sem, sib_recv.at[0], sibling).wait_send()

    for q in range(sections):
        given = LENT[q] if q < len(LENT) else 0
        taken = LENT[last - q] if last - q < len(LENT) else 0

        @pl.when((s == q) & jnp.logical_not(is_end))
        def _():
            sent(tot_in, tot_send, pieces - given + taken)

        @pl.when(s == q)
        def _():
            sent(part, part_send, pieces + taken)
            if taken:
                sent(guest_in, back_send, taken)

    sent(tot_in, fin_send, pieces)
    their_half = dw_ref.at[:, pl.ds(pl.multiple_of((1 - mine) * half, half), half)]
    remote(their_half, their_half, fin_send, fin_recv, sibling).wait_recv()


def finish_kernel(
    dw_ref, ig_ref, dgain_ref, fmean_ref, ig_out, dw_out, dgain_out, fmean_out, wide_dw, ig, dgain, fmean, sem, small_sem
):
    slots, step = wide_dw.shape[:2]
    steps = dw_ref.shape[0] // step

    def copy(k):
        return pltpu.make_async_copy(
            wide_dw.at[k % slots], dw_out.at[pl.ds(k * step, step)], sem.at[k % slots]
        )

    def convert(k):
        wide_dw[k % slots] = dw_ref[k * step : (k + 1) * step].astype(F32)
        copy(k).start()

    for k in range(slots):
        convert(k)
    slot = ig_ref.shape[1]
    token_rows = lax.broadcasted_iota(jnp.int32, (slot, slot), 0)
    order = jnp.where(time_of_row(slot, (slot, slot), 1) == token_rows, 1.0, 0.0).astype(BF16)
    ig[0] = dot(order, ig_ref[0]).astype(BF16)
    dgain[...] = dgain_ref[0]
    fmean[...] = fmean_ref[0, : fmean.shape[0]]
    small = [
        pltpu.make_async_copy(src, dst, small_sem.at[k])
        for k, (src, dst) in enumerate(((ig, ig_out), (dgain, dgain_out), (fmean, fmean_out)))
    ]
    for one in small:
        one.start()
    for k in range(slots, steps):
        copy(k - slots).wait()
        convert(k)
    for one in small:
        one.wait()
    for k in range(steps - slots, steps):
        copy(k).wait()


def finish(input_grad, weight_grads, gain_grads, means, sections):
    width, pack = weight_grads.shape
    vmem = pl.BlockSpec(memory_space=pltpu.VMEM)
    anywhere = pl.BlockSpec(memory_space=pl.ANY)
    slots = 8
    return pl.pallas_call(
        finish_kernel,
        out_shape=(
            jax.ShapeDtypeStruct(input_grad.shape, BF16),
            jax.ShapeDtypeStruct(weight_grads.shape, F32),
            jax.ShapeDtypeStruct((width,), F32),
            jax.ShapeDtypeStruct((sections // 2,), F32),
        ),
        in_specs=[vmem] * 4,
        out_specs=(anywhere,) * 4,
        scratch_shapes=[
            pltpu.VMEM((slots, FINISH_ROWS, pack), F32),
            pltpu.VMEM(input_grad.shape, BF16),
            pltpu.VMEM((width,), F32),
            pltpu.VMEM((sections // 2,), F32),
            pltpu.SemaphoreType.DMA((slots,)),
            pltpu.SemaphoreType.DMA((3,)),
        ],
        compiler_params=pltpu.CompilerParams(vmem_limit_bytes=16 * 1024 * 1024),
    )(weight_grads, input_grad, gain_grads, means)


def local(count, inputs, cotangent, section_weights, norm_gains, doc_lengths, slot_fill):
    sections = lax.axis_size("section")
    slot, width = inputs.shape[1:]
    pack = section_weights.shape[1]
    gate, ff, half = pack // 4, pack // 2, pack // 2
    tokens = sections * slot
    pieces = half * width // (PIECE[0] * PIECE[1])
    dma = pltpu.SemaphoreType.DMA
    ring = min(pieces + max(LENT), RING_PER_CHIP * (count // 2))
    own = pltpu.VMEM((pieces, *PIECE), BF16)
    hosted = pltpu.VMEM((pieces + max(LENT), *PIECE), BF16)
    small = pltpu.VMEM((8, width), F32)
    stack = pltpu.VMEM((tokens, width), BF16)
    vmem = pl.BlockSpec(memory_space=pltpu.VMEM)
    anywhere = pl.BlockSpec(memory_space=pl.ANY)
    input_grad, weight_grads, gain_grads, means = pl.pallas_call(
        functools.partial(kernel, count),
        out_shape=(
            pltpu.VMEM((1, slot, width), BF16),
            pltpu.VMEM((width, pack), BF16),
            pltpu.VMEM((1, width), F32),
            pltpu.VMEM((1, LANES), F32),
        ),
        in_specs=[anywhere] * 6,
        out_specs=(vmem, vmem, vmem, vmem),
        scratch_shapes=[
            pltpu.VMEM((width, pack), BF16), pltpu.VMEM((pack, width), BF16),
            stack, stack, stack, stack, stack,
            pltpu.VMEM((slot, width), BF16), pltpu.VMEM((slot, width), BF16),
            pltpu.VMEM((sections, 8, slot), F32), pltpu.VMEM((8, slot), F32),
            pltpu.VMEM((slot, LANES), F32), pltpu.VMEM((slot, LANES), F32),
            pltpu.VMEM((slot, width), BF16),
            pltpu.VMEM(inputs.shape, BF16), pltpu.VMEM(inputs.shape, BF16), pltpu.VMEM((1, width), F32),
            pltpu.SMEM(doc_lengths.shape, jnp.int32), pltpu.SMEM(slot_fill.shape, jnp.int32),
            pltpu.VMEM((tokens, pack), F32),
            pltpu.VMEM((tokens, pack), BF16),
            pltpu.VMEM((2, width, tokens), BF16),
            pltpu.VMEM((8, GATE_CHUNK), F32),
            own, own, hosted, hosted, hosted,
            pltpu.VMEM((max(LENT), *PIECE), BF16), pltpu.VMEM(PIECE, F32),
            small, small, small, small, small,
            pltpu.VMEM((sections // 2, 8, width), F32),
            dma, dma((5,)), dma, dma,
            dma((sections // 2,)),
            dma((sections,)), dma((sections,)), dma((sections,)), dma((sections,)),
            dma((sections,)), dma, dma, dma, pltpu.SemaphoreType.REGULAR,
            dma, dma((SIB_RING,)), dma, dma((ring * SUB,)), dma, dma((ring * SUB,)),
            dma, dma, dma((max(LENT),)), dma, dma((max(LENT),)),
            dma((3,)), dma((3,)), dma((sections - 1,)), dma((sections // 2,)),
        ],
        compiler_params=pltpu.CompilerParams(
            collective_id=0, has_side_effects=True, vmem_limit_bytes=56 * 1024 * 1024
        ),
    )(inputs, cotangent, section_weights, norm_gains.reshape(1, width), doc_lengths, slot_fill)
    return finish(input_grad, weight_grads, gain_grads, means, sections)


def solution(mesh):
    placed = (
        P("section", "dp", None),
        P("section", "dp", None),
        P("section", None),
        P("section"),
        P("section", "dp", None),
        P("section", "dp"),
    )
    return jax.shard_map(
        functools.partial(local, mesh.shape["dp"]),
        mesh=mesh,
        in_specs=placed,
        out_specs=(P("section", "dp", None), P("section", None), P("section"), P()),
        check_vma=False,
    )
```

```python
import functools

import jax
import jax.numpy as jnp
from jax import lax
from jax.experimental import pallas as pl
from jax.experimental.pallas import tpu as pltpu
from jax.sharding import PartitionSpec as P

EPS = 1e-06
MESH = pl.DeviceIdType.MESH
F32 = jnp.float32
BF16 = jnp.bfloat16
LANES = 128
GATE_CHUNK = 256
BACK_CHUNK = 512
DENSE_CHUNK = 512
LAST_CHUNK = 256
TURN = 256
PIECE = (256, 128)
LENT = (7, 2)
HOST_AT = 23
SUB = 2
RING_PER_CHIP = 3
SIB_RING = 6
LAG = 2
STRIDE = 2
SECOND_TURNS = 5
FIRST_TURNS = 1
SMALL_STEP = 3
FINISH_ROWS = 32


def dot(left, right):
    return jnp.dot(left, right, preferred_element_type=F32)


def time_of_row(slot, shape, axis):
    row = lax.broadcasted_iota(jnp.int32, shape, axis)
    return (row & 7) * (slot // 8) + (row >> 3)


def scan_down(decay, drive):
    blocks = range(8, decay.shape[0], 8)
    factor, value = [decay[:8]], [drive[:8]]
    for at in blocks:
        here = decay[at : at + 8]
        value.append(drive[at : at + 8] + here * value[-1])
        factor.append(here * factor[-1])
    joined, through = value[-1], factor[-1]
    for by in (1, 2, 4):
        joined = joined + through * pltpu.roll(joined, by, 0)
        through = through * pltpu.roll(through, by, 0)
    before = pltpu.roll(joined, 1, 0)
    state = [v + f * before for v, f in zip(value, factor)]
    return jnp.concatenate(state, 0), jnp.concatenate([before] + state[:-1], 0)


def scan_up(decay, source):
    rows = decay.shape[0]
    ahead = [decay[at : at + 8] for at in range(8, rows, 8)] + [pltpu.roll(decay[:8], 7, 0)]
    factor, value = [ahead[-1]], [source[rows - 8 :]]
    for k in range(rows // 8 - 2, -1, -1):
        value.append(source[8 * k : 8 * k + 8] + ahead[k] * value[-1])
        factor.append(ahead[k] * factor[-1])
    joined, through = value[-1], factor[-1]
    for by in (1, 2, 4):
        joined = joined + through * pltpu.roll(joined, 8 - by, 0)
        through = through * pltpu.roll(through, 8 - by, 0)
    after = pltpu.roll(joined, 7, 0)
    return jnp.concatenate([v + f * after for v, f in zip(value[::-1], factor[::-1])], 0)


def ahead_of(starts, compute):
    coming = compute(starts[0])
    for k, start in enumerate(starts):
        now = coming
        if k + 1 < len(starts):
            coming = compute(starts[k + 1])
        yield start, now


def wide(column, width):
    return jnp.concatenate([column] * (width // LANES), 1)


def unit(x):
    return lax.rsqrt(jnp.mean(x * x, axis=-1, keepdims=True) + EPS)


def norm_back(x, q, gain, d_normed, grad_out):
    x_hat = x * q
    scaled = d_normed * gain
    mean = jnp.mean(scaled * x_hat, axis=-1, keepdims=True)
    d_gain = jnp.sum(d_normed * x_hat, axis=0, keepdims=True)
    return grad_out + q * (scaled - x_hat * mean), d_gain


def gelu_parts(u):
    cdf = 0.5 * lax.erf(u * 0.7071067811865476) + 0.5
    slope = cdf + u * (0.3989422804014327 * jnp.exp(-0.5 * u * u))
    return u * cdf, slope


def kernel(
    count,
    x_hbm, cot_hbm, w_hbm, gain_hbm, len_hbm, fill_hbm,
    ig_ref, dw_ref, dgain_ref, fmean_ref,
    w, wt, res, grad, out, gout, normal, x_own, dy_own, mask, mask_own, keep_col, valid_col, relay, x_ref, cot_ref, gain_ref, len_ref, fill_ref,
    stash, rows, left, forget_acc,
    sib_out, sib_in, outer_in, part, tot_in, guest_in, work,
    small, small_sib, small_outer, small_part, small_tot, small_far,
    w_sem, load_sem, x_send, dy_send, mask_send, res_send, res_recv, grad_send, grad_recv, mask_recv, ig_recv, relay_send, relay_recv, turn_sem,
    sib_send, sib_recv, part_send, outer_recv, tot_send, tot_recv, fin_send, fin_recv, guest_recv, back_send, back_recv,
    small_send, small_recv, far_send, far_recv,
):
    s = lax.axis_index("section")
    d = lax.axis_index("dp")
    core = lax.rem(d, 2)
    chip = d // 2
    chips = count // 2
    sections, slot = mask.shape[0], mask.shape[2]
    tokens, width = res.shape
    pack = w.shape[1]
    gate = pack // 4
    ff = pack // 2
    half = pack // 2
    pieces = sib_in.shape[0]
    piece_rows, piece = sib_in.shape[1:]
    ring = outer_recv.shape[0] // SUB
    stacked = width // piece_rows
    last = sections - 1
    partner = last - s
    lent = jnp.where(s == 0, LENT[0], jnp.where(s == 1, LENT[1], 0))
    hosted = jnp.where(partner == 0, LENT[0], jnp.where(partner == 1, LENT[1], 0))
    mine = lax.rem(core + chip, 2)
    is_first = s == 0
    is_last = s == last
    is_mixer = lax.rem(s, 2) == 0
    on_left = chip < chips // 2
    is_middle = (chip == chips // 2 - 1) | (chip == chips // 2)
    is_end = (chip == 0) | (chip == chips - 1)
    other = d + 1 - 2 * core
    sibling = (s, other)
    inner = (s, jnp.where(on_left, other + 2, other - 2))
    outer = (s, jnp.where(on_left, other - 2, other + 2))

    loads = [
        pltpu.make_async_copy(src, dst, load_sem.at[k])
        for k, (src, dst) in enumerate(
            ((x_hbm, x_ref), (len_hbm, len_ref), (fill_hbm, fill_ref), (cot_hbm, cot_ref), (gain_hbm, gain_ref))
        )
    ]
    w_copy = pltpu.make_async_copy(w_hbm, w, w_sem)
    for load in loads:
        load.start()
    w_early = is_first | is_last | (core == 0)

    @pl.when(w_early)
    def _():
        w_copy.start()

    barrier = pltpu.get_barrier_semaphore()
    for by in range(1, sections):
        for lane_of in (d, other):
            pl.semaphore_signal(
                barrier, inc=1, device_id=(lax.rem(s + by, sections), lane_of), device_id_type=MESH
            )
    pl.semaphore_signal(barrier, inc=1, device_id=sibling, device_id_type=MESH)

    @pl.when(chip > 0)
    def _():
        pl.semaphore_signal(barrier, inc=1, device_id=(s, other - 2), device_id_type=MESH)

    @pl.when(chip < chips - 1)
    def _():
        pl.semaphore_signal(barrier, inc=1, device_id=(s, other + 2), device_id_type=MESH)

    def remote(src, dst, send, recv, target):
        return pltpu.make_async_remote_copy(
            src_ref=src, dst_ref=dst, send_sem=send, recv_sem=recv, device_id=target, device_id_type=MESH
        )

    order = jnp.where(
        lax.broadcasted_iota(jnp.int32, (slot, slot), 1) == time_of_row(slot, (slot, slot), 0), 1.0, 0.0
    )
    order_low = order.astype(BF16)
    for load in loads:
        load.wait()
    x_own[...] = dot(order_low, x_ref[0]).astype(BF16)
    lane = lax.broadcasted_iota(jnp.int32, (8, slot), 1)
    row = lax.broadcasted_iota(jnp.int32, (8, slot), 0)
    starts = lane == 0
    position = len_ref[0, 0, 0]
    for k in range(1, len_ref.shape[2]):
        starts = starts | (lane == position)
        position = position + len_ref[0, 0, k]
    keep_rows = jnp.where(starts, 0.0, 1.0)
    valid_rows = jnp.where(lane < fill_ref[0, 0], 1.0, 0.0)
    mask_own[...] = jnp.where(row == 0, keep_rows, valid_rows)
    used_rows = jnp.where(time_of_row(slot, (slot, LANES), 0) < fill_ref[0, 0], 1.0, 0.0)
    dy_own[...] = (dot(order_low, cot_ref[0]) * wide(used_rows, width)).astype(BF16)
    forget_acc[...] = jnp.zeros_like(forget_acc)
    small[...] = jnp.zeros_like(small)

    def whole(m):
        return pl.ds(pl.multiple_of(m * slot, slot), slot)

    def res_in(m):
        return remote(
            out.at[whole(m)], res.at[whole(m)], res_send, res_recv.at[m], (jnp.minimum(s + 1, last), other)
        )

    def grad_in(m):
        return remote(
            gout.at[whole(m)], grad.at[whole(m)], grad_send, grad_recv.at[m], (jnp.maximum(s - 1, 0), other)
        )

    def home(m, to):
        return remote(gout.at[whole(m)], ig_ref.at[0], grad_send, ig_recv, (to, other))

    def wait_res(m):
        @pl.when((s != 0) | (m != 0))
        def _():
            res_in(m).wait_recv()

    def send_grad(m):
        @pl.when(s != 0)
        def _():
            grad_in(m).start()

        @pl.when((s == 0) & (m == 0))
        def _():
            ig_ref[0] = gout[whole(m)]

        @pl.when((s == 0) & (m != 0))
        def _():
            home(m, m).start()

    def turn(side, source, m):
        at = whole(m)
        left[side, :, at] = source[at].T

    def turn_weights(start, stop):
        def one(k, carry):
            at = pl.ds(pl.multiple_of(k * TURN, TURN), TURN)
            wt[at, :] = w[:, at].T
            return carry

        lax.fori_loop(start, stop, one, 0)

    def norm_in(m):
        x = res[whole(m)].astype(F32)
        q = unit(x)
        return x, q, (x * q * gain).astype(BF16)

    def finish_back(m, x, q, d_normed):
        d_res, d_gain = norm_back(x, q, gain, d_normed, grad[whole(m)].astype(F32))
        gout[whole(m)] = d_res.astype(BF16)
        send_grad(m)
        small[0:1, :] += d_gain

    gain = gain_ref[...]

    def mixer_forward(m, halfway=None):
        at = whole(m)
        masks = mask[m]
        keep_col[...] = jnp.broadcast_to(jnp.sum(order * masks[0:1], axis=1, keepdims=True), (slot, LANES))
        valid_col[...] = jnp.broadcast_to(jnp.sum(order * masks[1:2], axis=1, keepdims=True), (slot, LANES))
        wait_res(m)
        keep = wide(keep_col[...], GATE_CHUNK)
        valid = wide(valid_col[...], GATE_CHUNK)
        x, _, normed = norm_in(m)
        normal[at] = normed
        total = x

        def project(c):
            return [dot(normed, w[:, k * gate + c : k * gate + c + GATE_CHUNK]) for k in range(3)]

        for c, (f_in, i_in, c_in) in ahead_of(range(0, gate, GATE_CHUNK), project):
            least = jnp.minimum(jnp.minimum(f_in, i_in), 0.0)
            e_zero = jnp.exp(least)
            e_f = jnp.exp(least - f_in)
            e_i = jnp.exp(least - i_in)
            u_f = e_zero + e_f
            u_i = e_zero + e_i
            inv = 1.0 / (u_f + u_i)
            forget = u_i * inv
            intake = u_f * inv
            soft = jnp.maximum(c_in, 0.0) + jnp.log1p(jnp.exp(-jnp.abs(c_in)))
            decay = forget * keep
            state, previous = scan_down(decay, intake * soft)
            state_low = state.astype(BF16)
            total = total + dot(state_low, wt[3 * gate + c : 3 * gate + c + GATE_CHUNK, :])
            rows[at, 3 * gate + c : 3 * gate + c + GATE_CHUNK] = state_low
            bend = soft - keep * previous
            if halfway is not None and c == gate // 4:
                halfway()
            stash[at, c : c + GATE_CHUNK] = -forget * (e_f * inv) * bend
            stash[at, gate + c : gate + c + GATE_CHUNK] = intake * (e_i * inv) * bend
            stash[at, 2 * gate + c : 2 * gate + c + GATE_CHUNK] = intake * jnp.exp(c_in - soft)
            stash[at, 3 * gate + c : 3 * gate + c + GATE_CHUNK] = decay
            counted = forget * valid
            folded = counted[:8]
            for k in range(8, slot, 8):
                folded = folded + counted[k : k + 8]
            forget_acc[...] += folded
        out[at] = total.astype(BF16)

    inner_turns = 3 * gate // TURN

    @pl.when(is_first)
    def _():
        res[0:slot] = x_own[...]
        mask[0] = mask_own[...]
        w_copy.wait()
        turn_weights(inner_turns, pack // TURN)
        mixer_forward(0)

    pl.semaphore_wait(
        barrier, 2 * sections - 1 + jnp.where(chip > 0, 1, 0) + jnp.where(chip < chips - 1, 1, 0)
    )

    x_copy = remote(x_own, res.at[whole(s)], x_send, res_recv.at[s], (0, other))
    dy_copy = remote(
        dy_own, grad.at[whole(s)], dy_send, grad_recv.at[s], (last, d)
    )
    dy_relayed = remote(dy_own, relay, dy_send, relay_recv, (2, d))
    dy_onward = remote(relay, grad.at[whole(0)], relay_send, grad_recv.at[0], (last, other))
    mask_copies = [
        remote(mask_own, mask.at[s], mask_send.at[k], mask_recv.at[s], (2 * k, jnp.where(is_first, d, other)))
        for k in range(sections // 2)
    ]

    for k in range(sections // 2):

        @pl.when((s != 0) | (k != 0))
        def _():
            mask_copies[k].start()

    @pl.when(is_last)
    def _():
        grad[whole(last)] = dy_own[...]

    @pl.when(jnp.logical_not(w_early))
    def _():
        x_copy.start()
        x_copy.wait_send()
        w_copy.start()

    @pl.when(s != 0)
    def _():
        w_copy.wait()
        turn_weights(0, SECOND_TURNS)

        @pl.when((s != last) & (core == 0))
        def _():
            x_copy.start()

        turn_weights(SECOND_TURNS, pack // TURN)

        @pl.when(is_last & (core == 1))
        def _():
            x_copy.start()

    @pl.when(is_first)
    def _():
        @pl.when(core == 0)
        def _():
            res_in(0).start()

        dy_relayed.start()
        turn_weights(0, FIRST_TURNS)

        @pl.when(core == 1)
        def _():
            res_in(0).start()

        turn(0, normal, 0)

    def give_turn():
        pl.semaphore_signal(turn_sem, inc=1, device_id=sibling, device_id_type=MESH)

    def take_turn():
        pl.semaphore_wait(turn_sem, 1)

    @pl.when((s != 0) & (s != last))
    def _():
        dy_copy.start()

    @pl.when(is_mixer)
    def _():
        @pl.when(s == 2)
        def _():
            dy_relayed.wait_recv()
            dy_onward.start()

        def forward(m, carry):
            @pl.when((s != 0) | (m != 0))
            def _():
                remote(mask_own, mask.at[m], mask_send.at[0], mask_recv.at[m], (0, d)).wait_recv()

            mixer_forward(m)

            @pl.when(is_first & (core == 1))
            def _():
                take_turn()

            res_in(m).start()
            turn(0, normal, m)
            return carry

        lax.fori_loop(jnp.where(is_first, 1, 0), jnp.where(is_first, 2, sections), forward, 0)

        @pl.when(is_first)
        def _():
            def by_turns(m, carry):
                remote(mask_own, mask.at[m], mask_send.at[0], mask_recv.at[m], (0, d)).wait_recv()
                mixer_forward(m, give_turn)
                take_turn()
                res_in(m).start()
                turn(0, normal, m)
                return carry

            lax.fori_loop(2, sections, by_turns, 0)
            turn_weights(FIRST_TURNS, inner_turns)

            @pl.when(core == 0)
            def _():
                give_turn()

        def backward(m, carry):
            at = whole(m)
            x, q, _ = norm_in(m)
            grad_in(m).wait_recv()
            g_low = grad[at]
            d_normed = jnp.zeros((slot, width), F32)

            def project(c):
                return dot(g_low, w[:, 3 * gate + c : 3 * gate + c + BACK_CHUNK])

            for c, d_state in ahead_of(range(0, gate, BACK_CHUNK), project):
                adjoint = scan_up(stash[at, 3 * gate + c : 3 * gate + c + BACK_CHUNK], d_state)
                for k in range(3):
                    here = slice(k * gate + c, k * gate + c + BACK_CHUNK)
                    low = (adjoint * stash[at, here]).astype(BF16)
                    rows[at, here] = low
                    d_normed = d_normed + dot(low, wt[here, :])
            finish_back(m, x, q, d_normed)
            turn(1, grad, m)
            return carry

        lax.fori_loop(0, sections, backward, 0)

    @pl.when((lax.rem(s, 2) == 1) & (s != last))
    def _():
        def forward(m, carry):
            wait_res(m)
            at = whole(m)
            x, _, normed = norm_in(m)
            normal[at] = normed
            total = x

            def project(c):
                return dot(normed, w[:, c : c + DENSE_CHUNK])

            for c, hidden_in in ahead_of(range(0, ff, DENSE_CHUNK), project):
                hidden, bend = gelu_parts(hidden_in)
                low = hidden.astype(BF16)
                total = total + dot(low, wt[ff + c : ff + c + DENSE_CHUNK, :])
                rows[at, ff + c : ff + c + DENSE_CHUNK] = low
                stash[at, c : c + DENSE_CHUNK] = bend
            out[at] = total.astype(BF16)

            res_in(m).start()
            turn(0, normal, m)
            return carry

        lax.fori_loop(0, sections, forward, 0)

        def backward(m, carry):
            at = whole(m)
            x, q, _ = norm_in(m)
            grad_in(m).wait_recv()
            g_low = grad[at]
            d_normed = jnp.zeros((slot, width), F32)

            def project(c):
                return dot(g_low, w[:, ff + c : ff + c + DENSE_CHUNK])

            for c, d_act in ahead_of(range(0, ff, DENSE_CHUNK), project):
                low = (d_act * stash[at, c : c + DENSE_CHUNK]).astype(BF16)
                rows[at, c : c + DENSE_CHUNK] = low
                d_normed = d_normed + dot(low, wt[c : c + DENSE_CHUNK, :])
            finish_back(m, x, q, d_normed)
            turn(1, grad, m)
            return carry

        lax.fori_loop(0, sections, backward, 0)

    @pl.when(is_last)
    def _():
        def prepare(k, carry):
            m = last - k

            @pl.when(m != last)
            def _():
                grad_in(m).wait_recv()

            at = whole(m)
            g_low = grad[at]
            for c in range(0, ff, DENSE_CHUNK):
                stash[at, c : c + DENSE_CHUNK] = dot(g_low, w[:, ff + c : ff + c + DENSE_CHUNK])
            turn(1, grad, m)

            @pl.when((k == 0) & (core == 0))
            def _():
                x_copy.start()

            return carry

        lax.fori_loop(0, sections, prepare, 0)

        def both(m, carry):
            wait_res(m)
            at = whole(m)
            x, q, normed = norm_in(m)
            normal[at] = normed
            d_normed = jnp.zeros((slot, width), F32)

            def project(c):
                return dot(normed, w[:, c : c + LAST_CHUNK])

            for c, hidden_in in ahead_of(range(0, ff, LAST_CHUNK), project):
                hidden, bend = gelu_parts(hidden_in)
                rows[at, ff + c : ff + c + LAST_CHUNK] = hidden.astype(BF16)
                low = (stash[at, c : c + LAST_CHUNK] * bend).astype(BF16)
                rows[at, c : c + LAST_CHUNK] = low
                d_normed = d_normed + dot(low, wt[c : c + LAST_CHUNK, :])
            finish_back(m, x, q, d_normed)
            turn(0, normal, m)
            return carry

        lax.fori_loop(0, sections, both, 0)

    @pl.when(is_mixer)
    def _():
        small[1:2, 0:GATE_CHUNK] = jnp.sum(forget_acc[...], axis=0, keepdims=True)
        used = mask[0, 1:2]
        for m in range(1, sections):
            used = used + mask[m, 1:2]
        small[2:3, 0:slot] = used

    split = jnp.where(is_mixer, 3 * gate, ff)

    def rows_at(k):
        return pl.ds(pl.multiple_of(lax.rem(k, stacked) * piece_rows, piece_rows), piece_rows)

    def cols_at(k, part_of):
        return pl.ds(pl.multiple_of(part_of * half + k // stacked * piece, piece), piece)

    def grad_piece(k, part_of):
        side = jnp.where(part_of * half + k // stacked * piece < split, 0, 1)
        return dot(left[side, rows_at(k)], rows[:, cols_at(k, part_of)])

    def sib_copy(k):
        return remote(sib_out.at[k], sib_in.at[k], sib_send, sib_recv.at[lax.rem(k, sib_recv.shape[0])], sibling)

    sub_rows = piece_rows // SUB

    def sub(buffer, k, q):
        return buffer.at[k, q * sub_rows : (q + 1) * sub_rows]

    def sub_at(k, q):
        first = lax.rem(k, stacked) * piece_rows + q * sub_rows
        return pl.ds(pl.multiple_of(first, sub_rows), sub_rows)

    def sem_at(r, q):
        return lax.rem(r, ring) * SUB + q

    def inward(k, r, q):
        return remote(sub(part, k, q), sub(outer_in, k, q), part_send, outer_recv.at[sem_at(r, q)], inner)

    def across(k, r, q):
        return remote(sub(part, k, q), sub(tot_in, k, q), part_send, tot_recv.at[sem_at(r, q)], inner)

    def outward(k, r, q):
        return remote(sub(tot_in, k, q), sub(tot_in, k, q), tot_send, tot_recv.at[sem_at(r, q)], outer)

    def lent_piece(j):
        return STRIDE * j + STRIDE - 1

    def lend(k):
        return remote(part.at[lent_piece(k)], guest_in.at[k], part_send, guest_recv.at[k], (partner, d))

    def give_back(j):
        return remote(tot_in.at[pieces + j], tot_in.at[lent_piece(j)], back_send, back_recv.at[j], (partner, d))

    def final(k, q):
        return remote(sub(tot_in, k, q), dw_ref.at[sub_at(k, q), cols_at(k, mine)], fin_send, fin_recv, sibling)

    small_swap = remote(small, small_sib, small_send.at[0], small_recv.at[0], sibling)
    small_inward = remote(small_part, small_outer, small_send.at[1], small_recv.at[1], inner)
    small_across = remote(small_part, small_tot, small_send.at[1], small_recv.at[2], inner)
    small_outward = remote(small_tot, small_tot, small_send.at[2], small_recv.at[2], outer)

    def to_sibling(k):
        sib_out[k] = grad_piece(k, 1 - mine).astype(BF16)
        sib_copy(k).start()

    to_sibling(0)
    small_swap.start()

    def reduce_small():
        small_swap.wait_recv()

        @pl.when(is_end)
        def _():
            small_part[...] = small[...] + small_sib[...]

        @pl.when(jnp.logical_not(is_end))
        def _():
            small_inward.wait_recv()
            small_part[...] = small[...] + small_sib[...] + small_outer[...]

        @pl.when(is_middle)
        def _():
            small_across.start()

        @pl.when(jnp.logical_not(is_middle))
        def _():
            small_inward.start()

    def far_copy(k):
        return remote(
            small_tot, small_far.at[s // 2], far_send.at[k - 1], far_recv.at[s // 2], (lax.rem(s + k, sections), other)
        )

    def total_small():
        small_across.wait_recv()

        @pl.when(is_middle)
        def _():
            small_tot[...] = small_tot[...] + small_part[...]

        @pl.when(jnp.logical_not(is_end))
        def _():
            small_outward.start()

        @pl.when(is_mixer)
        def _():
            small_far[s // 2] = small_tot[...]
            for k in range(1, sections):
                far_copy(k).start()

    def is_lent(k):
        return (k < STRIDE * lent) & (lax.rem(k, STRIDE) == STRIDE - 1)

    def reduce_piece(k, r):
        @pl.when(k < pieces)
        def _():
            work[...] = grad_piece(k, mine)
            sib_copy(k).wait_recv()
            work[...] += sib_in[k].astype(F32)

        @pl.when(k >= pieces)
        def _():
            lend(k - pieces).wait_recv()
            work[...] = guest_in[k - pieces].astype(F32)

        on_line = jnp.logical_not(is_lent(k))

        def pass_on(has_outer, send):
            if not has_outer:
                part[k] = work[...].astype(BF16)
            for q in range(SUB):
                if has_outer:
                    inward(k, r, q).wait_recv()
                    here = slice(q * sub_rows, (q + 1) * sub_rows)
                    part[k, here] = (work[here] + outer_in[k, here].astype(F32)).astype(BF16)
                send(k, r, q).start()

        @pl.when(is_lent(k))
        def _():
            part[k] = work[...].astype(BF16)
            lend(k // STRIDE).start()

        @pl.when(on_line & is_middle)
        def _():
            pass_on(chips > 2, across)

        if chips > 2:

            @pl.when(on_line & is_end)
            def _():
                pass_on(False, inward)

        if chips > 4:

            @pl.when(on_line & jnp.logical_not(is_end | is_middle))
            def _():
                pass_on(True, inward)

    def total_piece(k, r):
        @pl.when(is_lent(k))
        def _():
            give_back(k // STRIDE).wait_recv()
            for q in range(SUB):
                final(k, q).start()

        @pl.when(jnp.logical_not(is_lent(k)))
        def _():
            for q in range(SUB):
                here = slice(q * sub_rows, (q + 1) * sub_rows)
                across(k, r, q).wait_recv()

                @pl.when(is_middle)
                def _():
                    tot_in[k, here] = (tot_in[k, here].astype(F32) + part[k, here].astype(F32)).astype(BF16)

                @pl.when(jnp.logical_not(is_end))
                def _():
                    outward(k, r, q).start()

                @pl.when(k < pieces)
                def _():
                    final(k, q).start()

        @pl.when(k < pieces)
        def _():
            dw_ref[rows_at(k), cols_at(k, mine)] = tot_in[k]

        @pl.when(k >= pieces)
        def _():
            give_back(k - pieces).start()

    on_list = pieces + hosted
    on_line = on_list - lent
    late = on_line - LAG

    def listed(i):
        return jnp.where(
            i < HOST_AT, i, jnp.where(i < HOST_AT + hosted, i - HOST_AT + pieces, i - hosted)
        )

    def line_place(i):
        return jnp.where(i < STRIDE * lent, i // STRIDE * (STRIDE - 1) + lax.rem(i, STRIDE), i - lent)

    def of_line(r):
        few = STRIDE - 1
        return listed(jnp.where(r < few * lent, r // few * STRIDE + lax.rem(r, few), r + lent))

    def in_order(p):
        r = jnp.where(p < late, p, p - lent)
        return jnp.where((p >= late) & (p < late + lent), lent_piece(p - late), of_line(r)), r

    lag = jnp.where(is_middle, LAG, jnp.minimum(ring - 2, on_line))

    def step(i, carry):
        own = jnp.where(i < HOST_AT, i, i - hosted)
        working = i < on_list
        place = line_place(i)

        @pl.when((own + 1 < pieces) & ((i < HOST_AT) | (i >= HOST_AT + hosted)))
        def _():
            to_sibling(own + 1)

        @pl.when(working)
        def _():
            reduce_piece(listed(i), place)

        @pl.when(i == SMALL_STEP)
        def _():
            reduce_small()

        @pl.when(i == jnp.where(is_middle, 3 * SMALL_STEP, on_list + SMALL_STEP))
        def _():
            total_small()

        taken = working & jnp.logical_not(is_lent(i)) & (place >= lag)
        at = jnp.where(working, place - lag, on_line - lag + i - on_list)

        @pl.when(taken | jnp.logical_not(working))
        def _():
            total_piece(*in_order(at))

        return carry

    lax.fori_loop(0, on_list + lag + lent, step, 0)

    for k in range(sections // 2):

        @pl.when(s != 2 * k)
        def _():
            remote(small_tot, small_far.at[k], far_send.at[0], far_recv.at[k], sibling).wait_recv()

    dgain_ref[...] = small_tot[0:1, :]
    lanes = lax.broadcasted_iota(jnp.int32, (1, LANES), 1)
    means = jnp.zeros((1, LANES), F32)
    for k in range(sections // 2):
        sums = jnp.sum(small_far[k], axis=1, keepdims=True)
        means = jnp.where(lanes == k, sums[1:2] / (sums[2:3] * gate), means)
    fmean_ref[...] = means

    @pl.when(s != 0)
    def _():
        home(0, s).wait_recv()
        remote(gout, grad, grad_send, grad_recv.at[0], sibling).wait_send()

    @pl.when(s == 0)
    def _():
        sent_home = gout.at[pl.ds(slot, tokens - slot)]
        remote(sent_home, sent_home, grad_send, ig_recv, sibling).wait_send()

    @pl.when(s == 2)
    def _():
        dy_onward.wait_send()

    @pl.when(s != last)
    def _():
        dy_copy.wait_send()

    @pl.when(w_early & (s != 0))
    def _():
        x_copy.wait_send()

    for k in range(sections // 2):

        @pl.when((s != 0) | (k != 0))
        def _():
            mask_copies[k].wait_send()

    @pl.when(s != last)
    def _():
        remote(out, res, res_send, res_recv.at[0], sibling).wait_send()

    small_swap.wait_send()
    small_across.wait_send()

    @pl.when(jnp.logical_not(is_end))
    def _():
        small_outward.wait_send()

    @pl.when(is_mixer)
    def _():
        for k in range(1, sections):
            far_copy(k).wait_send()

    remote(sib_out, sib_in, sib_send, sib_recv.at[0], sibling).wait_send()

    def sent(source, sem, n):
        remote(source.at[pl.ds(0, n)], source.at[pl.ds(0, n)], sem, sib_recv.at[0], sibling).wait_send()

    for q in range(sections):
        given = LENT[q] if q < len(LENT) else 0
        taken = LENT[last - q] if last - q < len(LENT) else 0

        @pl.when((s == q) & jnp.logical_not(is_end))
        def _():
            sent(tot_in, tot_send, pieces - given + taken)

        @pl.when(s == q)
        def _():
            sent(part, part_send, pieces + taken)
            if taken:
                sent(guest_in, back_send, taken)

    sent(tot_in, fin_send, pieces)
    their_half = dw_ref.at[:, pl.ds(pl.multiple_of((1 - mine) * half, half), half)]
    remote(their_half, their_half, fin_send, fin_recv, sibling).wait_recv()


def finish_kernel(
    dw_ref, ig_ref, dgain_ref, fmean_ref, ig_out, dw_out, dgain_out, fmean_out, wide_dw, ig, dgain, fmean, sem, small_sem
):
    slots, step = wide_dw.shape[:2]
    steps = dw_ref.shape[0] // step

    def copy(k):
        return pltpu.make_async_copy(
            wide_dw.at[k % slots], dw_out.at[pl.ds(k * step, step)], sem.at[k % slots]
        )

    def convert(k):
        wide_dw[k % slots] = dw_ref[k * step : (k + 1) * step].astype(F32)
        copy(k).start()

    for k in range(slots):
        convert(k)
    slot = ig_ref.shape[1]
    token_rows = lax.broadcasted_iota(jnp.int32, (slot, slot), 0)
    order = jnp.where(time_of_row(slot, (slot, slot), 1) == token_rows, 1.0, 0.0).astype(BF16)
    ig[0] = dot(order, ig_ref[0]).astype(BF16)
    dgain[...] = dgain_ref[0]
    fmean[...] = fmean_ref[0, : fmean.shape[0]]
    small = [
        pltpu.make_async_copy(src, dst, small_sem.at[k])
        for k, (src, dst) in enumerate(((ig, ig_out), (dgain, dgain_out), (fmean, fmean_out)))
    ]
    for one in small:
        one.start()
    for k in range(slots, steps):
        copy(k - slots).wait()
        convert(k)
    for one in small:
        one.wait()
    for k in range(steps - slots, steps):
        copy(k).wait()


def finish(input_grad, weight_grads, gain_grads, means, sections):
    width, pack = weight_grads.shape
    vmem = pl.BlockSpec(memory_space=pltpu.VMEM)
    anywhere = pl.BlockSpec(memory_space=pl.ANY)
    slots = 8
    return pl.pallas_call(
        finish_kernel,
        out_shape=(
            jax.ShapeDtypeStruct(input_grad.shape, BF16),
            jax.ShapeDtypeStruct(weight_grads.shape, F32),
            jax.ShapeDtypeStruct((width,), F32),
            jax.ShapeDtypeStruct((sections // 2,), F32),
        ),
        in_specs=[vmem] * 4,
        out_specs=(anywhere,) * 4,
        scratch_shapes=[
            pltpu.VMEM((slots, FINISH_ROWS, pack), F32),
            pltpu.VMEM(input_grad.shape, BF16),
            pltpu.VMEM((width,), F32),
            pltpu.VMEM((sections // 2,), F32),
            pltpu.SemaphoreType.DMA((slots,)),
            pltpu.SemaphoreType.DMA((3,)),
        ],
        compiler_params=pltpu.CompilerParams(vmem_limit_bytes=16 * 1024 * 1024),
    )(weight_grads, input_grad, gain_grads, means)


def local(count, inputs, cotangent, section_weights, norm_gains, doc_lengths, slot_fill):
    sections = lax.axis_size("section")
    slot, width = inputs.shape[1:]
    pack = section_weights.shape[1]
    gate, ff, half = pack // 4, pack // 2, pack // 2
    tokens = sections * slot
    pieces = half * width // (PIECE[0] * PIECE[1])
    dma = pltpu.SemaphoreType.DMA
    ring = min(pieces + max(LENT), RING_PER_CHIP * (count // 2))
    own = pltpu.VMEM((pieces, *PIECE), BF16)
    hosted = pltpu.VMEM((pieces + max(LENT), *PIECE), BF16)
    small = pltpu.VMEM((8, width), F32)
    stack = pltpu.VMEM((tokens, width), BF16)
    vmem = pl.BlockSpec(memory_space=pltpu.VMEM)
    anywhere = pl.BlockSpec(memory_space=pl.ANY)
    input_grad, weight_grads, gain_grads, means = pl.pallas_call(
        functools.partial(kernel, count),
        out_shape=(
            pltpu.VMEM((1, slot, width), BF16),
            pltpu.VMEM((width, pack), BF16),
            pltpu.VMEM((1, width), F32),
            pltpu.VMEM((1, LANES), F32),
        ),
        in_specs=[anywhere] * 6,
        out_specs=(vmem, vmem, vmem, vmem),
        scratch_shapes=[
            pltpu.VMEM((width, pack), BF16), pltpu.VMEM((pack, width), BF16),
            stack, stack, stack, stack, stack,
            pltpu.VMEM((slot, width), BF16), pltpu.VMEM((slot, width), BF16),
            pltpu.VMEM((sections, 8, slot), F32), pltpu.VMEM((8, slot), F32),
            pltpu.VMEM((slot, LANES), F32), pltpu.VMEM((slot, LANES), F32),
            pltpu.VMEM((slot, width), BF16),
            pltpu.VMEM(inputs.shape, BF16), pltpu.VMEM(inputs.shape, BF16), pltpu.VMEM((1, width), F32),
            pltpu.SMEM(doc_lengths.shape, jnp.int32), pltpu.SMEM(slot_fill.shape, jnp.int32),
            pltpu.VMEM((tokens, pack), F32),
            pltpu.VMEM((tokens, pack), BF16),
            pltpu.VMEM((2, width, tokens), BF16),
            pltpu.VMEM((8, GATE_CHUNK), F32),
            own, own, hosted, hosted, hosted,
            pltpu.VMEM((max(LENT), *PIECE), BF16), pltpu.VMEM(PIECE, F32),
            small, small, small, small, small,
            pltpu.VMEM((sections // 2, 8, width), F32),
            dma, dma((5,)), dma, dma,
            dma((sections // 2,)),
            dma, dma((sections,)), dma, dma((sections,)),
            dma((sections,)), dma, dma, dma, pltpu.SemaphoreType.REGULAR,
            dma, dma((SIB_RING,)), dma, dma((ring * SUB,)), dma, dma((ring * SUB,)),
            dma, dma, dma((max(LENT),)), dma, dma((max(LENT),)),
            dma((3,)), dma((3,)), dma((sections - 1,)), dma((sections // 2,)),
        ],
        compiler_params=pltpu.CompilerParams(
            collective_id=0, has_side_effects=True, vmem_limit_bytes=56 * 1024 * 1024
        ),
    )(inputs, cotangent, section_weights, norm_gains.reshape(1, width), doc_lengths, slot_fill)
    return finish(input_grad, weight_grads, gain_grads, means, sections)


def solution(mesh):
    placed = (
        P("section", "dp", None),
        P("section", "dp", None),
        P("section", None),
        P("section"),
        P("section", "dp", None),
        P("section", "dp"),
    )
    return jax.shard_map(
        functools.partial(local, mesh.shape["dp"]),
        mesh=mesh,
        in_specs=placed,
        out_specs=(P("section", "dp", None), P("section", None), P("section"), P()),
        check_vma=False,
    )
```
